256 devices in a mesh: row: 8 (over z), col: 32 (over y, x, core).
Axes of the slice: x: 4, y: 4, z: 8, core: 2. Of those that a mesh axis runs over, the one named last changes fastest.
Arguments:
- pair_act: bfloat16 [768, 768, 128], P('row', 'col'), may hold values from -6 to 6
- pair_gain: float32 [128], replicated, may hold values from 0.25 to 1.75
- left_proj: bfloat16 [128, 256], replicated, may hold values from -0.5 to 0.5
- right_proj: bfloat16 [128, 256], replicated, may hold values from -0.5 to 0.5
- gate_proj: bfloat16 [128, 128], replicated, may hold values from -0.5 to 0.5
- mix_gain: float32 [128], replicated, may hold values from 0.25 to 1.75
- out_proj: bfloat16 [128, 128], replicated, may hold values from -0.5 to 0.5
- bias_proj: bfloat16 [128, 4], replicated, may hold values from -0.5 to 0.5
- token_single: bfloat16 [768, 384], P('row'), may hold values from -18 to 18
- cond_proj: bfloat16 [384, 128], replicated, may hold values from -0.3125 to 0.3125
- atom_act: bfloat16 [32, 4096, 128], P('col', 'row'), may hold values from -6 to 6
- atom_gain: float32 [128], replicated, may hold values from 0.25 to 1.75
- qkv_proj: bfloat16 [128, 384], replicated, may hold values from -0.5 to 0.5
- attn_proj: bfloat16 [128, 128], replicated, may hold values from -0.5 to 0.5
- token_proj: bfloat16 [128, 768], replicated, may hold values from -0.5 to 0.5
- atom_token: int32 [4096], P('row'), may hold values from 0 to 767, as said below
- atom_mask: int32 [4096], P('row'), may hold values from 0 to 1, as said below
- key_start: int32 [128], P('row'), may hold values from 0 to 3968, as said below
Outputs:
- tri_update: bfloat16 [768, 768, 128], P('row', 'col')
- atom_update: bfloat16 [32, 4096, 128], P('col', 'row')
- token_update: bfloat16 [32, 768, 768], P('col', 'row')
The draws below stay inside these ranges and needn't reach their ends.
Inputs may be any that keep to these rules, and one draw needn't show every extreme that they name: `atom_token`: slots r * 512 to (r + 1) * 512 - 1 hold atoms of tokens r * 96 to (r + 1) * 96 - 1, in nondecreasing order of token. `atom_mask`: in each block of 512 slots the live slots come first; at least 128 of a block are live. Window w holds the query slots 32 * w to 32 * w + 31; key_start[w] lies between 32 * w - 64 and 32 * w - 32, moved into the range.
All inputs are finite; a program needn't handle non-finite values.
Results may differ from the reference program's by a relative error of at most 0.024.
The reference program's roundings to bfloat16 on the way count: a program that leaves them out, or rounds other values in their place, can miss the bound.
Values may be sent and summed in bfloat16 or wider, within the bound.
A program may use at most 192 MiB of HBM per device.

```python
import math
import jax
import jax.numpy as jnp
from jax import lax

C_PAIR = 128
C_ATOM = 128
C_SINGLE = 384
C_TOKEN = 768
HEADS = 4
QWIN = 32
KWIN = 128
HALO = 64
ROW_TOK = 96
ATOM_ROW = 512
TOKENS = 768
ATOMS = 4096
WINDOWS = 128
SAMPLES = 32
HDIM = 32


def atom_layout(key):
    live_key, pick_key, token_key = jax.random.split(key, 3)
    blocks = ATOMS // ATOM_ROW
    live_count = jax.random.randint(live_key, (blocks,), ATOM_ROW // 4, ATOM_ROW + 1)
    full_block = jax.random.randint(pick_key, (), 0, blocks)
    live_count = jnp.where(jnp.arange(blocks) == full_block, ATOM_ROW, live_count)
    alive = jnp.arange(ATOM_ROW)[None, :] < live_count[:, None]
    raw_tokens = jax.random.randint(token_key, (blocks, ATOM_ROW), 0, ROW_TOK)
    ordered = jnp.sort(jnp.where(alive, raw_tokens, ROW_TOK), axis=1)
    local_token = jnp.minimum(ordered, ROW_TOK - 1)
    global_token = local_token + ROW_TOK * jnp.arange(blocks)[:, None]
    return (global_token.reshape(-1).astype(jnp.int32), alive.reshape(-1).astype(jnp.int32))


def draw_atom_token(key, part):
    return atom_layout(key)[0]


def draw_atom_mask(key, part):
    return atom_layout(key)[1]


def draw_key_start(key, part):
    key = jax.random.fold_in(key, 7)
    jitter = jax.random.randint(key, (WINDOWS,), 0, QWIN + 1)
    starts = QWIN * jnp.arange(WINDOWS) - HALO + jitter
    return jnp.clip(starts, 0, ATOMS - KWIN).astype(jnp.int32)


def draw_token_single(key, part):
    key = jax.random.fold_in(key, 11)
    values = jnp.clip(jax.random.normal(key, (TOKENS, C_SINGLE), jnp.float32), -4.0, 4.0)
    return values.astype(jnp.bfloat16)


def steps_of(own_key, extent, shards, smallest, largest):
    level = 1.0
    for position, parts in shards:
        steps = jax.random.uniform(jax.random.fold_in(jax.random.fold_in(own_key, 6), position), (parts,), jnp.float32, smallest / len(shards), largest / len(shards))
        level = level * jnp.repeat(jnp.exp(steps), extent[position] // parts).reshape((-1,) + (1,) * (len(extent) - 1 - position))
    return level


def gaussian(rng, dims, scale, most, cuts=(), kind=jnp.bfloat16):
    result = jax.random.normal(rng, dims, jnp.float32) * scale
    if len(cuts) > 0:
        result = steps_of(rng, dims, cuts, -0.22, 0.18) * result
    return jnp.clip(result, min=-most, max=most).astype(kind)


def setup_inputs(seed: int = 0) -> dict:
    key_list = jax.random.split(jax.random.key(seed), 19)
    pair_act = gaussian(key_list[0], (TOKENS, TOKENS, C_PAIR), 1.0, 6.0, ((0, 8), (1, 32)))
    pair_gain = jnp.clip(1.0 + 0.15 * jax.random.normal(key_list[1], (C_PAIR,), jnp.float32), 0.25, 1.75)
    left_proj = gaussian(key_list[2], (C_PAIR, 2 * C_PAIR), C_PAIR ** -0.5, 0.5)
    right_proj = gaussian(key_list[3], (C_PAIR, 2 * C_PAIR), C_PAIR ** -0.5, 0.5)
    gate_proj = gaussian(key_list[4], (C_PAIR, C_PAIR), C_PAIR ** -0.5, 0.5)
    mix_gain = jnp.clip(1.0 + 0.15 * jax.random.normal(key_list[5], (C_PAIR,), jnp.float32), 0.25, 1.75)
    out_proj = gaussian(key_list[6], (C_PAIR, C_PAIR), C_PAIR ** -0.5, 0.5)
    bias_proj = gaussian(key_list[7], (C_PAIR, HEADS), C_PAIR ** -0.5, 0.5)
    token_single = draw_token_single(jax.random.fold_in(key_list[18], 71), 0)
    cond_proj = gaussian(key_list[9], (C_SINGLE, C_ATOM), C_SINGLE ** -0.5, 0.3125)
    atom_act = gaussian(key_list[10], (SAMPLES, ATOMS, C_ATOM), 1.0, 6.0, ((0, 32), (1, 8)))
    atom_gain = jnp.clip(1.0 + 0.15 * jax.random.normal(key_list[11], (C_ATOM,), jnp.float32), 0.25, 1.75)
    qkv_proj = gaussian(key_list[12], (C_ATOM, 3 * C_ATOM), C_ATOM ** -0.5, 0.5)
    attn_proj = gaussian(key_list[13], (C_ATOM, C_ATOM), C_ATOM ** -0.5, 0.5)
    token_proj = gaussian(key_list[14], (C_ATOM, C_TOKEN), C_ATOM ** -0.5, 0.5)
    atom_token = draw_atom_token(jax.random.fold_in(key_list[18], 71), 0)
    atom_mask = draw_atom_mask(jax.random.fold_in(key_list[18], 71), 0)
    key_start = draw_key_start(jax.random.fold_in(key_list[18], 71), 0)
    return dict(pair_act=pair_act, pair_gain=pair_gain, left_proj=left_proj, right_proj=right_proj, gate_proj=gate_proj, mix_gain=mix_gain, out_proj=out_proj, bias_proj=bias_proj, token_single=token_single, cond_proj=cond_proj, atom_act=atom_act, atom_gain=atom_gain, qkv_proj=qkv_proj, attn_proj=attn_proj, token_proj=token_proj, atom_token=atom_token, atom_mask=atom_mask, key_start=key_start)


def layer_norm(values, gain):
    centre = values - lax.optimization_barrier(jnp.mean(values, axis=-1, keepdims=True))
    spread = lax.optimization_barrier(jnp.mean(centre * centre, axis=-1, keepdims=True))
    return centre * lax.rsqrt(spread + 1e-05) * gain

def gated_proj(normed, weight):
    joined = jnp.dot(normed, weight, preferred_element_type=jnp.float32)
    return (jax.nn.sigmoid(joined[:, :C_PAIR]) * joined[:, C_PAIR:]).astype(jnp.bfloat16)

def reference(pair_act, pair_gain, left_proj, right_proj, gate_proj, mix_gain, out_proj, bias_proj, token_single, cond_proj, atom_act, atom_gain, qkv_proj, attn_proj, token_proj, atom_token, atom_mask, key_start):
    pair_norm = layer_norm(pair_act.astype(jnp.float32), pair_gain.astype(jnp.float32)).astype(jnp.bfloat16)
    flat_norm = pair_norm.reshape(TOKENS * TOKENS, C_PAIR)
    left_side = gated_proj(flat_norm, left_proj).reshape(TOKENS, TOKENS, C_PAIR)
    right_side = gated_proj(flat_norm, right_proj).reshape(TOKENS, TOKENS, C_PAIR)
    gate_vals = jax.nn.sigmoid(jnp.dot(flat_norm, gate_proj, preferred_element_type=jnp.float32))
    mixed_sum = jnp.einsum('ikc,jkc->ijc', left_side.astype(jnp.float32), right_side.astype(jnp.float32), precision=lax.Precision.HIGHEST)
    mixed_norm = layer_norm(mixed_sum, mix_gain.astype(jnp.float32)).astype(jnp.bfloat16)
    projected = jnp.dot(mixed_norm.reshape(TOKENS * TOKENS, C_PAIR), out_proj, preferred_element_type=jnp.float32)
    tri_update = (gate_vals * projected).astype(jnp.bfloat16).reshape(TOKENS, TOKENS, C_PAIR)
    updated_pair = (pair_act.astype(jnp.float32) + tri_update.astype(jnp.float32)).astype(jnp.bfloat16)
    pair_bias = jnp.dot(updated_pair.reshape(TOKENS * TOKENS, C_PAIR), bias_proj, preferred_element_type=jnp.float32).reshape(TOKENS, TOKENS, HEADS)
    cond_token = jnp.dot(token_single, cond_proj, preferred_element_type=jnp.float32).astype(jnp.bfloat16)
    token_hot = (atom_token[:, None] == jnp.arange(TOKENS, dtype=jnp.int32)[None, :]).astype(jnp.bfloat16)
    atom_cond = jnp.dot(token_hot, cond_token, preferred_element_type=jnp.float32)
    atom_hidden = (layer_norm(atom_act.astype(jnp.float32), atom_gain.astype(jnp.float32)) + atom_cond[None]).astype(jnp.bfloat16)
    qkv_all = jnp.dot(atom_hidden.reshape(SAMPLES * ATOMS, C_ATOM), qkv_proj, preferred_element_type=jnp.float32).astype(jnp.bfloat16).reshape(SAMPLES, ATOMS, 3 * C_ATOM)
    key_index = key_start[:, None] + jnp.arange(KWIN, dtype=jnp.int32)[None, :]
    key_live = (atom_mask > 0)[key_index]
    query_tokens = atom_token.reshape(WINDOWS, QWIN)
    key_tokens = atom_token[key_index]
    window_bias = jnp.transpose(pair_bias[query_tokens[:, :, None], key_tokens[:, None, :]], (0, 3, 1, 2))

    def attend_sample(inputs):
        queries, key_part, value_part = inputs
        query_heads = queries.astype(jnp.float32).reshape(WINDOWS, QWIN, HEADS, HDIM)
        key_heads = key_part[key_index].astype(jnp.float32).reshape(WINDOWS, KWIN, HEADS, HDIM)
        value_heads = value_part[key_index].astype(jnp.float32).reshape(WINDOWS, KWIN, HEADS, HDIM)
        scores = jnp.einsum('wqhd,wkhd->whqk', query_heads, key_heads, precision=lax.Precision.HIGHEST) / math.sqrt(HDIM) + window_bias
        scores = jnp.where(key_live[:, None, None, :], scores, -1000000000.0)
        weights = jax.nn.softmax(scores, axis=-1).astype(jnp.bfloat16)
        attended = jnp.einsum('whqk,wkhd->wqhd', weights.astype(jnp.float32), value_heads, precision=lax.Precision.HIGHEST)
        return attended.astype(jnp.bfloat16).reshape(ATOMS, C_ATOM)
    attended = lax.map(attend_sample, (qkv_all[:, :, :C_ATOM], qkv_all[:, :, C_ATOM:2 * C_ATOM], qkv_all[:, :, 2 * C_ATOM:]))
    slot_live = (atom_mask > 0).astype(jnp.float32)
    atom_update = (jnp.dot(attended.reshape(SAMPLES * ATOMS, C_ATOM), attn_proj, preferred_element_type=jnp.float32).reshape(SAMPLES, ATOMS, C_ATOM) * slot_live[None, :, None]).astype(jnp.bfloat16)
    token_terms = jax.nn.relu(jnp.dot(atom_update.reshape(SAMPLES * ATOMS, C_ATOM), token_proj, preferred_element_type=jnp.float32)).astype(jnp.bfloat16).reshape(SAMPLES, ATOMS, C_TOKEN)
    live_hot = token_hot * slot_live.astype(jnp.bfloat16)[:, None]
    counts = lax.optimization_barrier(jnp.sum(live_hot.astype(jnp.float32), axis=0))

    def token_sample(sample_terms):
        return jnp.dot(live_hot.T, sample_terms, preferred_element_type=jnp.float32)
    token_sums = lax.map(token_sample, token_terms)
    token_update = (token_sums / jnp.maximum(counts, 1.0)[None, :, None]).astype(jnp.bfloat16)
    return (tri_update, atom_update, token_update)
```

```python
import functools
import math

import jax
import jax.numpy as jnp
from jax import lax
from jax.experimental import pallas as pl
from jax.experimental.pallas import tpu as pltpu
from jax.sharding import PartitionSpec as P

MESH = pl.DeviceIdType.MESH
HEADS = 4
QWIN = 32
KWIN = 128
HALO = 64
LANES = 128
F32 = jnp.float32
BF16 = jnp.bfloat16
NT = (((1,), (1,)), ((), ()))
TN = (((0,), (0,)), ((), ()))


def dot(a, b, dims=None):
    if dims is None:
        return jnp.dot(a, b, preferred_element_type=F32)
    return lax.dot_general(a, b, dims, preferred_element_type=F32)


def normalised(values, axis):
    centre = values - jnp.mean(values, axis=axis, keepdims=True)
    spread = jnp.mean(centre * centre, axis=axis, keepdims=True)
    return centre * lax.rsqrt(spread + 1e-05)


def wait_bytes(ref, sem):
    pltpu.make_async_copy(ref, ref, sem).wait()


def padded(rows):
    return jnp.concatenate([rows, jnp.zeros((LANES - rows.shape[0], rows.shape[1]), rows.dtype)], axis=0)


def kernel(
    n_row,
    n_col,
    rt,
    cw,
    x_ref,
    pgain_ref,
    lproj_ref,
    rproj_ref,
    gproj_ref,
    mgain_ref,
    oproj_ref,
    bproj_ref,
    single_ref,
    cproj_ref,
    atom_ref,
    again_ref,
    qkvproj_ref,
    aproj_ref,
    tproj_ref,
    tok_ref,
    mask_ref,
    start_ref,
    tri_ref,
    aupd_ref,
    tupd_ref,
    xf,
    xn,
    wt,
    side_f,
    side_r,
    side_l,
    recv_r,
    recv_l,
    rtr,
    lt,
    ring,
    mf,
    msend,
    mrecv,
    mrf,
    gate,
    trif,
    biasf,
    bias_out,
    bias_in,
    bm,
    gcol,
    bpt,
    code,
    tokq,
    q_s,
    kv,
    att,
    sem_r,
    sem_l,
    sem_out,
    ring_send,
    ring_recv,
    m_send,
    m_recv,
    b_send,
    b_recv,
    halo_send,
    halo_recv,
):
    r = lax.axis_index("row")
    q = lax.axis_index("col")
    cpd = LANES // n_col
    half = cpd // 2
    sub = rt // cw
    blk = cpd * cw
    hb = half * cw
    right = lax.rem(r + 1, n_row)
    left = lax.rem(r + n_row - 1, n_row)
    slots = atom_ref.shape[0]
    far = n_row // 2

    def to_col(target, src, dst, send, recv):
        return pltpu.make_async_remote_copy(
            src_ref=src, dst_ref=dst, send_sem=send, recv_sem=recv, device_id={"col": target}, device_id_type=MESH
        )

    def to_row(target, src, dst, send, recv):
        return pltpu.make_async_remote_copy(
            src_ref=src, dst_ref=dst, send_sem=send, recv_sem=recv, device_id={"row": target}, device_id_type=MESH
        )

    barrier = pltpu.get_barrier_semaphore()

    def greet(d, _):
        pl.semaphore_signal(barrier, inc=1, device_id={"col": lax.rem(q + d, n_col)}, device_id_type=MESH)
        return 0

    lax.fori_loop(1, n_col, greet, 0)
    pl.semaphore_signal(barrier, inc=1, device_id={"row": right}, device_id_type=MESH)
    pl.semaphore_signal(barrier, inc=1, device_id={"row": left}, device_id_type=MESH)

    pgain = pgain_ref[...]

    def norm_step(t, _):
        rows = pl.ds(pl.multiple_of(t * rt, rt), rt)
        v = x_ref[rows, :].astype(F32)
        xf[rows, :] = v
        xn[rows, :] = normalised(v, -1) * pgain
        return 0

    lax.fori_loop(0, cw, norm_step, 0, unroll=2)

    def column(k):
        return padded(xn[pl.ds(k, rt, stride=cw), :].astype(BF16))

    def gated(xk):
        joined = dot(wt[...], xk, NT)
        return jax.nn.sigmoid(joined[:LANES]) * joined[LANES:]

    def pack(dst):
        def step(t, _):
            rows = pl.ds(pl.multiple_of(t * 384, 384), 384)
            dst[rows, :] = side_f[rows, :].astype(BF16)
            return 0

        lax.fori_loop(0, LANES * cw // 384, step, 0, unroll=2)

    def spread_half(src, dst, sem, h):
        def step(d, _):
            target = lax.rem(q + d, n_col)
            to_col(
                target,
                src.at[pl.ds(pl.multiple_of(target * blk + h * hb, 16), hb)],
                dst.at[h, pl.ds(pl.multiple_of(q * hb, 16), hb)],
                sem_out.at[0],
                sem.at[h],
            ).start()
            return 0

        lax.fori_loop(1, n_col, step, 0)
        pltpu.make_async_copy(
            src.at[pl.ds(pl.multiple_of(q * blk + h * hb, 16), hb)],
            dst.at[h, pl.ds(pl.multiple_of(q * hb, 16), hb)],
            sem.at[h],
        ).start()

    wt[...] = rproj_ref[...].astype(F32).T.astype(BF16)

    def right_step(k, _):
        side_f[pl.ds(k, LANES, stride=cw), :] = gated(column(k))
        return 0

    lax.fori_loop(0, cw, right_step, 0, unroll=2)
    pack(side_r)
    pl.semaphore_wait(barrier, n_col + 1)
    spread_half(side_r, recv_r, sem_r, 0)
    spread_half(side_r, recv_r, sem_r, 1)

    wt[...] = lproj_ref[...].astype(F32).T.astype(BF16)
    gproj = gproj_ref[...]

    def left_step(k, _):
        xk = column(k)
        side_f[pl.ds(k, LANES, stride=cw), :] = gated(xk)
        gate[k] = jax.nn.sigmoid(dot(xk, gproj))[:rt]
        return 0

    lax.fori_loop(0, cw, left_step, 0, unroll=2)
    pack(side_l)
    spread_half(side_l, recv_l, sem_l, 0)
    spread_half(side_l, recv_l, sem_l, 1)

    def channel_rows(src, h, p, c):
        pair = src[h, pl.ds(pl.multiple_of(p * 2 * hb, 16), 2 * hb), :].astype(F32)
        return jnp.concatenate([pair[c * cw : (c + 1) * cw], pair[hb + c * cw : hb + (c + 1) * cw]], axis=0)

    def ring_chunk(s, c):
        return ring.at[s, c]

    def forward(direction, s, c, src):
        target = right if direction == 0 else left
        dst = s + 1 if (direction == 0 or s + 1 == far) else far + s + 1
        return to_row(target, src, ring.at[dst, c], ring_send.at[direction, s, c], ring_recv.at[direction, s + 1, c])

    for h in range(2):
        wait_bytes(recv_r.at[h], sem_r.at[h])
        for cc in range(half):
            c = h * half + cc

            def gather_step(p, _, cc=cc, h=h):
                rtr[pl.ds(pl.multiple_of(p * 2 * cw, 16), 2 * cw), :] = channel_rows(recv_r, h, p, cc)
                return 0

            lax.fori_loop(0, n_col // 2, gather_step, 0, unroll=4)
            for b in range(n_col * cw // LANES):
                ring[0, c, :, b * LANES : (b + 1) * LANES] = rtr[b * LANES : (b + 1) * LANES, :].T[:rt].astype(BF16)
            forward(0, 0, c, ring.at[0, c]).start()
            forward(1, 0, c, ring.at[0, c]).start()

    lane = lax.broadcasted_iota(jnp.int32, (LANES, LANES), 1)
    first = (r * rt).astype(F32)
    code_rows = jnp.where(mask_ref[...] > 0, tok_ref[...] + 1, 0).astype(F32)
    tok_rows = tok_ref[...].astype(F32) - first
    cond = padded(dot(single_ref[...], cproj_ref[...]).astype(BF16))
    lane_f = lane.astype(F32)
    again = again_ref[...]
    for g in range(slots // LANES):
        rows = slice(g * LANES, (g + 1) * LANES)
        code[HALO + g * LANES : HALO + (g + 1) * LANES, :] = jnp.broadcast_to(code_rows[g : g + 1], (LANES, LANES)).T
        tcol = jnp.broadcast_to(tok_rows[g : g + 1], (LANES, LANES)).T
        hot = (tcol == lane_f).astype(F32).astype(BF16)
        hidden = (normalised(atom_ref[rows, :].astype(F32), -1) * again + dot(hot, cond)).astype(BF16)
        joined = dot(hidden, qkvproj_ref[...]).astype(BF16)
        q_s[rows, :] = joined[:, :LANES]
        kv[HALO + g * LANES : HALO + (g + 1) * LANES, :] = joined[:, LANES:]
    group = lax.broadcasted_iota(jnp.int32, tok_rows.shape, 1) // QWIN
    per_row = LANES // QWIN
    for g in range(per_row):
        own = jnp.where(group == g, tok_rows, 0.0)
        tiled = own + pltpu.roll(own, QWIN, 1) + pltpu.roll(own, 2 * QWIN, 1) + pltpu.roll(own, 3 * QWIN, 1)
        tokq[pl.ds(g, slots // LANES, stride=per_row), :] = tiled + (group * LANES).astype(F32)
    halos = []
    for n, buf in enumerate((kv, code)):
        halos.append(
            to_row(right, buf.at[pl.ds(slots, HALO)], buf.at[pl.ds(0, HALO)], halo_send.at[n, 0], halo_recv.at[n, 0])
        )
        halos.append(
            to_row(left, buf.at[pl.ds(HALO, HALO)], buf.at[pl.ds(HALO + slots, HALO)], halo_send.at[n, 1], halo_recv.at[n, 1])
        )
    for copy in halos:
        copy.start()

    for h in range(2):
        wait_bytes(recv_l.at[h], sem_l.at[h])
        for cc in range(half):

            def left_gather(p, _, cc=cc, h=h):
                lt[h * half + cc, pl.ds(pl.multiple_of(p * 2 * cw, 16), 2 * cw), :] = channel_rows(recv_l, h, p, cc).astype(BF16)
                return 0

            lax.fori_loop(0, n_col // 2, left_gather, 0, unroll=4)

    gcol[...] = jnp.broadcast_to(mgain_ref[...], (LANES, LANES)).T
    bpt[...] = jnp.concatenate([bproj_ref[...].astype(F32), jnp.zeros((LANES, LANES - HEADS), F32)], axis=1).T[:8].astype(BF16)

    def multiply(slot, c, d):
        m = dot(ring[slot, c], lt[c])
        for s in range(sub):
            mf[d, (s * cpd + c) * cw : (s * cpd + c + 1) * cw, :] = m[s * cw : (s + 1) * cw]

    def send_block(slot, d, source):
        msend[slot] = mf[d].astype(BF16)
        for s in range(sub):
            target = source * sub + s
            src = msend.at[slot, pl.ds(s * blk, blk)]
            dst = mrecv.at[pl.ds(pl.multiple_of(q * blk, 16), blk)]

            @pl.when(target == q)
            def _():
                pltpu.make_async_copy(src, dst, m_recv).start()

            @pl.when(target != q)
            def _():
                to_col(target, src, dst, m_send, m_recv).start()

    def finish(with_bias):
        wait_bytes(mrecv, m_recv)

        def widen(t, _):
            rows = pl.ds(pl.multiple_of(t * 384, 384), 384)
            mrf[rows, :] = mrecv[rows, :].astype(F32)
            return 0

        lax.fori_loop(0, LANES * cw // 384, widen, 0, unroll=2)
        oproj = oproj_ref[...]

        def step(j, _):
            v = mrf[pl.ds(j, LANES, stride=cw), :]
            n = (normalised(v, 0) * gcol[...]).astype(BF16)
            projected = dot(n, oproj, TN)[:rt]
            tri = (gate[j] * projected).astype(BF16).astype(F32)
            trif[pl.ds(j, rt, stride=cw), :] = tri
            if with_bias:
                updated = (xf[pl.ds(j, rt, stride=cw), :] + tri).astype(BF16)
                biasf[pl.ds(j, HEADS, stride=cw), :] = dot(bpt[...], padded(updated), NT)[:HEADS]
            return 0

        lax.fori_loop(0, cw, step, 0, unroll=2)

        def narrow(t, _):
            rows = pl.ds(pl.multiple_of(t * 384, 384), 384)
            tri_ref[rows, :] = trif[rows, :].astype(BF16)
            return 0

        lax.fori_loop(0, rt * cw // 384, narrow, 0, unroll=2)

    owner = q // sub
    near = lax.rem(owner - r + 1 + n_row, n_row)
    is_near = near < 3

    def step_in(direction, s, c):
        slot = s if (direction == 0 or s == far) else far + s
        wait_bytes(ring.at[slot, c], ring_recv.at[direction, s, c])
        if s + 1 < far or (s + 1 == far and (c < half) == (direction == 0)):
            forward(direction, s, c, ring.at[slot, c]).start()
        multiply(slot, c, direction)

    for c in range(cpd):
        multiply(0, c, 0)
    send_block(0, 0, r)

    for s in range(1, far):
        for c in range(cpd):
            step_in(0, s, c)
            step_in(1, s, c)
        send_block(s, 0, lax.rem(r + n_row - s, n_row))
        send_block(far + s, 1, lax.rem(r + s, n_row))
        if s == 1:

            @pl.when(is_near)
            def _():
                finish(True)
                bias_out[...] = biasf[...].astype(BF16)
                dst = bias_in.at[pl.ds(pl.multiple_of((near * sub + lax.rem(q, sub)) * HEADS * cw, 16), HEADS * cw)]

                def share(d, _):
                    to_col(lax.rem(q + d, n_col), bias_out, dst, b_send, b_recv).start()
                    return 0

                lax.fori_loop(1, n_col, share, 0)
                pltpu.make_async_copy(bias_out, dst, b_recv).start()

        if s == 2:
            attend(
                n_row, r, rt, cw, sub, slots, bias_in, b_recv, bm, code, tokq, q_s, kv, att, halos, start_ref,
                aproj_ref, tproj_ref, code_rows, aupd_ref, tupd_ref,
            )
    for c in range(half):
        step_in(0, far, c)
        step_in(1, far, c + half)
    merge = half * cw
    for s in range(sub):
        mf[0, s * blk + merge : (s + 1) * blk, :] = mf[1, s * blk + merge : (s + 1) * blk, :]
    send_block(far, 0, lax.rem(r + far, n_row))

    @pl.when(jnp.logical_not(is_near))
    def _():
        finish(False)

    for _ in range(2):
        wait_bytes(side_r.at[pl.ds(0, (n_col - 1) * blk)], sem_out.at[0])
    wait_bytes(mrecv.at[pl.ds(0, (n_col - 1) * blk)], m_send)

    @pl.when(is_near)
    def _():
        wait_bytes(mrecv.at[pl.ds(0, (n_col - 1) * HEADS * cw)], b_send)

    for direction in range(2):
        for s in range(far):
            for c in range(cpd):
                if s + 1 < far or (c < half) == (direction == 0):
                    wait_bytes(ring.at[0, c], ring_send.at[direction, s, c])
    for copy in halos:
        copy.wait_send()


def attend(
    n_row, r, rt, cw, sub, slots, bias_in, b_recv, bm, code, tokq, q_s, kv, att, halos, start_ref, aproj_ref, tproj_ref,
    code_rows, aupd_ref, tupd_ref,
):
    hq = HEADS * QWIN
    span = QWIN + KWIN
    windows = slots // QWIN
    hb = HEADS * cw
    for copy in halos:
        copy.wait_recv()
    wait_bytes(bias_in, b_recv)
    count = 3 * sub
    for p in range(count // 2):
        pair = bias_in[p * 2 * hb : (p + 1) * 2 * hb, :].astype(F32)
        heads = [
            jnp.concatenate([pair[h * cw : (h + 1) * cw], pair[hb + h * cw : hb + (h + 1) * cw]], axis=0)
            for h in range(HEADS)
        ]
        bm[p * 2 * cw : (p + 1) * 2 * cw, :] = jnp.concatenate(heads, axis=1).astype(BF16)
    bm[count * cw :, :] = jnp.zeros((bm.shape[0] - count * cw, bm.shape[1]), BF16)
    wide = bm.shape[0]
    row_head = lax.broadcasted_iota(jnp.int32, (hq, LANES), 0) // QWIN
    col_head = lax.broadcasted_iota(jnp.int32, (hq, LANES), 1) // (LANES // HEADS)
    own_head = row_head == col_head
    pick = lax.broadcasted_iota(jnp.int32, (HEADS * LANES, LANES), 0).astype(F32)
    place = lax.broadcasted_iota(jnp.int32, (span, LANES), 0)
    tokens = lax.broadcasted_iota(jnp.int32, (span, LANES), 1).astype(F32) + ((r - 1) * rt + 1).astype(F32)
    scale = 1.0 / math.sqrt(LANES // HEADS)

    def window(w, _):
        at = pl.multiple_of(w * QWIN, QWIN)
        first = (1 - (r + n_row - 1) // n_row) * (1 - (w + windows - 1) // windows)
        last = ((r + 1) // n_row) * ((w + 1) // windows)
        base = pl.multiple_of((w + first - last) * QWIN, QWIN)
        kw = kv[pl.ds(base, span), :LANES]
        vw = kv[pl.ds(base, span), LANES:]
        qw = q_s[pl.ds(at, QWIN), :]
        qm = jnp.where(own_head, jnp.concatenate([qw] * HEADS, axis=0).astype(F32), 0.0).astype(BF16)
        hot_q = (pick == tokq[pl.ds(w, 1), :]).astype(F32).astype(BF16)
        bias_q = dot(bm[...], hot_q).astype(BF16)
        cw_code = code[pl.ds(base, span), :]
        hot_k = jnp.concatenate(
            [(cw_code == tokens + float(t * LANES)).astype(F32) for t in range(wide // LANES)], axis=1
        ).astype(BF16)
        scores = dot(kw, qm, NT) * scale + dot(hot_k, bias_q)
        begin = start_ref[w] - r * slots + HALO - base
        valid = (cw_code > 0.0) & (place >= begin) & (place < begin + KWIN)
        scores = jnp.where(valid, scores, -1000000000.0)
        raised = jnp.exp(scores - jnp.max(scores, axis=0, keepdims=True))
        weights = (raised / jnp.sum(raised, axis=0, keepdims=True)).astype(BF16)
        mixed = jnp.where(own_head, dot(weights, vw, TN), 0.0)
        total = mixed[:QWIN]
        for h in range(1, HEADS):
            total = total + mixed[h * QWIN : (h + 1) * QWIN]
        att[pl.ds(at, QWIN), :] = total.astype(BF16)
        return 0

    lax.fori_loop(0, windows, window, 0, unroll=2)

    live = code[HALO : HALO + slots, :] > 0.0
    updated = jnp.where(live, dot(att[...], aproj_ref[...]), 0.0).astype(BF16)
    aupd_ref[...] = updated
    terms = jnp.maximum(dot(updated, tproj_ref[...]), 0.0).astype(BF16)
    own = (lax.broadcasted_iota(jnp.int32, (rt, LANES), 0) + r * rt + 1).astype(F32)
    hot = jnp.concatenate(
        [(own == code_rows[g : g + 1]).astype(F32) for g in range(slots // LANES)], axis=1
    )
    counts = jnp.maximum(jnp.sum(hot, axis=1, keepdims=True), 1.0)
    tupd_ref[...] = (dot(hot.astype(BF16), terms) / counts).astype(BF16)


def body(n_row, n_col, *args):
    (
        pair_act, pair_gain, left_proj, right_proj, gate_proj, mix_gain, out_proj, bias_proj, token_single, cond_proj,
        atom_act, atom_gain, qkv_proj, attn_proj, token_proj, atom_token, atom_mask, key_start,
    ) = args
    rt, cw, channels = pair_act.shape
    cpd = channels // n_col
    sub = rt // cw
    slots = atom_act.shape[1]
    far = n_row // 2
    depth = n_col * cw
    blk = cpd * cw
    vmem = pl.BlockSpec(memory_space=pltpu.VMEM)
    smem = pl.BlockSpec(memory_space=pltpu.SMEM)
    dma = pltpu.SemaphoreType.DMA
    rows = rt * cw
    scratch = [
        pltpu.VMEM((rows, LANES), F32),
        pltpu.VMEM((rows, LANES), F32),
        pltpu.VMEM((2 * LANES, LANES), BF16),
        pltpu.VMEM((LANES * cw, LANES), F32),
        pltpu.VMEM((LANES * cw, LANES), BF16),
        pltpu.VMEM((LANES * cw, LANES), BF16),
        pltpu.VMEM((2, n_col * blk // 2, LANES), BF16),
        pltpu.VMEM((2, n_col * blk // 2, LANES), BF16),
        pltpu.VMEM((depth, LANES), F32),
        pltpu.VMEM((cpd, depth, LANES), BF16),
        pltpu.VMEM((2 * far, cpd, rt, depth), BF16),
        pltpu.VMEM((2, sub * blk, LANES), F32),
        pltpu.VMEM((2 * far, sub * blk, LANES), BF16),
        pltpu.VMEM((LANES * cw, LANES), BF16),
        pltpu.VMEM((LANES * cw, LANES), F32),
        pltpu.VMEM((cw, rt, LANES), F32),
        pltpu.VMEM((rows, LANES), F32),
        pltpu.VMEM((HEADS * cw, LANES), F32),
        pltpu.VMEM((HEADS * cw, LANES), BF16),
        pltpu.VMEM((3 * sub * HEADS * cw, LANES), BF16),
        pltpu.VMEM((-(-3 * rt // LANES) * LANES, HEADS * LANES), BF16),
        pltpu.VMEM((LANES, LANES), F32),
        pltpu.VMEM((8, LANES), BF16),
        pltpu.VMEM((slots + 2 * HALO, LANES), F32),
        pltpu.VMEM((slots // QWIN, LANES), F32),
        pltpu.VMEM((slots, LANES), BF16),
        pltpu.VMEM((slots + 2 * HALO, 2 * LANES), BF16),
        pltpu.VMEM((slots, LANES), BF16),
        dma((2,)),
        dma((2,)),
        dma((1,)),
        dma((2, far, cpd)),
        dma((2, far + 1, cpd)),
        dma,
        dma,
        dma,
        dma,
        dma((2, 2)),
        dma((2, 2)),
    ]
    tri, aupd, tupd = pl.pallas_call(
        functools.partial(kernel, n_row, n_col, rt, cw),
        out_shape=[
            jax.ShapeDtypeStruct((rows, channels), BF16),
            jax.ShapeDtypeStruct((slots, channels), BF16),
            jax.ShapeDtypeStruct((rt, token_proj.shape[1]), BF16),
        ],
        in_specs=[vmem] * 17 + [smem],
        out_specs=[vmem] * 3,
        scratch_shapes=scratch,
        compiler_params=pltpu.CompilerParams(collective_id=0, has_side_effects=True, vmem_limit_bytes=56 * 1024 * 1024),
        name="triangle_attention",
    )(
        pair_act.reshape(rows, channels), pair_gain.reshape(1, -1), left_proj, right_proj, gate_proj, mix_gain.reshape(1, -1),
        out_proj, bias_proj, token_single, cond_proj, atom_act.reshape(slots, channels), atom_gain.reshape(1, -1), qkv_proj,
        attn_proj, token_proj, atom_token.reshape(-1, LANES), atom_mask.reshape(-1, LANES), key_start,
    )
    return tri.reshape(pair_act.shape), aupd.reshape(atom_act.shape), tupd[None]


def solution(mesh):
    none = P()
    row = P("row")
    atoms = P("col", "row", None)
    pair = P("row", "col", None)
    placed = (pair,) + (none,) * 7 + (P("row", None), none, atoms) + (none,) * 4 + (row,) * 3
    return jax.shard_map(
        functools.partial(body, mesh.shape["row"], mesh.shape["col"]),
        mesh=mesh,
        in_specs=placed,
        out_specs=(pair, atoms, atoms),
        check_vma=False,
    )
```

```python
import functools
import math

import jax
import jax.numpy as jnp
from jax import lax
from jax.experimental import pallas as pl
from jax.experimental.pallas import tpu as pltpu
from jax.sharding import PartitionSpec as P

MESH = pl.DeviceIdType.MESH
HEADS = 4
QWIN = 32
KWIN = 128
HALO = 64
LANES = 128
F32 = jnp.float32
BF16 = jnp.bfloat16
NT = (((1,), (1,)), ((), ()))
TN = (((0,), (0,)), ((), ()))


def dot(a, b, dims=None):
    if dims is None:
        return jnp.dot(a, b, preferred_element_type=F32)
    return lax.dot_general(a, b, dims, preferred_element_type=F32)


def normalised(values, axis):
    centre = values - jnp.mean(values, axis=axis, keepdims=True)
    spread = jnp.mean(centre * centre, axis=axis, keepdims=True)
    return centre * lax.rsqrt(spread + 1e-05)


def wait_bytes(ref, sem):
    pltpu.make_async_copy(ref, ref, sem).wait()


def padded(rows):
    return jnp.concatenate([rows, jnp.zeros((LANES - rows.shape[0], rows.shape[1]), rows.dtype)], axis=0)


def kernel(
    n_row,
    n_col,
    rt,
    cw,
    x_ref,
    pgain_ref,
    lproj_ref,
    rproj_ref,
    gproj_ref,
    mgain_ref,
    oproj_ref,
    bproj_ref,
    single_ref,
    cproj_ref,
    atom_ref,
    again_ref,
    qkvproj_ref,
    aproj_ref,
    tproj_ref,
    tok_ref,
    mask_ref,
    start_ref,
    tri_ref,
    aupd_ref,
    tupd_ref,
    xf,
    xn,
    wt,
    side_f,
    side_r,
    side_l,
    recv_r,
    recv_l,
    rtr,
    lt,
    ring,
    mf,
    msend,
    mrecv,
    mrf,
    gate,
    trif,
    biasf,
    bias_out,
    bias_in,
    bm,
    gcol,
    bpt,
    code,
    tokq,
    q_s,
    kv,
    att,
    sem_r,
    sem_l,
    sem_out,
    ring_send,
    ring_recv,
    m_send,
    m_recv,
    b_send,
    b_recv,
    halo_send,
    halo_recv,
):
    r = lax.axis_index("row")
    q = lax.axis_index("col")
    cpd = LANES // n_col
    half = cpd // 2
    sub = rt // cw
    blk = cpd * cw
    hb = half * cw
    right = lax.rem(r + 1, n_row)
    left = lax.rem(r + n_row - 1, n_row)
    slots = atom_ref.shape[0]
    far = n_row // 2

    def to_col(target, src, dst, send, recv):
        return pltpu.make_async_remote_copy(
            src_ref=src, dst_ref=dst, send_sem=send, recv_sem=recv, device_id={"col": target}, device_id_type=MESH
        )

    def to_row(target, src, dst, send, recv):
        return pltpu.make_async_remote_copy(
            src_ref=src, dst_ref=dst, send_sem=send, recv_sem=recv, device_id={"row": target}, device_id_type=MESH
        )

    barrier = pltpu.get_barrier_semaphore()

    def greet(d, _):
        pl.semaphore_signal(barrier, inc=1, device_id={"col": lax.rem(q + d, n_col)}, device_id_type=MESH)
        return 0

    lax.fori_loop(1, n_col, greet, 0)
    pl.semaphore_signal(barrier, inc=1, device_id={"row": right}, device_id_type=MESH)
    pl.semaphore_signal(barrier, inc=1, device_id={"row": left}, device_id_type=MESH)

    pgain = pgain_ref[...]

    def norm_step(t, _):
        rows = pl.ds(pl.multiple_of(t * rt, rt), rt)
        v = x_ref[rows, :].astype(F32)
        xf[rows, :] = v
        xn[rows, :] = normalised(v, -1) * pgain
        return 0

    lax.fori_loop(0, cw, norm_step, 0, unroll=2)

    def column(k):
        return padded(xn[pl.ds(k, rt, stride=cw), :].astype(BF16))

    def gated(xk):
        joined = dot(wt[...], xk, NT)
        return jax.nn.sigmoid(joined[:LANES]) * joined[LANES:]

    def pack(dst):
        def step(t, _):
            rows = pl.ds(pl.multiple_of(t * 384, 384), 384)
            dst[rows, :] = side_f[rows, :].astype(BF16)
            return 0

        lax.fori_loop(0, LANES * cw // 384, step, 0, unroll=2)

    def spread_half(src, dst, sem, h):
        def step(d, _):
            target = lax.rem(q + d, n_col)
            to_col(
                target,
                src.at[pl.ds(pl.multiple_of(target * blk + h * hb, 16), hb)],
                dst.at[h, pl.ds(pl.multiple_of(q * hb, 16), hb)],
                sem_out.at[0],
                sem.at[h],
            ).start()
            return 0

        lax.fori_loop(1, n_col, step, 0)
        pltpu.make_async_copy(
            src.at[pl.ds(pl.multiple_of(q * blk + h * hb, 16), hb)],
            dst.at[h, pl.ds(pl.multiple_of(q * hb, 16), hb)],
            sem.at[h],
        ).start()

    wt[...] = rproj_ref[...].astype(F32).T.astype(BF16)

    def right_step(k, _):
        side_f[pl.ds(k, LANES, stride=cw), :] = gated(column(k))
        return 0

    lax.fori_loop(0, cw, right_step, 0, unroll=2)
    pack(side_r)
    pl.semaphore_wait(barrier, n_col + 1)
    spread_half(side_r, recv_r, sem_r, 0)
    spread_half(side_r, recv_r, sem_r, 1)

    wt[...] = lproj_ref[...].astype(F32).T.astype(BF16)
    gproj = gproj_ref[...]

    def left_step(k, _):
        xk = column(k)
        side_f[pl.ds(k, LANES, stride=cw), :] = gated(xk)
        gate[k] = jax.nn.sigmoid(dot(xk, gproj))[:rt]
        return 0

    lax.fori_loop(0, cw, left_step, 0, unroll=2)
    pack(side_l)
    spread_half(side_l, recv_l, sem_l, 0)
    spread_half(side_l, recv_l, sem_l, 1)

    def channel_rows(src, h, p, c):
        pair = src[h, pl.ds(pl.multiple_of(p * 2 * hb, 16), 2 * hb), :].astype(F32)
        return jnp.concatenate([pair[c * cw : (c + 1) * cw], pair[hb + c * cw : hb + (c + 1) * cw]], axis=0)

    for h in range(2):
        wait_bytes(recv_r.at[h], sem_r.at[h])
        for cc in range(half):
            c = h * half + cc

            def gather_step(p, _, cc=cc, h=h):
                rtr[pl.ds(pl.multiple_of(p * 2 * cw, 16), 2 * cw), :] = channel_rows(recv_r, h, p, cc)
                return 0

            lax.fori_loop(0, n_col // 2, gather_step, 0, unroll=4)
            for b in range(n_col * cw // LANES):
                ring[0, c, :, b * LANES : (b + 1) * LANES] = rtr[b * LANES : (b + 1) * LANES, :].T[:rt].astype(BF16)
            to_row(right, ring.at[0, c], ring.at[1, c], ring_send.at[0, 0, c], ring_recv.at[0, 1, c]).start()
            to_row(left, ring.at[0, c], ring.at[far + 1, c], ring_send.at[1, 0, c], ring_recv.at[1, 1, c]).start()

    lane = lax.broadcasted_iota(jnp.int32, (LANES, LANES), 1)
    first = (r * rt).astype(F32)
    code_rows = jnp.where(mask_ref[...] > 0, tok_ref[...] + 1, 0).astype(F32)
    tok_rows = tok_ref[...].astype(F32) - first
    cond = padded(dot(single_ref[...], cproj_ref[...]).astype(BF16))
    lane_f = lane.astype(F32)
    again = again_ref[...]
    for g in range(slots // LANES):
        rows = slice(g * LANES, (g + 1) * LANES)
        code[HALO + g * LANES : HALO + (g + 1) * LANES, :] = jnp.broadcast_to(code_rows[g : g + 1], (LANES, LANES)).T
        tcol = jnp.broadcast_to(tok_rows[g : g + 1], (LANES, LANES)).T
        hot = (tcol == lane_f).astype(F32).astype(BF16)
        hidden = (normalised(atom_ref[rows, :].astype(F32), -1) * again + dot(hot, cond)).astype(BF16)
        joined = dot(hidden, qkvproj_ref[...]).astype(BF16)
        q_s[rows, :] = joined[:, :LANES]
        kv[HALO + g * LANES : HALO + (g + 1) * LANES, :] = joined[:, LANES:]
    group = lax.broadcasted_iota(jnp.int32, tok_rows.shape, 1) // QWIN
    per_row = LANES // QWIN
    for g in range(per_row):
        own = jnp.where(group == g, tok_rows, 0.0)
        tiled = own + pltpu.roll(own, QWIN, 1) + pltpu.roll(own, 2 * QWIN, 1) + pltpu.roll(own, 3 * QWIN, 1)
        tokq[pl.ds(g, slots // LANES, stride=per_row), :] = tiled + (group * LANES).astype(F32)
    halos = []
    for n, buf in enumerate((kv, code)):
        halos.append(
            to_row(right, buf.at[pl.ds(slots, HALO)], buf.at[pl.ds(0, HALO)], halo_send.at[n, 0], halo_recv.at[n, 0])
        )
        halos.append(
            to_row(left, buf.at[pl.ds(HALO, HALO)], buf.at[pl.ds(HALO + slots, HALO)], halo_send.at[n, 1], halo_recv.at[n, 1])
        )
    for copy in halos:
        copy.start()

    def gather_left():
        for h in range(2):
            wait_bytes(recv_l.at[h], sem_l.at[h])

            def left_gather(p, _, h=h):
                for cc in range(half):
                    lt[h * half + cc, pl.ds(pl.multiple_of(p * 2 * cw, 16), 2 * cw), :] = channel_rows(recv_l, h, p, cc).astype(BF16)
                return 0

            lax.fori_loop(0, n_col // 2, left_gather, 0, unroll=2)

    gcol[...] = jnp.broadcast_to(mgain_ref[...], (LANES, LANES)).T
    bpt[...] = jnp.concatenate([bproj_ref[...].astype(F32), jnp.zeros((8 - HEADS, LANES), F32)], axis=0).astype(BF16)

    def multiply(slot, c, d):
        m = dot(ring[slot, c], lt[c])
        for s in range(sub):
            mf[d, pl.ds(pl.multiple_of((s * cpd + c) * cw, 8), cw), :] = m[s * cw : (s + 1) * cw]

    def send_block(slot, d, source, first, size):
        msend[slot] = mf[d].astype(BF16)

        def step(s, _):
            target = source * sub + s
            src = msend.at[slot, pl.ds(pl.multiple_of(s * blk + first, 16), size)]
            dst = mrecv.at[pl.ds(pl.multiple_of(q * blk + first, 16), size)]

            @pl.when(target == q)
            def _():
                pltpu.make_async_copy(src, dst, m_recv).start()

            @pl.when(target != q)
            def _():
                to_col(target, src, dst, m_send, m_recv).start()

            return 0

        lax.fori_loop(0, sub, step, 0)

    owner = q // sub
    near = lax.rem(owner - r + 1 + n_row, n_row)
    is_near = near < 3
    final = (far - 1) * cpd
    events = final + half
    early = 3
    finish_at = cpd + 1
    attend_at = final - 4
    portion = slots // QWIN // 4

    def place(e):
        s = e // cpd + 1
        c = lax.rem(e, cpd)
        last = e // final
        c0 = c + last * c
        return s, c0, c0 + last, s + far * (1 - last), last

    def pass_on(e):
        s, c0, c1, slot1, last = place(e)
        wait_bytes(ring.at[s, c0], ring_recv.at[0, s, c0])
        before = (s + 1) // far

        @pl.when((last == 0) & (before * lax.rem(c0, 2) == 0))
        def _():
            to_row(right, ring.at[s, c0], ring.at[s + 1, c0], ring_send.at[0, s, c0], ring_recv.at[0, s + 1, c0]).start()

        wait_bytes(ring.at[slot1, c1], ring_recv.at[1, s, c1])

        @pl.when((last == 0) & (before * lax.rem(c0 + 1, 2) == 0))
        def _():
            to_row(
                left,
                ring.at[slot1, c1],
                ring.at[s + 1 + far * (1 - before), c1],
                ring_send.at[1, s, c1],
                ring_recv.at[1, s + 1, c1],
            ).start()

    def finish():
        wait_bytes(mrecv, m_recv)

        def widen(t, _):
            rows = pl.ds(pl.multiple_of(t * 384, 384), 384)
            mrf[rows, :] = mrecv[rows, :].astype(F32)
            return 0

        lax.fori_loop(0, LANES * cw // 384, widen, 0, unroll=2)
        oproj = oproj_ref[...]

        def step(j, _):
            v = mrf[pl.ds(j, LANES, stride=cw), :]
            n = (normalised(v, 0) * gcol[...]).astype(BF16)
            projected = dot(n, oproj, TN)[:rt]
            trif[pl.ds(j, rt, stride=cw), :] = (gate[j] * projected).astype(BF16).astype(F32)
            return 0

        lax.fori_loop(0, cw, step, 0, unroll=4)

        @pl.when(is_near)
        def _():
            def bias_step(j, _):
                updated = (xf[pl.ds(j, rt, stride=cw), :] + trif[pl.ds(j, rt, stride=cw), :]).astype(BF16)
                biasf[pl.ds(j, HEADS, stride=cw), :] = dot(bpt[...], padded(updated), NT)[:HEADS]
                return 0

            lax.fori_loop(0, cw, bias_step, 0, unroll=2)
            bias_out[...] = biasf[...].astype(BF16)
            dst = bias_in.at[pl.ds(pl.multiple_of((near * sub + lax.rem(q, sub)) * HEADS * cw, 16), HEADS * cw)]

            def share(d, _):
                to_col(lax.rem(q + d, n_col), bias_out, dst, b_send, b_recv).start()
                return 0

            lax.fori_loop(1, n_col, share, 0)
            pltpu.make_async_copy(bias_out, dst, b_recv).start()

        def narrow(t, _):
            rows = pl.ds(pl.multiple_of(t * 384, 384), 384)
            tri_ref[rows, :] = trif[rows, :].astype(BF16)
            return 0

        lax.fori_loop(0, rt * cw // 384, narrow, 0, unroll=2)

    def early_step(e, _):
        pass_on(e)
        return 0

    lax.fori_loop(0, early, early_step, 0)
    gather_left()

    def own_step(c, _):
        multiply(0, c, 0)
        return 0

    lax.fori_loop(0, cpd, own_step, 0)
    send_block(0, 0, r, 0, blk)

    prepare, window, conclude = attention(
        n_row, r, rt, cw, sub, slots, bias_in, b_recv, bm, code, tokq, q_s, kv, att, halos, start_ref, aproj_ref, tproj_ref,
        code_rows, aupd_ref, tupd_ref,
    )

    def event(e, _):
        @pl.when((e >= early) & (e < events))
        def _():
            pass_on(e)

        @pl.when(e < events)
        def _():
            s, c0, c1, slot1, last = place(e)
            multiply(s, c0, 0)
            multiply(slot1, c1, 1 - last)

            @pl.when((last == 0) & (c0 == cpd - 1))
            def _():
                send_block(s, 0, lax.rem(r + n_row - s, n_row), 0, blk)
                send_block(slot1, 1, lax.rem(r + s, n_row), 0, blk)

            @pl.when(last == 1)
            def _():
                send_block(far + far * (e - final), 0, lax.rem(r + far, n_row), (e - final) * hb, hb)

        @pl.when(e == attend_at)
        def _():
            prepare()

        @pl.when((e >= attend_at) & (e < attend_at + 4))
        def _():
            lax.fori_loop((e - attend_at) * portion, (e - attend_at + 1) * portion, window, 0)

        @pl.when(e == events)
        def _():
            conclude()

        @pl.when(e == jnp.where(is_near, finish_at, events))
        def _():
            finish()

        return 0

    lax.fori_loop(0, events + 1, event, 0)

    for _ in range(2):
        wait_bytes(side_r.at[pl.ds(0, (n_col - 1) * blk)], sem_out.at[0])
    wait_bytes(mrecv.at[pl.ds(0, (n_col - 1) * blk)], m_send)

    @pl.when(is_near)
    def _():
        wait_bytes(mrecv.at[pl.ds(0, (n_col - 1) * HEADS * cw)], b_send)

    def ring_left(n, _):
        s = n // cpd
        c = lax.rem(n, cpd)
        wait_bytes(ring.at[0, c], ring_send.at[0, s, c])
        wait_bytes(ring.at[0, c], ring_send.at[1, s, c])
        return 0

    lax.fori_loop(0, final, ring_left, 0)
    for c in range(cpd):
        wait_bytes(ring.at[0, c], ring_send.at[c % 2, far - 1, c])
    for copy in halos:
        copy.wait_send()


def attention(
    n_row, r, rt, cw, sub, slots, bias_in, b_recv, bm, code, tokq, q_s, kv, att, halos, start_ref, aproj_ref, tproj_ref,
    code_rows, aupd_ref, tupd_ref,
):
    hq = HEADS * QWIN
    span = QWIN + KWIN
    windows = slots // QWIN
    hb = HEADS * cw
    def prepare():
        for copy in halos:
            copy.wait_recv()
        wait_bytes(bias_in, b_recv)
        count = 3 * sub
        for p in range(count // 2):
            pair = bias_in[p * 2 * hb : (p + 1) * 2 * hb, :].astype(F32)
            heads = [
                jnp.concatenate([pair[h * cw : (h + 1) * cw], pair[hb + h * cw : hb + (h + 1) * cw]], axis=0)
                for h in range(HEADS)
            ]
            bm[p * 2 * cw : (p + 1) * 2 * cw, :] = jnp.concatenate(heads, axis=1).astype(BF16)
        bm[count * cw :, :] = jnp.zeros((bm.shape[0] - count * cw, bm.shape[1]), BF16)

    wide = bm.shape[0]
    row_head = lax.broadcasted_iota(jnp.int32, (hq, LANES), 0) // QWIN
    col_head = lax.broadcasted_iota(jnp.int32, (hq, LANES), 1) // (LANES // HEADS)
    own_head = row_head == col_head
    pick = lax.broadcasted_iota(jnp.int32, (HEADS * LANES, LANES), 0).astype(F32)
    place = lax.broadcasted_iota(jnp.int32, (span, LANES), 0)
    tokens = lax.broadcasted_iota(jnp.int32, (span, LANES), 1).astype(F32) + ((r - 1) * rt + 1).astype(F32)
    scale = 1.0 / math.sqrt(LANES // HEADS)

    def window(w, _):
        at = pl.multiple_of(w * QWIN, QWIN)
        first = (1 - (r + n_row - 1) // n_row) * (1 - (w + windows - 1) // windows)
        last = ((r + 1) // n_row) * ((w + 1) // windows)
        base = pl.multiple_of((w + first - last) * QWIN, QWIN)
        kw = kv[pl.ds(base, span), :LANES]
        vw = kv[pl.ds(base, span), LANES:]
        qw = q_s[pl.ds(at, QWIN), :]
        qm = jnp.where(own_head, jnp.concatenate([qw] * HEADS, axis=0).astype(F32), 0.0).astype(BF16)
        hot_q = (pick == tokq[pl.ds(w, 1), :]).astype(F32).astype(BF16)
        bias_q = dot(bm[...], hot_q).astype(BF16)
        cw_code = code[pl.ds(base, span), :]
        hot_k = jnp.concatenate(
            [(cw_code == tokens + float(t * LANES)).astype(F32) for t in range(wide // LANES)], axis=1
        ).astype(BF16)
        scores = dot(kw, qm, NT) * scale + dot(hot_k, bias_q)
        begin = start_ref[w] - r * slots + HALO - base
        valid = (cw_code > 0.0) & (place >= begin) & (place < begin + KWIN)
        scores = jnp.where(valid, scores, -1000000000.0)
        raised = jnp.exp(scores - jnp.max(scores, axis=0, keepdims=True))
        weights = (raised / jnp.sum(raised, axis=0, keepdims=True)).astype(BF16)
        mixed = jnp.where(own_head, dot(weights, vw, TN), 0.0)
        total = mixed[:QWIN]
        for h in range(1, HEADS):
            total = total + mixed[h * QWIN : (h + 1) * QWIN]
        att[pl.ds(at, QWIN), :] = total.astype(BF16)
        return 0

    def conclude():

        live = code[HALO : HALO + slots, :] > 0.0
        updated = jnp.where(live, dot(att[...], aproj_ref[...]), 0.0).astype(BF16)
        aupd_ref[...] = updated
        terms = jnp.maximum(dot(updated, tproj_ref[...]), 0.0).astype(BF16)
        own = (lax.broadcasted_iota(jnp.int32, (rt, LANES), 0) + r * rt + 1).astype(F32)
        hot = jnp.concatenate(
            [(own == code_rows[g : g + 1]).astype(F32) for g in range(slots // LANES)], axis=1
        )
        counts = jnp.maximum(jnp.sum(hot, axis=1, keepdims=True), 1.0)
        tupd_ref[...] = (dot(hot.astype(BF16), terms) / counts).astype(BF16)

    return prepare, window, conclude


def hand_over(a_ref, b_ref, c_ref, a_out, b_out, c_out, sems):
    copies = [
        pltpu.make_async_copy(src, dst, sems.at[n])
        for n, (src, dst) in enumerate(((a_ref, a_out), (b_ref, b_out), (c_ref, c_out)))
    ]
    for copy in copies:
        copy.start()
    for copy in copies:
        copy.wait()


def body(n_row, n_col, *args):
    (
        pair_act, pair_gain, left_proj, right_proj, gate_proj, mix_gain, out_proj, bias_proj, token_single, cond_proj,
        atom_act, atom_gain, qkv_proj, attn_proj, token_proj, atom_token, atom_mask, key_start,
    ) = args
    rt, cw, channels = pair_act.shape
    cpd = channels // n_col
    sub = rt // cw
    slots = atom_act.shape[1]
    far = n_row // 2
    depth = n_col * cw
    blk = cpd * cw
    vmem = pl.BlockSpec(memory_space=pltpu.VMEM)
    smem = pl.BlockSpec(memory_space=pltpu.SMEM)
    dma = pltpu.SemaphoreType.DMA
    rows = rt * cw
    scratch = [
        pltpu.VMEM((rows, LANES), F32),
        pltpu.VMEM((rows, LANES), F32),
        pltpu.VMEM((2 * LANES, LANES), BF16),
        pltpu.VMEM((LANES * cw, LANES), F32),
        pltpu.VMEM((LANES * cw, LANES), BF16),
        pltpu.VMEM((LANES * cw, LANES), BF16),
        pltpu.VMEM((2, n_col * blk // 2, LANES), BF16),
        pltpu.VMEM((2, n_col * blk // 2, LANES), BF16),
        pltpu.VMEM((depth, LANES), F32),
        pltpu.VMEM((cpd, depth, LANES), BF16),
        pltpu.VMEM((2 * far, cpd, rt, depth), BF16),
        pltpu.VMEM((2, sub * blk, LANES), F32),
        pltpu.VMEM((2 * far + 1, sub * blk, LANES), BF16),
        pltpu.VMEM((LANES * cw, LANES), BF16),
        pltpu.VMEM((LANES * cw, LANES), F32),
        pltpu.VMEM((cw, rt, LANES), F32),
        pltpu.VMEM((rows, LANES), F32),
        pltpu.VMEM((HEADS * cw, LANES), F32),
        pltpu.VMEM((HEADS * cw, LANES), BF16),
        pltpu.VMEM((3 * sub * HEADS * cw, LANES), BF16),
        pltpu.VMEM((-(-3 * rt // LANES) * LANES, HEADS * LANES), BF16),
        pltpu.VMEM((LANES, LANES), F32),
        pltpu.VMEM((8, LANES), BF16),
        pltpu.VMEM((slots + 2 * HALO, LANES), F32),
        pltpu.VMEM((slots // QWIN, LANES), F32),
        pltpu.VMEM((slots, LANES), BF16),
        pltpu.VMEM((slots + 2 * HALO, 2 * LANES), BF16),
        pltpu.VMEM((slots, LANES), BF16),
        dma((2,)),
        dma((2,)),
        dma((1,)),
        dma((2, far, cpd)),
        dma((2, far + 1, cpd)),
        dma,
        dma,
        dma,
        dma,
        dma((2, 2)),
        dma((2, 2)),
    ]
    made = pl.pallas_call(
        functools.partial(kernel, n_row, n_col, rt, cw),
        out_shape=[
            jax.ShapeDtypeStruct((rows, channels), BF16),
            jax.ShapeDtypeStruct((slots, channels), BF16),
            jax.ShapeDtypeStruct((rt, token_proj.shape[1]), BF16),
        ],
        in_specs=[vmem] * 17 + [smem],
        out_specs=[vmem] * 3,
        scratch_shapes=scratch,
        compiler_params=pltpu.CompilerParams(collective_id=0, has_side_effects=True, vmem_limit_bytes=56 * 1024 * 1024),
        name="triangle_attention",
    )(
        pair_act.reshape(rows, channels), pair_gain.reshape(1, -1), left_proj, right_proj, gate_proj, mix_gain.reshape(1, -1),
        out_proj, bias_proj.T, token_single, cond_proj, atom_act.reshape(slots, channels), atom_gain.reshape(1, -1), qkv_proj,
        attn_proj, token_proj, atom_token.reshape(-1, LANES), atom_mask.reshape(-1, LANES), key_start,
    )
    tri, aupd, tupd = pl.pallas_call(
        hand_over,
        out_shape=[jax.ShapeDtypeStruct(a.shape, a.dtype) for a in made],
        in_specs=[pl.BlockSpec(memory_space=pl.ANY)] * 3,
        out_specs=[pl.BlockSpec(memory_space=pl.ANY)] * 3,
        scratch_shapes=[dma((3,))],
        name="hand_over",
    )(*made)
    return tri.reshape(pair_act.shape), aupd.reshape(atom_act.shape), tupd[None]


def solution(mesh):
    none = P()
    row = P("row")
    atoms = P("col", "row", None)
    pair = P("row", "col", None)
    placed = (pair,) + (none,) * 7 + (P("row", None), none, atoms) + (none,) * 4 + (row,) * 3
    return jax.shard_map(
        functools.partial(body, mesh.shape["row"], mesh.shape["col"]),
        mesh=mesh,
        in_specs=placed,
        out_specs=(pair, atoms, atoms),
        check_vma=False,
    )
```

```python
import functools
import math

import jax
import jax.numpy as jnp
from jax import lax
from jax.experimental import pallas as pl
from jax.experimental.pallas import tpu as pltpu
from jax.sharding import PartitionSpec as P

MESH = pl.DeviceIdType.MESH
HEADS = 4
QWIN = 32
KWIN = 128
HALO = 64
LANES = 128
F32 = jnp.float32
BF16 = jnp.bfloat16
NT = (((1,), (1,)), ((), ()))
TN = (((0,), (0,)), ((), ()))


def dot(a, b, dims=None):
    if dims is None:
        return jnp.dot(a, b, preferred_element_type=F32)
    return lax.dot_general(a, b, dims, preferred_element_type=F32)


def normalised(values, axis):
    centre = values - jnp.mean(values, axis=axis, keepdims=True)
    spread = jnp.mean(centre * centre, axis=axis, keepdims=True)
    return centre * lax.rsqrt(spread + 1e-05)


def wait_bytes(ref, sem):
    pltpu.make_async_copy(ref, ref, sem).wait()


def padded(rows):
    return jnp.concatenate([rows, jnp.zeros((LANES - rows.shape[0], rows.shape[1]), rows.dtype)], axis=0)


def kernel(
    n_row,
    n_col,
    rt,
    cw,
    x_ref,
    pgain_ref,
    lproj_ref,
    rproj_ref,
    gproj_ref,
    mgain_ref,
    oproj_ref,
    bproj_ref,
    single_ref,
    cproj_ref,
    atom_ref,
    again_ref,
    qkvproj_ref,
    aproj_ref,
    tproj_ref,
    tok_ref,
    mask_ref,
    start_ref,
    tri_ref,
    aupd_ref,
    tupd_ref,
    xf,
    xn,
    wt,
    side_f,
    side_r,
    side_l,
    recv_r,
    recv_l,
    rtr,
    lt,
    ring,
    mf,
    msend,
    mrecv,
    mrf,
    gate,
    trif,
    biasf,
    bias_out,
    bias_in,
    bm,
    gcol,
    bpt,
    code,
    hot_q,
    hot_k,
    scores,
    bias_q,
    q_s,
    kv,
    att,
    sem_r,
    sem_l,
    sem_out,
    ring_send,
    ring_recv,
    m_send,
    m_recv,
    b_send,
    b_recv,
    halo_send,
    halo_recv,
):
    r = lax.axis_index("row")
    q = lax.axis_index("col")
    cpd = LANES // n_col
    half = cpd // 2
    sub = rt // cw
    blk = cpd * cw
    hb = half * cw
    right = lax.rem(r + 1, n_row)
    left = lax.rem(r + n_row - 1, n_row)
    slots = atom_ref.shape[0]
    far = n_row // 2

    def to_col(target, src, dst, send, recv):
        return pltpu.make_async_remote_copy(
            src_ref=src, dst_ref=dst, send_sem=send, recv_sem=recv, device_id={"col": target}, device_id_type=MESH
        )

    def to_row(target, src, dst, send, recv):
        return pltpu.make_async_remote_copy(
            src_ref=src, dst_ref=dst, send_sem=send, recv_sem=recv, device_id={"row": target}, device_id_type=MESH
        )

    barrier = pltpu.get_barrier_semaphore()

    def greet(d, _):
        pl.semaphore_signal(barrier, inc=1, device_id={"col": lax.rem(q + d, n_col)}, device_id_type=MESH)
        return 0

    lax.fori_loop(1, n_col, greet, 0)
    pl.semaphore_signal(barrier, inc=1, device_id={"row": right}, device_id_type=MESH)
    pl.semaphore_signal(barrier, inc=1, device_id={"row": left}, device_id_type=MESH)

    pgain = pgain_ref[...]

    def norm_step(t, _):
        rows = pl.ds(pl.multiple_of(t * rt, rt), rt)
        v = x_ref[rows, :].astype(F32)
        xf[rows, :] = v
        xn[rows, :] = normalised(v, -1) * pgain
        return 0

    lax.fori_loop(0, cw, norm_step, 0, unroll=2)

    def column(k):
        return padded(xn[pl.ds(k, rt, stride=cw), :].astype(BF16))

    def gated(xk):
        joined = dot(wt[...], xk, NT)
        return jax.nn.sigmoid(joined[:LANES]) * joined[LANES:]

    def pack(dst):
        def step(t, _):
            rows = pl.ds(pl.multiple_of(t * 384, 384), 384)
            dst[rows, :] = side_f[rows, :].astype(BF16)
            return 0

        lax.fori_loop(0, LANES * cw // 384, step, 0, unroll=2)

    def spread_half(src, dst, sem, h):
        def step(d, _):
            target = lax.rem(q + d, n_col)
            to_col(
                target,
                src.at[pl.ds(pl.multiple_of(target * blk + h * hb, 16), hb)],
                dst.at[h, pl.ds(pl.multiple_of(q * hb, 16), hb)],
                sem_out.at[0],
                sem.at[h],
            ).start()
            return 0

        lax.fori_loop(1, n_col, step, 0)
        pltpu.make_async_copy(
            src.at[pl.ds(pl.multiple_of(q * blk + h * hb, 16), hb)],
            dst.at[h, pl.ds(pl.multiple_of(q * hb, 16), hb)],
            sem.at[h],
        ).start()

    wt[...] = rproj_ref[...].astype(F32).T.astype(BF16)

    def right_step(k, _):
        side_f[pl.ds(k, LANES, stride=cw), :] = gated(column(k))
        return 0

    lax.fori_loop(0, cw, right_step, 0, unroll=2)
    pack(side_r)
    pl.semaphore_wait(barrier, n_col + 1)
    spread_half(side_r, recv_r, sem_r, 0)
    spread_half(side_r, recv_r, sem_r, 1)

    wt[...] = lproj_ref[...].astype(F32).T.astype(BF16)
    gproj = gproj_ref[...]

    def left_step(k, _):
        xk = column(k)
        side_f[pl.ds(k, LANES, stride=cw), :] = gated(xk)
        gate[k] = jax.nn.sigmoid(dot(xk, gproj))[:rt]
        return 0

    lax.fori_loop(0, cw, left_step, 0, unroll=2)
    pack(side_l)
    spread_half(side_l, recv_l, sem_l, 0)
    spread_half(side_l, recv_l, sem_l, 1)

    def channel_rows(src, h, p, c):
        pair = src[h, pl.ds(pl.multiple_of(p * 2 * hb, 16), 2 * hb), :].astype(F32)
        return jnp.concatenate([pair[c * cw : (c + 1) * cw], pair[hb + c * cw : hb + (c + 1) * cw]], axis=0)

    for h in range(2):
        wait_bytes(recv_r.at[h], sem_r.at[h])
        for cc in range(half):
            c = h * half + cc

            def gather_step(p, _, cc=cc, h=h):
                rtr[pl.ds(pl.multiple_of(p * 2 * cw, 16), 2 * cw), :] = channel_rows(recv_r, h, p, cc)
                return 0

            lax.fori_loop(0, n_col // 2, gather_step, 0, unroll=4)
            for b in range(n_col * cw // LANES):
                ring[0, c, :, b * LANES : (b + 1) * LANES] = rtr[b * LANES : (b + 1) * LANES, :].T[:rt].astype(BF16)
            to_row(right, ring.at[0, c], ring.at[1, c], ring_send.at[0, 0, c], ring_recv.at[0, 1, c]).start()
            to_row(left, ring.at[0, c], ring.at[far + 1, c], ring_send.at[1, 0, c], ring_recv.at[1, 1, c]).start()

    lane = lax.broadcasted_iota(jnp.int32, (LANES, LANES), 1)
    first = (r * rt).astype(F32)
    code_rows = jnp.where(mask_ref[...] > 0, tok_ref[...] + 1, 0).astype(F32)
    tok_rows = tok_ref[...].astype(F32) - first
    cond = padded(dot(single_ref[...], cproj_ref[...]).astype(BF16))
    lane_f = lane.astype(F32)
    again = again_ref[...]
    for g in range(slots // LANES):
        rows = slice(g * LANES, (g + 1) * LANES)
        code[HALO + g * LANES : HALO + (g + 1) * LANES, :] = jnp.broadcast_to(code_rows[g : g + 1], (LANES, LANES)).T
        tcol = jnp.broadcast_to(tok_rows[g : g + 1], (LANES, LANES)).T
        hot = (tcol == lane_f).astype(F32).astype(BF16)
        hot_q[rows, :] = hot
        hidden = (normalised(atom_ref[rows, :].astype(F32), -1) * again + dot(hot, cond)).astype(BF16)
        joined = dot(hidden, qkvproj_ref[...]).astype(BF16)
        q_s[rows, :] = joined[:, :LANES]
        kv[HALO + g * LANES : HALO + (g + 1) * LANES, :] = joined[:, LANES:]
    halos = []
    for n, buf in enumerate((kv, code)):
        halos.append(
            to_row(right, buf.at[pl.ds(slots, HALO)], buf.at[pl.ds(0, HALO)], halo_send.at[n, 0], halo_recv.at[n, 0])
        )
        halos.append(
            to_row(left, buf.at[pl.ds(HALO, HALO)], buf.at[pl.ds(HALO + slots, HALO)], halo_send.at[n, 1], halo_recv.at[n, 1])
        )
    for copy in halos:
        copy.start()

    def gather_left():
        for h in range(2):
            wait_bytes(recv_l.at[h], sem_l.at[h])

            def left_gather(p, _, h=h):
                for cc in range(half):
                    lt[h * half + cc, pl.ds(pl.multiple_of(p * 2 * cw, 16), 2 * cw), :] = channel_rows(recv_l, h, p, cc).astype(BF16)
                return 0

            lax.fori_loop(0, n_col // 2, left_gather, 0, unroll=2)

    gcol[...] = jnp.broadcast_to(mgain_ref[...], (LANES, LANES)).T
    bpt[...] = jnp.concatenate([bproj_ref[...].astype(F32), jnp.zeros((8 - HEADS, LANES), F32)], axis=0).astype(BF16)

    def multiply(slot, c, d):
        m = dot(ring[slot, c], lt[c])
        for s in range(sub):
            mf[d, pl.ds(pl.multiple_of((s * cpd + c) * cw, 8), cw), :] = m[s * cw : (s + 1) * cw]

    def send_block(slot, d, source, first, size):
        msend[slot] = mf[d].astype(BF16)

        def step(s, _):
            target = source * sub + s
            src = msend.at[slot, pl.ds(pl.multiple_of(s * blk + first, 16), size)]
            dst = mrecv.at[pl.ds(pl.multiple_of(q * blk + first, 16), size)]

            @pl.when(target == q)
            def _():
                pltpu.make_async_copy(src, dst, m_recv).start()

            @pl.when(target != q)
            def _():
                to_col(target, src, dst, m_send, m_recv).start()

            return 0

        lax.fori_loop(0, sub, step, 0)

    owner = q // sub
    near = lax.rem(owner - r + 1 + n_row, n_row)
    is_near = near < 3
    final = (far - 1) * cpd
    events = final + half
    early = 3
    finish_at = cpd + 1
    attend_at = final - 3
    portion = slots // QWIN // 8

    def place(e):
        s = e // cpd + 1
        c = lax.rem(e, cpd)
        last = e // final
        c0 = c + last * c
        return s, c0, c0 + last, s + far * (1 - last), last

    def pass_on(e):
        s, c0, c1, slot1, last = place(e)
        wait_bytes(ring.at[s, c0], ring_recv.at[0, s, c0])
        before = (s + 1) // far

        @pl.when((last == 0) & (before * lax.rem(c0, 2) == 0))
        def _():
            to_row(right, ring.at[s, c0], ring.at[s + 1, c0], ring_send.at[0, s, c0], ring_recv.at[0, s + 1, c0]).start()

        wait_bytes(ring.at[slot1, c1], ring_recv.at[1, s, c1])

        @pl.when((last == 0) & (before * lax.rem(c0 + 1, 2) == 0))
        def _():
            to_row(
                left,
                ring.at[slot1, c1],
                ring.at[s + 1 + far * (1 - before), c1],
                ring_send.at[1, s, c1],
                ring_recv.at[1, s + 1, c1],
            ).start()

    def finish():
        wait_bytes(mrecv, m_recv)

        def widen(t, _):
            rows = pl.ds(pl.multiple_of(t * 384, 384), 384)
            mrf[rows, :] = mrecv[rows, :].astype(F32)
            return 0

        lax.fori_loop(0, LANES * cw // 384, widen, 0, unroll=2)
        oproj = oproj_ref[...]

        def step(j, _):
            v = mrf[pl.ds(j, LANES, stride=cw), :]
            n = (normalised(v, 0) * gcol[...]).astype(BF16)
            projected = dot(n, oproj, TN)[:rt]
            trif[pl.ds(j, rt, stride=cw), :] = (gate[j] * projected).astype(BF16).astype(F32)
            return 0

        lax.fori_loop(0, cw, step, 0, unroll=4)

        @pl.when(is_near)
        def _():
            def bias_step(j, _):
                updated = (xf[pl.ds(j, rt, stride=cw), :] + trif[pl.ds(j, rt, stride=cw), :]).astype(BF16)
                biasf[pl.ds(j, HEADS, stride=cw), :] = dot(bpt[...], padded(updated), NT)[:HEADS]
                return 0

            lax.fori_loop(0, cw, bias_step, 0, unroll=2)
            bias_out[...] = biasf[...].astype(BF16)
            dst = bias_in.at[pl.ds(pl.multiple_of((near * sub + lax.rem(q, sub)) * HEADS * cw, 16), HEADS * cw)]

            def share(d, _):
                to_col(lax.rem(q + d, n_col), bias_out, dst, b_send, b_recv).start()
                return 0

            lax.fori_loop(1, n_col, share, 0)
            pltpu.make_async_copy(bias_out, dst, b_recv).start()

        def narrow(t, _):
            rows = pl.ds(pl.multiple_of(t * 384, 384), 384)
            tri_ref[rows, :] = trif[rows, :].astype(BF16)
            return 0

        lax.fori_loop(0, rt * cw // 384, narrow, 0, unroll=2)

    ahead, prepare, window, conclude = attention(
        n_row, r, rt, cw, sub, slots, bias_in, b_recv, bm, bias_q, code, hot_q, hot_k, scores, q_s, kv, att, halos, start_ref,
        aproj_ref, tproj_ref, code_rows, aupd_ref, tupd_ref,
    )

    pairs = slots // QWIN // 2

    def early_step(e, _):
        pass_on(e)

        @pl.when(e == 1)
        def _():
            for copy in halos:
                copy.wait_recv()

        @pl.when(e > 0)
        def _():
            lax.fori_loop((e - 1) * (pairs // 2), e * (pairs // 2), ahead, 0)

        return 0

    lax.fori_loop(0, early, early_step, 0)
    gather_left()

    def own_step(c, _):
        multiply(0, c, 0)
        return 0

    lax.fori_loop(0, cpd, own_step, 0)
    send_block(0, 0, r, 0, blk)

    def event(e, _):
        @pl.when((e >= early) & (e < events))
        def _():
            pass_on(e)

        @pl.when(e < events)
        def _():
            s, c0, c1, slot1, last = place(e)
            multiply(s, c0, 0)
            multiply(slot1, c1, 1 - last)

            @pl.when((last == 0) & (c0 == cpd - 1))
            def _():
                send_block(s, 0, lax.rem(r + n_row - s, n_row), 0, blk)
                send_block(slot1, 1, lax.rem(r + s, n_row), 0, blk)

            @pl.when(last == 1)
            def _():
                send_block(far + far * (e - final), 0, lax.rem(r + far, n_row), (e - final) * hb, hb)

        @pl.when(e == attend_at)
        def _():
            prepare()

        @pl.when((e >= attend_at) & (e < attend_at + 4))
        def _():
            lax.fori_loop((e - attend_at) * portion, (e - attend_at + 1) * portion, window, 0)

        @pl.when(e == events)
        def _():
            conclude()

        @pl.when(e == jnp.where(is_near, finish_at, events))
        def _():
            finish()

        return 0

    lax.fori_loop(0, events + 1, event, 0)

    for _ in range(2):
        wait_bytes(side_r.at[pl.ds(0, (n_col - 1) * blk)], sem_out.at[0])
    wait_bytes(mrecv.at[pl.ds(0, (n_col - 1) * blk)], m_send)

    @pl.when(is_near)
    def _():
        wait_bytes(mrecv.at[pl.ds(0, (n_col - 1) * HEADS * cw)], b_send)

    def ring_left(n, _):
        s = n // cpd
        c = lax.rem(n, cpd)
        wait_bytes(ring.at[0, c], ring_send.at[0, s, c])
        wait_bytes(ring.at[0, c], ring_send.at[1, s, c])
        return 0

    lax.fori_loop(0, final, ring_left, 0)
    for c in range(cpd):
        wait_bytes(ring.at[0, c], ring_send.at[c % 2, far - 1, c])
    for copy in halos:
        copy.wait_send()


def attention(
    n_row, r, rt, cw, sub, slots, bias_in, b_recv, bm, bias_q, code, hot_q, hot_k, scores, q_s, kv, att, halos, start_ref,
    aproj_ref, tproj_ref, code_rows, aupd_ref, tupd_ref,
):
    hq = HEADS * QWIN
    span = QWIN + KWIN
    windows = slots // QWIN
    hb = HEADS * cw
    count = 3 * sub
    wide = bm.shape[0] // HEADS
    row_head = lax.broadcasted_iota(jnp.int32, (hq, LANES), 0) // QWIN
    col_head = lax.broadcasted_iota(jnp.int32, (hq, LANES), 1) // (LANES // HEADS)
    own_head = row_head == col_head
    place = lax.broadcasted_iota(jnp.int32, (span, LANES), 0)
    tokens = lax.broadcasted_iota(jnp.int32, (span, LANES), 1).astype(F32) + ((r - 1) * rt + 1).astype(F32)
    scale = 1.0 / math.sqrt(LANES // HEADS)

    def key_base(w):
        first = (1 - (r + n_row - 1) // n_row) * (1 - (w + windows - 1) // windows)
        last = ((r + 1) // n_row) * ((w + 1) // windows)
        return pl.multiple_of((w + first - last) * QWIN, QWIN)

    def ahead(w):
        at = pl.multiple_of(w * QWIN, QWIN)
        base = key_base(w)
        kw = kv[pl.ds(base, span), :LANES]
        qw = q_s[pl.ds(at, QWIN), :]
        qm = jnp.where(own_head, jnp.concatenate([qw] * HEADS, axis=0).astype(F32), 0.0).astype(BF16)
        key_code = code[pl.ds(base, span), :]
        for t in range(wide // LANES):
            hot_k[w, :, t * LANES : (t + 1) * LANES] = (key_code == tokens + float(t * LANES)).astype(F32).astype(BF16)
        begin = start_ref[w] - r * slots + HALO - base
        valid = (key_code > 0.0) & (place >= begin) & (place < begin + KWIN)
        scores[w] = jnp.where(valid, dot(kw, qm, NT) * scale, -1000000000.0)

    def prepare():
        wait_bytes(bias_in, b_recv)
        for p in range(count // 2):
            pair = bias_in[p * 2 * hb : (p + 1) * 2 * hb, :].astype(F32)
            for h in range(HEADS):
                rows = jnp.concatenate([pair[h * cw : (h + 1) * cw], pair[hb + h * cw : hb + (h + 1) * cw]], axis=0)
                bm[h * wide + p * 2 * cw : h * wide + (p + 1) * 2 * cw, :] = rows.astype(BF16)
        for h in range(HEADS):
            bm[h * wide + count * cw : (h + 1) * wide, :] = jnp.zeros((wide - count * cw, LANES), BF16)

        def spread(g, _):
            rows = pl.ds(pl.multiple_of(g * LANES, LANES), LANES)
            for h in range(HEADS):
                bias_q[rows, h * wide : (h + 1) * wide] = dot(hot_q[rows, :], bm[h * wide : (h + 1) * wide, :], NT).astype(BF16)
            return 0

        lax.fori_loop(0, slots // LANES, spread, 0)

    def window(w):
        at = pl.multiple_of(w * QWIN, QWIN)
        bias_w = jnp.concatenate([bias_q[pl.ds(at, QWIN), h * wide : (h + 1) * wide] for h in range(HEADS)], axis=0)
        total = scores[w] + dot(hot_k[w], bias_w, NT)
        raised = jnp.exp(total - jnp.max(total, axis=0, keepdims=True))
        weights = (raised / jnp.sum(raised, axis=0, keepdims=True)).astype(BF16)
        mixed = jnp.where(own_head, dot(weights, kv[pl.ds(key_base(w), span), LANES:], TN), 0.0)
        out = mixed[:QWIN]
        for h in range(1, HEADS):
            out = out + mixed[h * QWIN : (h + 1) * QWIN]
        att[pl.ds(at, QWIN), :] = out.astype(BF16)

    def conclude():
        live = code[HALO : HALO + slots, :] > 0.0
        updated = jnp.where(live, dot(att[...], aproj_ref[...]), 0.0).astype(BF16)
        aupd_ref[...] = updated
        terms = jnp.maximum(dot(updated, tproj_ref[...]), 0.0).astype(BF16)
        own = (lax.broadcasted_iota(jnp.int32, (rt, LANES), 0) + r * rt + 1).astype(F32)
        hot = jnp.concatenate([(own == code_rows[g : g + 1]).astype(F32) for g in range(slots // LANES)], axis=1)
        counts = jnp.maximum(jnp.sum(hot, axis=1, keepdims=True), 1.0)
        tupd_ref[...] = (dot(hot.astype(BF16), terms) / counts).astype(BF16)

    def in_pairs(work):
        def step(p, _):
            work(2 * p)
            work(2 * p + 1)
            return 0

        return step

    return in_pairs(ahead), prepare, in_pairs(window), conclude


def hand_over(a_ref, b_ref, c_ref, a_out, b_out, c_out, ins, outs, a_mid, b_mid, c_mid):
    steps = ((a_ref, a_mid, a_out), (b_ref, b_mid, b_out), (c_ref, c_mid, c_out))
    first = [pltpu.make_async_copy(src, mid, ins.at[n]) for n, (src, mid, _) in enumerate(steps)]
    then = [pltpu.make_async_copy(mid, dst, outs.at[n]) for n, (_, mid, dst) in enumerate(steps)]
    for copy in first:
        copy.start()
    for came, copy in zip(first, then):
        came.wait()
        copy.start()
    for copy in then:
        copy.wait()


def body(n_row, n_col, *args):
    (
        pair_act, pair_gain, left_proj, right_proj, gate_proj, mix_gain, out_proj, bias_proj, token_single, cond_proj,
        atom_act, atom_gain, qkv_proj, attn_proj, token_proj, atom_token, atom_mask, key_start,
    ) = args
    rt, cw, channels = pair_act.shape
    cpd = channels // n_col
    sub = rt // cw
    slots = atom_act.shape[1]
    far = n_row // 2
    depth = n_col * cw
    blk = cpd * cw
    vmem = pl.BlockSpec(memory_space=pltpu.VMEM)
    smem = pl.BlockSpec(memory_space=pltpu.SMEM)
    dma = pltpu.SemaphoreType.DMA
    rows = rt * cw
    wide = -(-3 * rt // LANES) * LANES
    scratch = [
        pltpu.VMEM((rows, LANES), F32),
        pltpu.VMEM((rows, LANES), F32),
        pltpu.VMEM((2 * LANES, LANES), BF16),
        pltpu.VMEM((LANES * cw, LANES), F32),
        pltpu.VMEM((LANES * cw, LANES), BF16),
        pltpu.VMEM((LANES * cw, LANES), BF16),
        pltpu.VMEM((2, n_col * blk // 2, LANES), BF16),
        pltpu.VMEM((2, n_col * blk // 2, LANES), BF16),
        pltpu.VMEM((depth, LANES), F32),
        pltpu.VMEM((cpd, depth, LANES), BF16),
        pltpu.VMEM((2 * far, cpd, rt, depth), BF16),
        pltpu.VMEM((2, sub * blk, LANES), F32),
        pltpu.VMEM((2 * far + 1, sub * blk, LANES), BF16),
        pltpu.VMEM((LANES * cw, LANES), BF16),
        pltpu.VMEM((LANES * cw, LANES), F32),
        pltpu.VMEM((cw, rt, LANES), F32),
        pltpu.VMEM((rows, LANES), F32),
        pltpu.VMEM((HEADS * cw, LANES), F32),
        pltpu.VMEM((HEADS * cw, LANES), BF16),
        pltpu.VMEM((3 * sub * HEADS * cw, LANES), BF16),
        pltpu.VMEM((HEADS * wide, LANES), BF16),
        pltpu.VMEM((LANES, LANES), F32),
        pltpu.VMEM((8, LANES), BF16),
        pltpu.VMEM((slots + 2 * HALO, LANES), F32),
        pltpu.VMEM((slots, LANES), BF16),
        pltpu.VMEM((slots // QWIN, QWIN + KWIN, wide), BF16),
        pltpu.VMEM((slots // QWIN, QWIN + KWIN, LANES), F32),
        pltpu.VMEM((slots, HEADS * wide), BF16),
        pltpu.VMEM((slots, LANES), BF16),
        pltpu.VMEM((slots + 2 * HALO, 2 * LANES), BF16),
        pltpu.VMEM((slots, LANES), BF16),
        dma((2,)),
        dma((2,)),
        dma((1,)),
        dma((2, far, cpd)),
        dma((2, far + 1, cpd)),
        dma,
        dma,
        dma,
        dma,
        dma((2, 2)),
        dma((2, 2)),
    ]
    made = pl.pallas_call(
        functools.partial(kernel, n_row, n_col, rt, cw),
        out_shape=[
            jax.ShapeDtypeStruct((rows, channels), BF16),
            jax.ShapeDtypeStruct((slots, channels), BF16),
            jax.ShapeDtypeStruct((rt, token_proj.shape[1]), BF16),
        ],
        in_specs=[vmem] * 17 + [smem],
        out_specs=[vmem] * 3,
        scratch_shapes=scratch,
        compiler_params=pltpu.CompilerParams(collective_id=0, has_side_effects=True, vmem_limit_bytes=56 * 1024 * 1024),
        name="triangle_attention",
    )(
        pair_act.reshape(rows, channels), pair_gain.reshape(1, -1), left_proj, right_proj, gate_proj, mix_gain.reshape(1, -1),
        out_proj, bias_proj.T, token_single, cond_proj, atom_act.reshape(slots, channels), atom_gain.reshape(1, -1), qkv_proj,
        attn_proj, token_proj, atom_token.reshape(-1, LANES), atom_mask.reshape(-1, LANES), key_start,
    )
    tri, aupd, tupd = pl.pallas_call(
        hand_over,
        out_shape=[jax.ShapeDtypeStruct(a.shape, a.dtype) for a in made],
        in_specs=[pl.BlockSpec(memory_space=pl.ANY)] * 3,
        out_specs=[pl.BlockSpec(memory_space=pl.ANY)] * 3,
        scratch_shapes=[dma((3,)), dma((3,))] + [pltpu.VMEM(a.shape, a.dtype) for a in made],
        name="hand_over",
    )(*made)
    return tri.reshape(pair_act.shape), aupd.reshape(atom_act.shape), tupd[None]


def solution(mesh):
    none = P()
    row = P("row")
    atoms = P("col", "row", None)
    pair = P("row", "col", None)
    placed = (pair,) + (none,) * 7 + (P("row", None), none, atoms) + (none,) * 4 + (row,) * 3
    return jax.shard_map(
        functools.partial(body, mesh.shape["row"], mesh.shape["col"]),
        mesh=mesh,
        in_specs=placed,
        out_specs=(pair, atoms, atoms),
        check_vma=False,
    )
```

```python
import functools
import math

import jax
import jax.numpy as jnp
from jax import lax
from jax.experimental import pallas as pl
from jax.experimental.pallas import tpu as pltpu
from jax.sharding import PartitionSpec as P

MESH = pl.DeviceIdType.MESH
HEADS = 4
QWIN = 32
KWIN = 128
HALO = 64
LANES = 128
F32 = jnp.float32
BF16 = jnp.bfloat16
NT = (((1,), (1,)), ((), ()))
TN = (((0,), (0,)), ((), ()))
FIRST = (0, 1, 3)
SECOND = (2, 4)
THIRD = (5, 6, 7, 8, 9, 10, 11, 12, 13, 14, 15, 16, 17)
LOAD_ORDER = FIRST + SECOND + THIRD


def dot(a, b, dims=None):
    if dims is None:
        return jnp.dot(a, b, preferred_element_type=F32)
    return lax.dot_general(a, b, dims, preferred_element_type=F32)


def normalised(values, axis):
    centre = values - jnp.mean(values, axis=axis, keepdims=True)
    spread = jnp.mean(centre * centre, axis=axis, keepdims=True)
    return centre * lax.rsqrt(spread + 1e-05)


def wait_bytes(ref, sem):
    pltpu.make_async_copy(ref, ref, sem).wait()


def padded(rows):
    return jnp.concatenate([rows, jnp.zeros((LANES - rows.shape[0], rows.shape[1]), rows.dtype)], axis=0)


def kernel(
    n_row,
    n_col,
    rt,
    cw,
    ins,
    outs,
    held,
    in_sems,
    out_sems,
    tri_ref,
    aupd_ref,
    tupd_ref,
    xf,
    xn,
    wt,
    side_f,
    side_r,
    side_l,
    recv_r,
    recv_l,
    rtr,
    lt,
    ring,
    mf,
    msend,
    mrecv,
    mrf,
    gate,
    trif,
    biasf,
    bias_out,
    bias_in,
    bm,
    gcol,
    bpt,
    code,
    hot_q,
    hot_k,
    scores,
    bias_q,
    q_s,
    kv,
    att,
    sem_r,
    sem_l,
    sem_out,
    ring_send,
    ring_recv,
    m_send,
    m_recv,
    b_send,
    b_recv,
    halo_send,
    halo_recv,
):
    (
        x_ref, pgain_ref, lproj_ref, rproj_ref, gproj_ref, mgain_ref, oproj_ref, bproj_ref, single_ref, cproj_ref, atom_ref,
        again_ref, qkvproj_ref, aproj_ref, tproj_ref, tok_ref, mask_ref, start_ref,
    ) = held
    loads = [pltpu.make_async_copy(src, dst, in_sems.at[n]) for n, (src, dst) in enumerate(zip(ins, held))]
    for n in LOAD_ORDER:
        loads[n].start()
    r = lax.axis_index("row")
    q = lax.axis_index("col")
    cpd = LANES // n_col
    half = cpd // 2
    sub = rt // cw
    blk = cpd * cw
    hb = half * cw
    right = lax.rem(r + 1, n_row)
    left = lax.rem(r + n_row - 1, n_row)
    slots = atom_ref.shape[0]
    far = n_row // 2

    def to_col(target, src, dst, send, recv):
        return pltpu.make_async_remote_copy(
            src_ref=src, dst_ref=dst, send_sem=send, recv_sem=recv, device_id={"col": target}, device_id_type=MESH
        )

    def to_row(target, src, dst, send, recv):
        return pltpu.make_async_remote_copy(
            src_ref=src, dst_ref=dst, send_sem=send, recv_sem=recv, device_id={"row": target}, device_id_type=MESH
        )

    barrier = pltpu.get_barrier_semaphore()

    def greet(d, _):
        pl.semaphore_signal(barrier, inc=1, device_id={"col": lax.rem(q + d, n_col)}, device_id_type=MESH)
        return 0

    lax.fori_loop(1, n_col, greet, 0)
    pl.semaphore_signal(barrier, inc=1, device_id={"row": right}, device_id_type=MESH)
    pl.semaphore_signal(barrier, inc=1, device_id={"row": left}, device_id_type=MESH)

    for n in FIRST:
        loads[n].wait()

    pgain = pgain_ref[...]

    def norm_step(t, _):
        rows = pl.ds(pl.multiple_of(t * rt, rt), rt)
        v = x_ref[rows, :].astype(F32)
        xf[rows, :] = v
        xn[rows, :] = normalised(v, -1) * pgain
        return 0

    lax.fori_loop(0, cw, norm_step, 0, unroll=2)

    def column(k):
        return padded(xn[pl.ds(k, rt, stride=cw), :].astype(BF16))

    def gated(xk):
        joined = dot(wt[...], xk, NT)
        return jax.nn.sigmoid(joined[:LANES]) * joined[LANES:]

    def pack(dst):
        def step(t, _):
            rows = pl.ds(pl.multiple_of(t * 384, 384), 384)
            dst[rows, :] = side_f[rows, :].astype(BF16)
            return 0

        lax.fori_loop(0, LANES * cw // 384, step, 0, unroll=2)

    def spread_half(src, dst, sem, h):
        def step(d, _):
            target = lax.rem(q + d, n_col)
            to_col(
                target,
                src.at[pl.ds(pl.multiple_of(target * blk + h * hb, 16), hb)],
                dst.at[h, pl.ds(pl.multiple_of(q * hb, 16), hb)],
                sem_out.at[0],
                sem.at[h],
            ).start()
            return 0

        lax.fori_loop(1, n_col, step, 0)
        pltpu.make_async_copy(
            src.at[pl.ds(pl.multiple_of(q * blk + h * hb, 16), hb)],
            dst.at[h, pl.ds(pl.multiple_of(q * hb, 16), hb)],
            sem.at[h],
        ).start()

    wt[...] = rproj_ref[...].astype(F32).T.astype(BF16)

    def right_step(k, _):
        side_f[pl.ds(k, LANES, stride=cw), :] = gated(column(k))
        return 0

    lax.fori_loop(0, cw, right_step, 0, unroll=2)
    pack(side_r)
    pl.semaphore_wait(barrier, n_col + 1)
    spread_half(side_r, recv_r, sem_r, 0)
    spread_half(side_r, recv_r, sem_r, 1)

    for n in SECOND:
        loads[n].wait()
    wt[...] = lproj_ref[...].astype(F32).T.astype(BF16)
    gproj = gproj_ref[...]

    def left_step(k, _):
        xk = column(k)
        side_f[pl.ds(k, LANES, stride=cw), :] = gated(xk)
        gate[k] = jax.nn.sigmoid(dot(xk, gproj))[:rt]
        return 0

    lax.fori_loop(0, cw, left_step, 0, unroll=2)
    pack(side_l)
    spread_half(side_l, recv_l, sem_l, 0)
    spread_half(side_l, recv_l, sem_l, 1)

    def channel_rows(src, h, p, c):
        pair = src[h, pl.ds(pl.multiple_of(p * 2 * hb, 16), 2 * hb), :].astype(F32)
        return jnp.concatenate([pair[c * cw : (c + 1) * cw], pair[hb + c * cw : hb + (c + 1) * cw]], axis=0)

    for h in range(2):
        wait_bytes(recv_r.at[h], sem_r.at[h])
        for cc in range(half):
            c = h * half + cc

            def gather_step(p, _, cc=cc, h=h):
                rtr[pl.ds(pl.multiple_of(p * 2 * cw, 16), 2 * cw), :] = channel_rows(recv_r, h, p, cc)
                return 0

            lax.fori_loop(0, n_col // 2, gather_step, 0, unroll=4)
            for b in range(n_col * cw // LANES):
                ring[0, c, :, b * LANES : (b + 1) * LANES] = rtr[b * LANES : (b + 1) * LANES, :].T[:rt].astype(BF16)
            to_row(right, ring.at[0, c], ring.at[1, c], ring_send.at[0, 0, c], ring_recv.at[0, 1, c]).start()
            to_row(left, ring.at[0, c], ring.at[far + 1, c], ring_send.at[1, 0, c], ring_recv.at[1, 1, c]).start()

    for n in THIRD:
        loads[n].wait()

    lane = lax.broadcasted_iota(jnp.int32, (LANES, LANES), 1)
    first = (r * rt).astype(F32)
    code_rows = jnp.where(mask_ref[...] > 0, tok_ref[...] + 1, 0).astype(F32)
    tok_rows = tok_ref[...].astype(F32) - first
    cond = padded(dot(single_ref[...], cproj_ref[...]).astype(BF16))
    lane_f = lane.astype(F32)
    again = again_ref[...]
    for g in range(slots // LANES):
        rows = slice(g * LANES, (g + 1) * LANES)
        code[HALO + g * LANES : HALO + (g + 1) * LANES, :] = jnp.broadcast_to(code_rows[g : g + 1], (LANES, LANES)).T
        tcol = jnp.broadcast_to(tok_rows[g : g + 1], (LANES, LANES)).T
        hot = (tcol == lane_f).astype(F32).astype(BF16)
        hot_q[rows, :] = hot
        hidden = (normalised(atom_ref[rows, :].astype(F32), -1) * again + dot(hot, cond)).astype(BF16)
        joined = dot(hidden, qkvproj_ref[...]).astype(BF16)
        q_s[rows, :] = joined[:, :LANES]
        kv[HALO + g * LANES : HALO + (g + 1) * LANES, :] = joined[:, LANES:]
    halos = []
    for n, buf in enumerate((kv, code)):
        halos.append(
            to_row(right, buf.at[pl.ds(slots, HALO)], buf.at[pl.ds(0, HALO)], halo_send.at[n, 0], halo_recv.at[n, 0])
        )
        halos.append(
            to_row(left, buf.at[pl.ds(HALO, HALO)], buf.at[pl.ds(HALO + slots, HALO)], halo_send.at[n, 1], halo_recv.at[n, 1])
        )
    for copy in halos:
        copy.start()

    def gather_left():
        for h in range(2):
            wait_bytes(recv_l.at[h], sem_l.at[h])

            def left_gather(p, _, h=h):
                for cc in range(half):
                    lt[h * half + cc, pl.ds(pl.multiple_of(p * 2 * cw, 16), 2 * cw), :] = channel_rows(recv_l, h, p, cc).astype(BF16)
                return 0

            lax.fori_loop(0, n_col // 2, left_gather, 0, unroll=2)

    gcol[...] = jnp.broadcast_to(mgain_ref[...], (LANES, LANES)).T
    bpt[...] = jnp.concatenate([bproj_ref[...].astype(F32), jnp.zeros((8 - HEADS, LANES), F32)], axis=0).astype(BF16)

    def multiply(slot, c, d):
        m = dot(ring[slot, c], lt[c])
        for s in range(sub):
            mf[d, pl.ds(pl.multiple_of((s * cpd + c) * cw, 8), cw), :] = m[s * cw : (s + 1) * cw]

    def send_half(slot, d, source, h):
        def step(s, _):
            target = source * sub + s
            rows = pl.ds(pl.multiple_of(s * blk + h * hb, 16), hb)
            msend[slot, rows, :] = mf[d, rows, :].astype(BF16)
            src = msend.at[slot, rows]
            dst = mrecv.at[pl.ds(pl.multiple_of(q * blk + h * hb, 16), hb)]

            @pl.when(target == q)
            def _():
                pltpu.make_async_copy(src, dst, m_recv).start()

            @pl.when(target != q)
            def _():
                to_col(target, src, dst, m_send, m_recv).start()

            return 0

        lax.fori_loop(0, sub, step, 0)

    owner = q // sub
    near = lax.rem(owner - r + 1 + n_row, n_row)
    is_near = near < 3
    final = (far - 1) * cpd
    events = final + half
    early = 3
    finish_at = cpd + 2
    attend_at = final - 1
    pairs = slots // QWIN // 2

    def place(e):
        s = e // cpd + 1
        c = lax.rem(e, cpd)
        last = e // final
        c0 = c + last * c
        return s, c0, c0 + last, s + far * (1 - last), last

    def pass_on(e):
        s, c0, c1, slot1, last = place(e)
        wait_bytes(ring.at[s, c0], ring_recv.at[0, s, c0])
        before = (s + 1) // far

        @pl.when((last == 0) & (before * lax.rem(c0, 2) == 0))
        def _():
            to_row(right, ring.at[s, c0], ring.at[s + 1, c0], ring_send.at[0, s, c0], ring_recv.at[0, s + 1, c0]).start()

        wait_bytes(ring.at[slot1, c1], ring_recv.at[1, s, c1])

        @pl.when((last == 0) & (before * lax.rem(c0 + 1, 2) == 0))
        def _():
            to_row(
                left,
                ring.at[slot1, c1],
                ring.at[s + 1 + far * (1 - before), c1],
                ring_send.at[1, s, c1],
                ring_recv.at[1, s + 1, c1],
            ).start()

    def finish():
        wait_bytes(mrecv, m_recv)

        def widen(t, _):
            rows = pl.ds(pl.multiple_of(t * 384, 384), 384)
            mrf[rows, :] = mrecv[rows, :].astype(F32)
            return 0

        lax.fori_loop(0, LANES * cw // 384, widen, 0, unroll=2)
        oproj = oproj_ref[...]

        def step(j, _):
            v = mrf[pl.ds(j, LANES, stride=cw), :]
            n = (normalised(v, 0) * gcol[...]).astype(BF16)
            projected = dot(n, oproj, TN)[:rt]
            trif[pl.ds(j, rt, stride=cw), :] = (gate[j] * projected).astype(BF16).astype(F32)
            return 0

        lax.fori_loop(0, cw, step, 0, unroll=8)

        @pl.when(is_near)
        def _():
            def bias_step(j, _):
                updated = (xf[pl.ds(j, rt, stride=cw), :] + trif[pl.ds(j, rt, stride=cw), :]).astype(BF16)
                biasf[pl.ds(j, HEADS, stride=cw), :] = dot(bpt[...], padded(updated), NT)[:HEADS]
                return 0

            lax.fori_loop(0, cw, bias_step, 0, unroll=8)
            bias_out[...] = biasf[...].astype(BF16)
            dst = bias_in.at[pl.ds(pl.multiple_of((near * sub + lax.rem(q, sub)) * HEADS * cw, 16), HEADS * cw)]

            def share(d, _):
                to_col(lax.rem(q + d, n_col), bias_out, dst, b_send, b_recv).start()
                return 0

            lax.fori_loop(1, n_col, share, 0)
            pltpu.make_async_copy(bias_out, dst, b_recv).start()

        def narrow(t, _):
            rows = pl.ds(pl.multiple_of(t * 384, 384), 384)
            tri_ref[rows, :] = trif[rows, :].astype(BF16)
            return 0

        lax.fori_loop(0, rt * cw // 384, narrow, 0, unroll=2)

    ahead, prepare, window, conclude = attention(
        n_row, r, rt, cw, sub, slots, bias_in, b_recv, bm, bias_q, code, hot_q, hot_k, scores, q_s, kv, att, halos, start_ref,
        aproj_ref, tproj_ref, code_rows, aupd_ref, tupd_ref,
    )

    def early_step(e, _):
        pass_on(e)

        @pl.when(e == 1)
        def _():
            for copy in halos:
                copy.wait_recv()

        @pl.when(e > 0)
        def _():
            lax.fori_loop((e - 1) * (pairs // 2), e * (pairs // 2), ahead, 0)

        return 0

    lax.fori_loop(0, early, early_step, 0)
    gather_left()

    def own_step(c, _):
        multiply(0, c, 0)
        return 0

    lax.fori_loop(0, cpd, own_step, 0)
    send_half(0, 0, r, 0)
    send_half(0, 0, r, 1)

    def event(e, _):
        @pl.when((e >= early) & (e < events))
        def _():
            pass_on(e)

        @pl.when(e < events)
        def _():
            s, c0, c1, slot1, last = place(e)
            multiply(s, c0, 0)
            multiply(slot1, c1, 1 - last)

            @pl.when((last == 1) | (lax.rem(c0 + 1, half) == 0))
            def _():
                send_half(s, 0, lax.rem(r + n_row - s, n_row), c0 // half)

            @pl.when((last == 0) & (lax.rem(c0 + 1, half) == 0))
            def _():
                send_half(slot1, 1, lax.rem(r + s, n_row), c0 // half)

        @pl.when(e == attend_at)
        def _():
            prepare()

        @pl.when((e >= attend_at) & (e < attend_at + 3))
        def _():
            begin = jnp.maximum(2 * pairs * (e - attend_at) - pairs // 2, 0) // 2
            end = jnp.minimum(2 * pairs * (e - attend_at + 1) - pairs // 2, 2 * pairs) // 2
            lax.fori_loop(begin, end, window, 0)

        @pl.when(e == events)
        def _():
            conclude()
            for n, ref in ((1, aupd_ref), (2, tupd_ref)):
                pltpu.make_async_copy(ref, outs[n], out_sems.at[n]).start()

        @pl.when(e == jnp.where(is_near, finish_at, events))
        def _():
            finish()

        return 0

    lax.fori_loop(0, events + 1, event, 0)

    pltpu.make_async_copy(tri_ref, outs[0], out_sems.at[0]).start()
    for _ in range(2):
        wait_bytes(side_r.at[pl.ds(0, (n_col - 1) * blk)], sem_out.at[0])
    wait_bytes(mrecv.at[pl.ds(0, (n_col - 1) * blk)], m_send)

    @pl.when(is_near)
    def _():
        wait_bytes(mrecv.at[pl.ds(0, (n_col - 1) * HEADS * cw)], b_send)

    def ring_left(n, _):
        s = n // cpd
        c = lax.rem(n, cpd)
        wait_bytes(ring.at[0, c], ring_send.at[0, s, c])
        wait_bytes(ring.at[0, c], ring_send.at[1, s, c])
        return 0

    lax.fori_loop(0, final, ring_left, 0)
    for c in range(cpd):
        wait_bytes(ring.at[0, c], ring_send.at[c % 2, far - 1, c])
    for copy in halos:
        copy.wait_send()
    for n, ref in enumerate((tri_ref, aupd_ref, tupd_ref)):
        pltpu.make_async_copy(ref, outs[n], out_sems.at[n]).wait()


def attention(
    n_row, r, rt, cw, sub, slots, bias_in, b_recv, bm, bias_q, code, hot_q, hot_k, scores, q_s, kv, att, halos, start_ref,
    aproj_ref, tproj_ref, code_rows, aupd_ref, tupd_ref,
):
    hq = HEADS * QWIN
    span = QWIN + KWIN
    windows = slots // QWIN
    hb = HEADS * cw
    count = 3 * sub
    wide = bm.shape[0] // HEADS
    row_head = lax.broadcasted_iota(jnp.int32, (hq, LANES), 0) // QWIN
    col_head = lax.broadcasted_iota(jnp.int32, (hq, LANES), 1) // (LANES // HEADS)
    own_head = row_head == col_head
    place = lax.broadcasted_iota(jnp.int32, (span, LANES), 0)
    tokens = lax.broadcasted_iota(jnp.int32, (span, LANES), 1).astype(F32) + ((r - 1) * rt + 1).astype(F32)
    scale = 1.0 / math.sqrt(LANES // HEADS)

    def key_base(w):
        first = (1 - (r + n_row - 1) // n_row) * (1 - (w + windows - 1) // windows)
        last = ((r + 1) // n_row) * ((w + 1) // windows)
        return pl.multiple_of((w + first - last) * QWIN, QWIN)

    def ahead(w):
        at = pl.multiple_of(w * QWIN, QWIN)
        base = key_base(w)
        kw = kv[pl.ds(base, span), :LANES]
        qw = q_s[pl.ds(at, QWIN), :]
        qm = jnp.where(own_head, jnp.concatenate([qw] * HEADS, axis=0).astype(F32), 0.0).astype(BF16)
        key_code = code[pl.ds(base, span), :]
        for t in range(wide // LANES):
            hot_k[w, :, t * LANES : (t + 1) * LANES] = (key_code == tokens + float(t * LANES)).astype(F32).astype(BF16)
        begin = start_ref[w] - r * slots + HALO - base
        valid = (key_code > 0.0) & (place >= begin) & (place < begin + KWIN)
        scores[w] = jnp.where(valid, dot(kw, qm, NT) * scale, -1000000000.0)

    def prepare():
        wait_bytes(bias_in, b_recv)
        for p in range(count // 2):
            pair = bias_in[p * 2 * hb : (p + 1) * 2 * hb, :].astype(F32)
            for h in range(HEADS):
                rows = jnp.concatenate([pair[h * cw : (h + 1) * cw], pair[hb + h * cw : hb + (h + 1) * cw]], axis=0)
                bm[h * wide + p * 2 * cw : h * wide + (p + 1) * 2 * cw, :] = rows.astype(BF16)
        for h in range(HEADS):
            bm[h * wide + count * cw : (h + 1) * wide, :] = jnp.zeros((wide - count * cw, LANES), BF16)

        def spread(g, _):
            rows = pl.ds(pl.multiple_of(g * LANES, LANES), LANES)
            for h in range(HEADS):
                bias_q[rows, h * wide : (h + 1) * wide] = dot(hot_q[rows, :], bm[h * wide : (h + 1) * wide, :], NT).astype(BF16)
            return 0

        lax.fori_loop(0, slots // LANES, spread, 0)

    def window(w):
        at = pl.multiple_of(w * QWIN, QWIN)
        bias_w = jnp.concatenate([bias_q[pl.ds(at, QWIN), h * wide : (h + 1) * wide] for h in range(HEADS)], axis=0)
        total = scores[w] + dot(hot_k[w], bias_w, NT)
        raised = jnp.exp(total - jnp.max(total, axis=0, keepdims=True))
        weights = (raised / jnp.sum(raised, axis=0, keepdims=True)).astype(BF16)
        mixed = jnp.where(own_head, dot(weights, kv[pl.ds(key_base(w), span), LANES:], TN), 0.0)
        out = mixed[:QWIN]
        for h in range(1, HEADS):
            out = out + mixed[h * QWIN : (h + 1) * QWIN]
        att[pl.ds(at, QWIN), :] = out.astype(BF16)

    def conclude():
        live = code[HALO : HALO + slots, :] > 0.0
        updated = jnp.where(live, dot(att[...], aproj_ref[...]), 0.0).astype(BF16)
        aupd_ref[...] = updated
        terms = jnp.maximum(dot(updated, tproj_ref[...]), 0.0).astype(BF16)
        own = (lax.broadcasted_iota(jnp.int32, (rt, LANES), 0) + r * rt + 1).astype(F32)
        hot = jnp.concatenate([(own == code_rows[g : g + 1]).astype(F32) for g in range(slots // LANES)], axis=1)
        counts = jnp.maximum(jnp.sum(hot, axis=1, keepdims=True), 1.0)
        tupd_ref[...] = (dot(hot.astype(BF16), terms) / counts).astype(BF16)

    def in_pairs(work):
        def step(p, _):
            work(2 * p)
            work(2 * p + 1)
            return 0

        return step

    return in_pairs(ahead), prepare, in_pairs(window), conclude


def hand_over(a_ref, b_ref, c_ref, a_out, b_out, c_out, ins, outs, a_mid, b_mid, c_mid):
    steps = ((a_ref, a_mid, a_out), (b_ref, b_mid, b_out), (c_ref, c_mid, c_out))
    first = [pltpu.make_async_copy(src, mid, ins.at[n]) for n, (src, mid, _) in enumerate(steps)]
    then = [pltpu.make_async_copy(mid, dst, outs.at[n]) for n, (_, mid, dst) in enumerate(steps)]
    for copy in first:
        copy.start()
    for came, copy in zip(first, then):
        came.wait()
        copy.start()
    for copy in then:
        copy.wait()


def body(n_row, n_col, *args):
    (
        pair_act, pair_gain, left_proj, right_proj, gate_proj, mix_gain, out_proj, bias_proj, token_single, cond_proj,
        atom_act, atom_gain, qkv_proj, attn_proj, token_proj, atom_token, atom_mask, key_start,
    ) = args
    rt, cw, channels = pair_act.shape
    cpd = channels // n_col
    sub = rt // cw
    slots = atom_act.shape[1]
    far = n_row // 2
    depth = n_col * cw
    blk = cpd * cw
    hbm = pl.BlockSpec(memory_space=pl.ANY)
    dma = pltpu.SemaphoreType.DMA
    rows = rt * cw
    wide = -(-3 * rt // LANES) * LANES
    scratch = [
        pltpu.VMEM((rows, LANES), F32),
        pltpu.VMEM((rows, LANES), F32),
        pltpu.VMEM((2 * LANES, LANES), BF16),
        pltpu.VMEM((LANES * cw, LANES), F32),
        pltpu.VMEM((LANES * cw, LANES), BF16),
        pltpu.VMEM((LANES * cw, LANES), BF16),
        pltpu.VMEM((2, n_col * blk // 2, LANES), BF16),
        pltpu.VMEM((2, n_col * blk // 2, LANES), BF16),
        pltpu.VMEM((depth, LANES), F32),
        pltpu.VMEM((cpd, depth, LANES), BF16),
        pltpu.VMEM((2 * far, cpd, rt, depth), BF16),
        pltpu.VMEM((2, sub * blk, LANES), F32),
        pltpu.VMEM((2 * far, sub * blk, LANES), BF16),
        pltpu.VMEM((LANES * cw, LANES), BF16),
        pltpu.VMEM((LANES * cw, LANES), F32),
        pltpu.VMEM((cw, rt, LANES), F32),
        pltpu.VMEM((rows, LANES), F32),
        pltpu.VMEM((HEADS * cw, LANES), F32),
        pltpu.VMEM((HEADS * cw, LANES), BF16),
        pltpu.VMEM((3 * sub * HEADS * cw, LANES), BF16),
        pltpu.VMEM((HEADS * wide, LANES), BF16),
        pltpu.VMEM((LANES, LANES), F32),
        pltpu.VMEM((8, LANES), BF16),
        pltpu.VMEM((slots + 2 * HALO, LANES), F32),
        pltpu.VMEM((slots, LANES), BF16),
        pltpu.VMEM((slots // QWIN, QWIN + KWIN, wide), BF16),
        pltpu.VMEM((slots // QWIN, QWIN + KWIN, LANES), F32),
        pltpu.VMEM((slots, HEADS * wide), BF16),
        pltpu.VMEM((slots, LANES), BF16),
        pltpu.VMEM((slots + 2 * HALO, 2 * LANES), BF16),
        pltpu.VMEM((slots, LANES), BF16),
        dma((2,)),
        dma((2,)),
        dma((1,)),
        dma((2, far, cpd)),
        dma((2, far + 1, cpd)),
        dma,
        dma,
        dma,
        dma,
        dma((2, 2)),
        dma((2, 2)),
    ]
    given = [
        pair_act.reshape(rows, channels), pair_gain.reshape(1, -1), left_proj, right_proj, gate_proj, mix_gain.reshape(1, -1),
        out_proj, bias_proj.T, token_single, cond_proj, atom_act.reshape(slots, channels), atom_gain.reshape(1, -1), qkv_proj,
        attn_proj, token_proj, atom_token.reshape(-1, LANES), atom_mask.reshape(-1, LANES), key_start,
    ]
    held = [pltpu.VMEM(a.shape, a.dtype) for a in given[:-1]] + [pltpu.SMEM(given[-1].shape, given[-1].dtype)]
    held += [pltpu.VMEM((rows, channels), BF16), pltpu.VMEM((slots, channels), BF16), pltpu.VMEM((rt, token_proj.shape[1]), BF16)]
    held += [dma((len(given),)), dma((3,))]
    n_in = len(given)

    def unpack(*refs):
        ins, outs, refs = refs[:n_in], refs[n_in : n_in + 3], refs[n_in + 3 :]
        here, results, sems, rest = refs[:n_in], refs[n_in : n_in + 3], refs[n_in + 3 : n_in + 5], refs[n_in + 5 :]
        kernel(n_row, n_col, rt, cw, ins, outs, here, *sems, *results, *rest)

    made = pl.pallas_call(
        unpack,
        out_shape=[
            jax.ShapeDtypeStruct((rows, channels), BF16),
            jax.ShapeDtypeStruct((slots, channels), BF16),
            jax.ShapeDtypeStruct((rt, token_proj.shape[1]), BF16),
        ],
        in_specs=[hbm] * len(given),
        out_specs=[hbm] * 3,
        scratch_shapes=held + scratch,
        compiler_params=pltpu.CompilerParams(collective_id=0, has_side_effects=True, vmem_limit_bytes=56 * 1024 * 1024),
        name="triangle_attention",
    )(*given)
    tri, aupd, tupd = pl.pallas_call(
        hand_over,
        out_shape=[jax.ShapeDtypeStruct(a.shape, a.dtype) for a in made],
        in_specs=[pl.BlockSpec(memory_space=pl.ANY)] * 3,
        out_specs=[pl.BlockSpec(memory_space=pl.ANY)] * 3,
        scratch_shapes=[dma((3,)), dma((3,))] + [pltpu.VMEM(a.shape, a.dtype) for a in made],
        name="hand_over",
    )(*made)
    return tri.reshape(pair_act.shape), aupd.reshape(atom_act.shape), tupd[None]


def solution(mesh):
    none = P()
    row = P("row")
    atoms = P("col", "row", None)
    pair = P("row", "col", None)
    placed = (pair,) + (none,) * 7 + (P("row", None), none, atoms) + (none,) * 4 + (row,) * 3
    return jax.shard_map(
        functools.partial(body, mesh.shape["row"], mesh.shape["col"]),
        mesh=mesh,
        in_specs=placed,
        out_specs=(pair, atoms, atoms),
        check_vma=False,
    )
```

```python
import functools
import math

import jax
import jax.numpy as jnp
from jax import lax
from jax.experimental import pallas as pl
from jax.experimental.pallas import tpu as pltpu
from jax.sharding import PartitionSpec as P

MESH = pl.DeviceIdType.MESH
HEADS = 4
QWIN = 32
KWIN = 128
HALO = 64
LANES = 128
F32 = jnp.float32
BF16 = jnp.bfloat16
NT = (((1,), (1,)), ((), ()))
TN = (((0,), (0,)), ((), ()))
FIRST = (0, 1, 3)
SECOND = (2, 4)
THIRD = (5, 6, 7, 8, 9, 10, 11, 12, 13, 14, 15, 16, 17)
LOAD_ORDER = FIRST + SECOND + THIRD


def dot(a, b, dims=None):
    if dims is None:
        return jnp.dot(a, b, preferred_element_type=F32)
    return lax.dot_general(a, b, dims, preferred_element_type=F32)


def normalised(values, axis):
    centre = values - jnp.mean(values, axis=axis, keepdims=True)
    spread = jnp.mean(centre * centre, axis=axis, keepdims=True)
    return centre * lax.rsqrt(spread + 1e-05)


def wait_bytes(ref, sem):
    pltpu.make_async_copy(ref, ref, sem).wait()


def padded(rows):
    return jnp.concatenate([rows, jnp.zeros((LANES - rows.shape[0], rows.shape[1]), rows.dtype)], axis=0)


def kernel(
    n_row,
    n_col,
    rt,
    cw,
    ins,
    outs,
    held,
    in_sems,
    out_sems,
    tri_ref,
    aupd_ref,
    tupd_ref,
    xf,
    xn,
    wt,
    side_f,
    side_r,
    side_l,
    recv_r,
    recv_l,
    rtr,
    lt,
    ring,
    mf,
    msend,
    mrecv,
    mrf,
    gate,
    trif,
    biasf,
    bias_out,
    bias_in,
    bm,
    gcol,
    bpt,
    code,
    hot_q,
    hot_k,
    scores,
    bias_q,
    q_s,
    kv,
    att,
    sem_r,
    sem_l,
    sem_out,
    ring_send,
    ring_recv,
    ring_tail,
    m_send,
    m_recv,
    b_send,
    b_recv,
    halo_send,
    halo_recv,
):
    (
        x_ref, pgain_ref, lproj_ref, rproj_ref, gproj_ref, mgain_ref, oproj_ref, bproj_ref, single_ref, cproj_ref, atom_ref,
        again_ref, qkvproj_ref, aproj_ref, tproj_ref, tok_ref, mask_ref, start_ref,
    ) = held
    loads = [pltpu.make_async_copy(src, dst, in_sems.at[n]) for n, (src, dst) in enumerate(zip(ins, held))]
    for n in LOAD_ORDER:
        loads[n].start()
    r = lax.axis_index("row")
    q = lax.axis_index("col")
    cpd = LANES // n_col
    half = cpd // 2
    sub = rt // cw
    blk = cpd * cw
    hb = half * cw
    right = lax.rem(r + 1, n_row)
    left = lax.rem(r + n_row - 1, n_row)
    slots = atom_ref.shape[0]
    far = n_row // 2

    def to_col(target, src, dst, send, recv):
        return pltpu.make_async_remote_copy(
            src_ref=src, dst_ref=dst, send_sem=send, recv_sem=recv, device_id={"col": target}, device_id_type=MESH
        )

    def to_row(target, src, dst, send, recv):
        return pltpu.make_async_remote_copy(
            src_ref=src, dst_ref=dst, send_sem=send, recv_sem=recv, device_id={"row": target}, device_id_type=MESH
        )

    barrier = pltpu.get_barrier_semaphore()

    def greet(d, _):
        pl.semaphore_signal(barrier, inc=1, device_id={"col": lax.rem(q + d, n_col)}, device_id_type=MESH)
        return 0

    lax.fori_loop(1, n_col, greet, 0)
    pl.semaphore_signal(barrier, inc=1, device_id={"row": right}, device_id_type=MESH)
    pl.semaphore_signal(barrier, inc=1, device_id={"row": left}, device_id_type=MESH)

    for n in FIRST:
        loads[n].wait()

    pgain = pgain_ref[...]

    def norm_step(t, _):
        rows = pl.ds(pl.multiple_of(t * rt, rt), rt)
        v = x_ref[rows, :].astype(F32)
        xf[rows, :] = v
        xn[rows, :] = normalised(v, -1) * pgain
        return 0

    lax.fori_loop(0, cw, norm_step, 0, unroll=2)

    def column(k):
        return padded(xn[pl.ds(k, rt, stride=cw), :].astype(BF16))

    def gated(xk):
        joined = dot(wt[...], xk, NT)
        return jax.nn.sigmoid(joined[:LANES]) * joined[LANES:]

    def pack(dst):
        def step(t, _):
            rows = pl.ds(pl.multiple_of(t * 384, 384), 384)
            dst[rows, :] = side_f[rows, :].astype(BF16)
            return 0

        lax.fori_loop(0, LANES * cw // 384, step, 0, unroll=2)

    def spread_half(src, dst, sem, h):
        def step(d, _):
            target = lax.rem(q + d, n_col)
            to_col(
                target,
                src.at[pl.ds(pl.multiple_of(target * blk + h * hb, 16), hb)],
                dst.at[h, pl.ds(pl.multiple_of(q * hb, 16), hb)],
                sem_out.at[0],
                sem.at[h],
            ).start()
            return 0

        lax.fori_loop(1, n_col, step, 0)
        pltpu.make_async_copy(
            src.at[pl.ds(pl.multiple_of(q * blk + h * hb, 16), hb)],
            dst.at[h, pl.ds(pl.multiple_of(q * hb, 16), hb)],
            sem.at[h],
        ).start()

    wt[...] = rproj_ref[...].astype(F32).T.astype(BF16)

    def right_step(k, _):
        side_f[pl.ds(k, LANES, stride=cw), :] = gated(column(k))
        return 0

    lax.fori_loop(0, cw, right_step, 0, unroll=2)
    pack(side_r)
    pl.semaphore_wait(barrier, n_col + 1)
    spread_half(side_r, recv_r, sem_r, 0)
    spread_half(side_r, recv_r, sem_r, 1)

    for n in SECOND:
        loads[n].wait()
    wt[...] = lproj_ref[...].astype(F32).T.astype(BF16)
    gproj = gproj_ref[...]

    def left_step(k, _):
        xk = column(k)
        side_f[pl.ds(k, LANES, stride=cw), :] = gated(xk)
        gate[k] = jax.nn.sigmoid(dot(xk, gproj))[:rt]
        return 0

    lax.fori_loop(0, cw, left_step, 0, unroll=2)
    pack(side_l)
    spread_half(side_l, recv_l, sem_l, 0)
    spread_half(side_l, recv_l, sem_l, 1)

    def channel_rows(src, h, p, c):
        pair = src[h, pl.ds(pl.multiple_of(p * 2 * hb, 16), 2 * hb), :].astype(F32)
        return jnp.concatenate([pair[c * cw : (c + 1) * cw], pair[hb + c * cw : hb + (c + 1) * cw]], axis=0)

    sub_order = list(range(0, sub, 2)) + list(range(1, sub, 2))
    piece = rt // 2

    for h in range(2):
        wait_bytes(recv_r.at[h], sem_r.at[h])
        for cc in range(half):
            c = h * half + cc

            def gather_step(p, _, cc=cc, h=h):
                rtr[pl.ds(pl.multiple_of(p * 2 * cw, 16), 2 * cw), :] = channel_rows(recv_r, h, p, cc)
                return 0

            lax.fori_loop(0, n_col // 2, gather_step, 0, unroll=4)
            for b in range(n_col * cw // LANES):
                block = rtr[b * LANES : (b + 1) * LANES, :].T
                block = jnp.concatenate([block[k * cw : (k + 1) * cw] for k in sub_order], axis=0)
                ring[0, c, :, b * LANES : (b + 1) * LANES] = block.astype(BF16)
            to_row(right, ring.at[0, c], ring.at[1, c], ring_send.at[0, 0, c], ring_recv.at[0, 1, c]).start()
            to_row(left, ring.at[0, c], ring.at[far + 1, c], ring_send.at[1, 0, c], ring_recv.at[1, 1, c]).start()

    for n in THIRD:
        loads[n].wait()

    lane = lax.broadcasted_iota(jnp.int32, (LANES, LANES), 1)
    first = (r * rt).astype(F32)
    code_rows = jnp.where(mask_ref[...] > 0, tok_ref[...] + 1, 0).astype(F32)
    tok_rows = tok_ref[...].astype(F32) - first
    cond = padded(dot(single_ref[...], cproj_ref[...]).astype(BF16))
    lane_f = lane.astype(F32)
    again = again_ref[...]
    for g in range(slots // LANES):
        rows = slice(g * LANES, (g + 1) * LANES)
        code[HALO + g * LANES : HALO + (g + 1) * LANES, :] = jnp.broadcast_to(code_rows[g : g + 1], (LANES, LANES)).T
        tcol = jnp.broadcast_to(tok_rows[g : g + 1], (LANES, LANES)).T
        hot = (tcol == lane_f).astype(F32).astype(BF16)
        hot_q[rows, :] = hot
        hidden = (normalised(atom_ref[rows, :].astype(F32), -1) * again + dot(hot, cond)).astype(BF16)
        joined = dot(hidden, qkvproj_ref[...]).astype(BF16)
        q_s[rows, :] = joined[:, :LANES]
        kv[HALO + g * LANES : HALO + (g + 1) * LANES, :] = joined[:, LANES:]
    halos = []
    for n, buf in enumerate((kv, code)):
        halos.append(
            to_row(right, buf.at[pl.ds(slots, HALO)], buf.at[pl.ds(0, HALO)], halo_send.at[n, 0], halo_recv.at[n, 0])
        )
        halos.append(
            to_row(left, buf.at[pl.ds(HALO, HALO)], buf.at[pl.ds(HALO + slots, HALO)], halo_send.at[n, 1], halo_recv.at[n, 1])
        )
    for copy in halos:
        copy.start()

    def gather_left():
        for h in range(2):
            wait_bytes(recv_l.at[h], sem_l.at[h])

            def left_gather(p, _, h=h):
                for cc in range(half):
                    lt[h * half + cc, pl.ds(pl.multiple_of(p * 2 * cw, 16), 2 * cw), :] = channel_rows(recv_l, h, p, cc).astype(BF16)
                return 0

            lax.fori_loop(0, n_col // 2, left_gather, 0, unroll=2)

    gcol[...] = jnp.broadcast_to(mgain_ref[...], (LANES, LANES)).T
    bpt[...] = jnp.concatenate([bproj_ref[...].astype(F32), jnp.zeros((8 - HEADS, LANES), F32)], axis=0).astype(BF16)

    def multiply(slot, c, d):
        m = dot(ring[slot, c], lt[c])
        for k, s in enumerate(sub_order):
            mf[d, pl.ds(pl.multiple_of((s * cpd + c) * cw, 8), cw), :] = m[k * cw : (k + 1) * cw]

    def multiply_piece(slot, c, part):
        m = dot(ring[slot, c, part * piece : (part + 1) * piece, :], lt[c])
        for k, s in enumerate(range(part, sub, 2)):
            mf[0, pl.ds(pl.multiple_of((s * cpd + c) * cw, 8), cw), :] = m[k * cw : (k + 1) * cw]

    def send_half(slot, d, source, h, first=0, stride=1):
        def step(n, _):
            s = first + n * stride
            target = source * sub + s
            rows = pl.ds(pl.multiple_of(s * blk + h * hb, 16), hb)
            msend[slot, rows, :] = mf[d, rows, :].astype(BF16)
            src = msend.at[slot, rows]
            dst = mrecv.at[pl.ds(pl.multiple_of(q * blk + h * hb, 16), hb)]

            @pl.when(target == q)
            def _():
                pltpu.make_async_copy(src, dst, m_recv).start()

            @pl.when(target != q)
            def _():
                to_col(target, src, dst, m_send, m_recv).start()

            return 0

        lax.fori_loop(0, sub // stride, step, 0)

    owner = q // sub
    near = lax.rem(owner - r + 1 + n_row, n_row)
    is_near = near < 3
    final = (far - 1) * cpd
    events = final + half
    early = 3
    finish_at = cpd + 2
    attend_at = final
    pairs = slots // QWIN // 2

    def place(e):
        s = e // cpd + 1
        c = lax.rem(e, cpd)
        last = e // final
        c0 = c + last * c
        return s, c0, c0 + last, s + far * (1 - last), last

    def pass_on(e):
        s, c0, c1, slot1, last = place(e)
        before = (s + 1) // far
        for direction, slot, target in ((0, s, right), (1, slot1, left)):
            wait_bytes(ring.at[slot, c0], ring_recv.at[direction, s, c0])
            src = ring.at[slot, c0]
            sent = ring_send.at[direction, s, c0]

            @pl.when(before == 0)
            def _():
                to_row(target, src, ring.at[slot + 1, c0], sent, ring_recv.at[direction, s + 1, c0]).start()

            @pl.when((before == 1) & (lax.rem(c0 + direction, 2) == 0))
            def _():
                for part in range(2):
                    rows = pl.ds(part * piece, piece)
                    to_row(target, src.at[rows], ring.at[far, c0, rows], sent, ring_tail.at[part, c0]).start()

    def finish():
        wait_bytes(mrecv, m_recv)

        def widen(t, _):
            rows = pl.ds(pl.multiple_of(t * 384, 384), 384)
            mrf[rows, :] = mrecv[rows, :].astype(F32)
            return 0

        lax.fori_loop(0, LANES * cw // 384, widen, 0, unroll=2)
        oproj = oproj_ref[...]

        def step(j, _):
            v = mrf[pl.ds(j, LANES, stride=cw), :]
            n = (normalised(v, 0) * gcol[...]).astype(BF16)
            projected = dot(n, oproj, TN)[:rt]
            trif[pl.ds(j, rt, stride=cw), :] = (gate[j] * projected).astype(BF16).astype(F32)
            return 0

        lax.fori_loop(0, cw, step, 0, unroll=8)

        @pl.when(is_near)
        def _():
            def bias_step(j, _):
                updated = (xf[pl.ds(j, rt, stride=cw), :] + trif[pl.ds(j, rt, stride=cw), :]).astype(BF16)
                biasf[pl.ds(j, HEADS, stride=cw), :] = dot(bpt[...], padded(updated), NT)[:HEADS]
                return 0

            lax.fori_loop(0, cw, bias_step, 0, unroll=8)
            bias_out[...] = biasf[...].astype(BF16)
            dst = bias_in.at[pl.ds(pl.multiple_of((near * sub + lax.rem(q, sub)) * HEADS * cw, 16), HEADS * cw)]

            def share(d, _):
                to_col(lax.rem(q + d, n_col), bias_out, dst, b_send, b_recv).start()
                return 0

            lax.fori_loop(1, n_col, share, 0)
            pltpu.make_async_copy(bias_out, dst, b_recv).start()

        def narrow(t, _):
            rows = pl.ds(pl.multiple_of(t * 384, 384), 384)
            tri_ref[rows, :] = trif[rows, :].astype(BF16)
            return 0

        lax.fori_loop(0, rt * cw // 384, narrow, 0, unroll=2)

    ahead, prepare, window, conclude = attention(
        n_row, r, rt, cw, sub, slots, bias_in, b_recv, bm, bias_q, code, hot_q, hot_k, scores, q_s, kv, att, halos, start_ref,
        aproj_ref, tproj_ref, code_rows, aupd_ref, tupd_ref,
    )

    def early_step(e, _):
        pass_on(e)

        @pl.when(e == 1)
        def _():
            for copy in halos:
                copy.wait_recv()

        @pl.when(e > 0)
        def _():
            lax.fori_loop((e - 1) * (pairs // 2), e * (pairs // 2), ahead, 0)

        return 0

    lax.fori_loop(0, early, early_step, 0)
    gather_left()

    def own_step(c, _):
        multiply(0, c, 0)
        return 0

    lax.fori_loop(0, cpd, own_step, 0)
    send_half(0, 0, r, 0)
    send_half(0, 0, r, 1)

    def event(e, _):
        @pl.when((e >= early) & (e < final))
        def _():
            pass_on(e)

        @pl.when(e < final)
        def _():
            s, c0, c1, slot1, last = place(e)
            multiply(s, c0, 0)
            multiply(slot1, c1, 1)

            @pl.when(lax.rem(c0 + 1, half) == 0)
            def _():
                send_half(s, 0, lax.rem(r + n_row - s, n_row), c0 // half)
                send_half(slot1, 1, lax.rem(r + s, n_row), c0 // half)

        @pl.when((e >= final) & (e < events))
        def _():
            s, c0, c1, slot1, last = place(e)
            for part in range(2):
                rows = pl.ds(part * piece, piece)
                for c in (c0, c1):
                    wait_bytes(ring.at[far, c, rows], ring_tail.at[part, c])
                    multiply_piece(far, c, part)
                send_half(far, 0, lax.rem(r + far, n_row), c0 // half, part, 2)

        @pl.when(e == attend_at)
        def _():
            prepare()

        @pl.when((e >= attend_at) & (e < attend_at + 2))
        def _():
            begin = (e - attend_at) * pairs // 4
            end = (e - attend_at + 1) * pairs // 4
            lax.fori_loop(begin, end, window, 0)

        @pl.when(e == events)
        def _():
            conclude()
            for n, ref in ((1, aupd_ref), (2, tupd_ref)):
                pltpu.make_async_copy(ref, outs[n], out_sems.at[n]).start()

        @pl.when(e == jnp.where(is_near, finish_at, events))
        def _():
            finish()

        return 0

    lax.fori_loop(0, events + 1, event, 0)

    pltpu.make_async_copy(tri_ref, outs[0], out_sems.at[0]).start()
    for _ in range(2):
        wait_bytes(side_r.at[pl.ds(0, (n_col - 1) * blk)], sem_out.at[0])
    wait_bytes(mrecv.at[pl.ds(0, (n_col - 1) * blk)], m_send)

    @pl.when(is_near)
    def _():
        wait_bytes(mrecv.at[pl.ds(0, (n_col - 1) * HEADS * cw)], b_send)

    def ring_left(n, _):
        s = n // cpd
        c = lax.rem(n, cpd)
        wait_bytes(ring.at[0, c], ring_send.at[0, s, c])
        wait_bytes(ring.at[0, c], ring_send.at[1, s, c])
        return 0

    lax.fori_loop(0, final, ring_left, 0)
    for c in range(cpd):
        wait_bytes(ring.at[0, c], ring_send.at[c % 2, far - 1, c])
    for copy in halos:
        copy.wait_send()
    for n, ref in enumerate((tri_ref, aupd_ref, tupd_ref)):
        pltpu.make_async_copy(ref, outs[n], out_sems.at[n]).wait()


def attention(
    n_row, r, rt, cw, sub, slots, bias_in, b_recv, bm, bias_q, code, hot_q, hot_k, scores, q_s, kv, att, halos, start_ref,
    aproj_ref, tproj_ref, code_rows, aupd_ref, tupd_ref,
):
    hq = HEADS * QWIN
    span = QWIN + KWIN
    windows = slots // QWIN
    hb = HEADS * cw
    count = 3 * sub
    wide = bm.shape[0] // HEADS
    row_head = lax.broadcasted_iota(jnp.int32, (hq, LANES), 0) // QWIN
    col_head = lax.broadcasted_iota(jnp.int32, (hq, LANES), 1) // (LANES // HEADS)
    own_head = row_head == col_head
    place = lax.broadcasted_iota(jnp.int32, (span, LANES), 0)
    tokens = lax.broadcasted_iota(jnp.int32, (span, LANES), 1).astype(F32) + ((r - 1) * rt + 1).astype(F32)
    scale = 1.0 / math.sqrt(LANES // HEADS)

    def key_base(w):
        first = (1 - (r + n_row - 1) // n_row) * (1 - (w + windows - 1) // windows)
        last = ((r + 1) // n_row) * ((w + 1) // windows)
        return pl.multiple_of((w + first - last) * QWIN, QWIN)

    def ahead(w):
        at = pl.multiple_of(w * QWIN, QWIN)
        base = key_base(w)
        kw = kv[pl.ds(base, span), :LANES]
        qw = q_s[pl.ds(at, QWIN), :]
        qm = jnp.where(own_head, jnp.concatenate([qw] * HEADS, axis=0).astype(F32), 0.0).astype(BF16)
        key_code = code[pl.ds(base, span), :]
        for t in range(wide // LANES):
            hot_k[w, :, t * LANES : (t + 1) * LANES] = (key_code == tokens + float(t * LANES)).astype(F32).astype(BF16)
        begin = start_ref[w] - r * slots + HALO - base
        valid = (key_code > 0.0) & (place >= begin) & (place < begin + KWIN)
        scores[w] = jnp.where(valid, dot(kw, qm, NT) * scale, -1000000000.0)

    def prepare():
        wait_bytes(bias_in, b_recv)
        for p in range(count // 2):
            pair = bias_in[p * 2 * hb : (p + 1) * 2 * hb, :].astype(F32)
            for h in range(HEADS):
                rows = jnp.concatenate([pair[h * cw : (h + 1) * cw], pair[hb + h * cw : hb + (h + 1) * cw]], axis=0)
                bm[h * wide + p * 2 * cw : h * wide + (p + 1) * 2 * cw, :] = rows.astype(BF16)
        for h in range(HEADS):
            bm[h * wide + count * cw : (h + 1) * wide, :] = jnp.zeros((wide - count * cw, LANES), BF16)

        def spread(g, _):
            rows = pl.ds(pl.multiple_of(g * LANES, LANES), LANES)
            for h in range(HEADS):
                bias_q[rows, h * wide : (h + 1) * wide] = dot(hot_q[rows, :], bm[h * wide : (h + 1) * wide, :], NT).astype(BF16)
            return 0

        lax.fori_loop(0, slots // LANES, spread, 0)

    def window(w):
        at = pl.multiple_of(w * QWIN, QWIN)
        bias_w = jnp.concatenate([bias_q[pl.ds(at, QWIN), h * wide : (h + 1) * wide] for h in range(HEADS)], axis=0)
        total = scores[w] + dot(hot_k[w], bias_w, NT)
        raised = jnp.exp(total - jnp.max(total, axis=0, keepdims=True))
        weights = (raised / jnp.sum(raised, axis=0, keepdims=True)).astype(BF16)
        mixed = jnp.where(own_head, dot(weights, kv[pl.ds(key_base(w), span), LANES:], TN), 0.0)
        out = mixed[:QWIN]
        for h in range(1, HEADS):
            out = out + mixed[h * QWIN : (h + 1) * QWIN]
        att[pl.ds(at, QWIN), :] = out.astype(BF16)

    def conclude():
        live = code[HALO : HALO + slots, :] > 0.0
        updated = jnp.where(live, dot(att[...], aproj_ref[...]), 0.0).astype(BF16)
        aupd_ref[...] = updated
        terms = jnp.maximum(dot(updated, tproj_ref[...]), 0.0).astype(BF16)
        own = (lax.broadcasted_iota(jnp.int32, (rt, LANES), 0) + r * rt + 1).astype(F32)
        hot = jnp.concatenate([(own == code_rows[g : g + 1]).astype(F32) for g in range(slots // LANES)], axis=1)
        counts = jnp.maximum(jnp.sum(hot, axis=1, keepdims=True), 1.0)
        tupd_ref[...] = (dot(hot.astype(BF16), terms) / counts).astype(BF16)

    def in_pairs(work):
        def step(p, _):
            for k in range(2):
                work(2 * p + k)
            return 0

        return step

    def in_fours(work):
        def step(p, _):
            for k in range(4):
                work(4 * p + k)
            return 0

        return step

    return in_pairs(ahead), prepare, in_fours(window), conclude


def hand_over(a_ref, b_ref, c_ref, a_out, b_out, c_out, ins, outs, a_mid, b_mid, c_mid):
    steps = ((a_ref, a_mid, a_out), (b_ref, b_mid, b_out), (c_ref, c_mid, c_out))
    first = [pltpu.make_async_copy(src, mid, ins.at[n]) for n, (src, mid, _) in enumerate(steps)]
    then = [pltpu.make_async_copy(mid, dst, outs.at[n]) for n, (_, mid, dst) in enumerate(steps)]
    for copy in first:
        copy.start()
    for came, copy in zip(first, then):
        came.wait()
        copy.start()
    for copy in then:
        copy.wait()


def body(n_row, n_col, *args):
    (
        pair_act, pair_gain, left_proj, right_proj, gate_proj, mix_gain, out_proj, bias_proj, token_single, cond_proj,
        atom_act, atom_gain, qkv_proj, attn_proj, token_proj, atom_token, atom_mask, key_start,
    ) = args
    rt, cw, channels = pair_act.shape
    cpd = channels // n_col
    sub = rt // cw
    slots = atom_act.shape[1]
    far = n_row // 2
    depth = n_col * cw
    blk = cpd * cw
    hbm = pl.BlockSpec(memory_space=pl.ANY)
    dma = pltpu.SemaphoreType.DMA
    rows = rt * cw
    wide = -(-3 * rt // LANES) * LANES
    scratch = [
        pltpu.VMEM((rows, LANES), F32),
        pltpu.VMEM((rows, LANES), F32),
        pltpu.VMEM((2 * LANES, LANES), BF16),
        pltpu.VMEM((LANES * cw, LANES), F32),
        pltpu.VMEM((LANES * cw, LANES), BF16),
        pltpu.VMEM((LANES * cw, LANES), BF16),
        pltpu.VMEM((2, n_col * blk // 2, LANES), BF16),
        pltpu.VMEM((2, n_col * blk // 2, LANES), BF16),
        pltpu.VMEM((depth, LANES), F32),
        pltpu.VMEM((cpd, depth, LANES), BF16),
        pltpu.VMEM((2 * far, cpd, rt, depth), BF16),
        pltpu.VMEM((2, sub * blk, LANES), F32),
        pltpu.VMEM((2 * far, sub * blk, LANES), BF16),
        pltpu.VMEM((LANES * cw, LANES), BF16),
        pltpu.VMEM((LANES * cw, LANES), F32),
        pltpu.VMEM((cw, rt, LANES), F32),
        pltpu.VMEM((rows, LANES), F32),
        pltpu.VMEM((HEADS * cw, LANES), F32),
        pltpu.VMEM((HEADS * cw, LANES), BF16),
        pltpu.VMEM((3 * sub * HEADS * cw, LANES), BF16),
        pltpu.VMEM((HEADS * wide, LANES), BF16),
        pltpu.VMEM((LANES, LANES), F32),
        pltpu.VMEM((8, LANES), BF16),
        pltpu.VMEM((slots + 2 * HALO, LANES), F32),
        pltpu.VMEM((slots, LANES), BF16),
        pltpu.VMEM((slots // QWIN, QWIN + KWIN, wide), BF16),
        pltpu.VMEM((slots // QWIN, QWIN + KWIN, LANES), F32),
        pltpu.VMEM((slots, HEADS * wide), BF16),
        pltpu.VMEM((slots, LANES), BF16),
        pltpu.VMEM((slots + 2 * HALO, 2 * LANES), BF16),
        pltpu.VMEM((slots, LANES), BF16),
        dma((2,)),
        dma((2,)),
        dma((1,)),
        dma((2, far, cpd)),
        dma((2, far, cpd)),
        dma((2, cpd)),
        dma,
        dma,
        dma,
        dma,
        dma((2, 2)),
        dma((2, 2)),
    ]
    given = [
        pair_act.reshape(rows, channels), pair_gain.reshape(1, -1), left_proj, right_proj, gate_proj, mix_gain.reshape(1, -1),
        out_proj, bias_proj.T, token_single, cond_proj, atom_act.reshape(slots, channels), atom_gain.reshape(1, -1), qkv_proj,
        attn_proj, token_proj, atom_token.reshape(-1, LANES), atom_mask.reshape(-1, LANES), key_start,
    ]
    held = [pltpu.VMEM(a.shape, a.dtype) for a in given[:-1]] + [pltpu.SMEM(given[-1].shape, given[-1].dtype)]
    held += [pltpu.VMEM((rows, channels), BF16), pltpu.VMEM((slots, channels), BF16), pltpu.VMEM((rt, token_proj.shape[1]), BF16)]
    held += [dma((len(given),)), dma((3,))]
    n_in = len(given)

    def unpack(*refs):
        ins, outs, refs = refs[:n_in], refs[n_in : n_in + 3], refs[n_in + 3 :]
        here, results, sems, rest = refs[:n_in], refs[n_in : n_in + 3], refs[n_in + 3 : n_in + 5], refs[n_in + 5 :]
        kernel(n_row, n_col, rt, cw, ins, outs, here, *sems, *results, *rest)

    made = pl.pallas_call(
        unpack,
        out_shape=[
            jax.ShapeDtypeStruct((rows, channels), BF16),
            jax.ShapeDtypeStruct((slots, channels), BF16),
            jax.ShapeDtypeStruct((rt, token_proj.shape[1]), BF16),
        ],
        in_specs=[hbm] * len(given),
        out_specs=[hbm] * 3,
        scratch_shapes=held + scratch,
        compiler_params=pltpu.CompilerParams(collective_id=0, has_side_effects=True, vmem_limit_bytes=56 * 1024 * 1024),
        name="triangle_attention",
    )(*given)
    tri, aupd, tupd = pl.pallas_call(
        hand_over,
        out_shape=[jax.ShapeDtypeStruct(a.shape, a.dtype) for a in made],
        in_specs=[pl.BlockSpec(memory_space=pl.ANY)] * 3,
        out_specs=[pl.BlockSpec(memory_space=pl.ANY)] * 3,
        scratch_shapes=[dma((3,)), dma((3,))] + [pltpu.VMEM(a.shape, a.dtype) for a in made],
        name="hand_over",
    )(*made)
    return tri.reshape(pair_act.shape), aupd.reshape(atom_act.shape), tupd[None]


def solution(mesh):
    none = P()
    row = P("row")
    atoms = P("col", "row", None)
    pair = P("row", "col", None)
    placed = (pair,) + (none,) * 7 + (P("row", None), none, atoms) + (none,) * 4 + (row,) * 3
    return jax.shard_map(
        functools.partial(body, mesh.shape["row"], mesh.shape["col"]),
        mesh=mesh,
        in_specs=placed,
        out_specs=(pair, atoms, atoms),
        check_vma=False,
    )
```

```python
import functools
import math

import jax
import jax.numpy as jnp
from jax import lax
from jax.experimental import pallas as pl
from jax.experimental.pallas import tpu as pltpu
from jax.sharding import PartitionSpec as P

MESH = pl.DeviceIdType.MESH
HEADS = 4
QWIN = 32
KWIN = 128
HALO = 64
LANES = 128
F32 = jnp.float32
BF16 = jnp.bfloat16
NT = (((1,), (1,)), ((), ()))
TN = (((0,), (0,)), ((), ()))
FIRST = (0, 1, 3)
SECOND = (2, 4)
THIRD = (5, 6, 7, 8, 9, 10, 11, 12, 13, 14, 15, 16, 17)
LOAD_ORDER = FIRST + SECOND + THIRD


def dot(a, b, dims=None):
    if dims is None:
        return jnp.dot(a, b, preferred_element_type=F32)
    return lax.dot_general(a, b, dims, preferred_element_type=F32)


def normalised(values, axis):
    centre = values - jnp.mean(values, axis=axis, keepdims=True)
    spread = jnp.mean(centre * centre, axis=axis, keepdims=True)
    return centre * lax.rsqrt(spread + 1e-05)


def wait_bytes(ref, sem):
    pltpu.make_async_copy(ref, ref, sem).wait()


def padded(rows):
    return jnp.concatenate([rows, jnp.zeros((LANES - rows.shape[0], rows.shape[1]), rows.dtype)], axis=0)


def kernel(
    n_row,
    n_col,
    rt,
    cw,
    ins,
    outs,
    held,
    in_sems,
    out_sems,
    tri_ref,
    aupd_ref,
    tupd_ref,
    xf,
    xn,
    wt,
    side_f,
    side_r,
    side_l,
    recv_r,
    recv_l,
    rtr,
    lt,
    ring,
    mf,
    msend,
    mrecv,
    mrf,
    gate,
    trif,
    biasf,
    bias_out,
    bias_in,
    bm,
    gcol,
    bpt,
    code,
    hot_q,
    hot_k,
    scores,
    bias_q,
    q_s,
    kv,
    att,
    sem_r,
    sem_l,
    sem_out,
    ring_send,
    ring_recv,
    ring_tail,
    m_send,
    m_recv,
    b_send,
    b_recv,
    halo_send,
    halo_recv,
):
    (
        x_ref, pgain_ref, lproj_ref, rproj_ref, gproj_ref, mgain_ref, oproj_ref, bproj_ref, single_ref, cproj_ref, atom_ref,
        again_ref, qkvproj_ref, aproj_ref, tproj_ref, tok_ref, mask_ref, start_ref,
    ) = held
    loads = [pltpu.make_async_copy(src, dst, in_sems.at[n]) for n, (src, dst) in enumerate(zip(ins, held))]
    for n in LOAD_ORDER:
        loads[n].start()
    r = lax.axis_index("row")
    q = lax.axis_index("col")
    cpd = LANES // n_col
    half = cpd // 2
    sub = rt // cw
    blk = cpd * cw
    hb = half * cw
    right = lax.rem(r + 1, n_row)
    left = lax.rem(r + n_row - 1, n_row)
    slots = atom_ref.shape[0]
    far = n_row // 2

    def to_col(target, src, dst, send, recv):
        return pltpu.make_async_remote_copy(
            src_ref=src, dst_ref=dst, send_sem=send, recv_sem=recv, device_id={"col": target}, device_id_type=MESH
        )

    def to_row(target, src, dst, send, recv):
        return pltpu.make_async_remote_copy(
            src_ref=src, dst_ref=dst, send_sem=send, recv_sem=recv, device_id={"row": target}, device_id_type=MESH
        )

    barrier = pltpu.get_barrier_semaphore()

    def greet(d, _):
        pl.semaphore_signal(barrier, inc=1, device_id={"col": lax.rem(q + d, n_col)}, device_id_type=MESH)
        return 0

    lax.fori_loop(1, n_col, greet, 0)
    pl.semaphore_signal(barrier, inc=1, device_id={"row": right}, device_id_type=MESH)
    pl.semaphore_signal(barrier, inc=1, device_id={"row": left}, device_id_type=MESH)

    for n in FIRST:
        loads[n].wait()

    pgain = pgain_ref[...]

    def norm_step(t, _):
        rows = pl.ds(pl.multiple_of(t * rt, rt), rt)
        v = x_ref[rows, :].astype(F32)
        xf[rows, :] = v
        xn[rows, :] = normalised(v, -1) * pgain
        return 0

    lax.fori_loop(0, cw, norm_step, 0, unroll=2)

    def column(k):
        return padded(xn[pl.ds(k, rt, stride=cw), :].astype(BF16))

    def gated(xk):
        joined = dot(wt[...], xk, NT)
        return jax.nn.sigmoid(joined[:LANES]) * joined[LANES:]

    def pack(dst):
        def step(t, _):
            rows = pl.ds(pl.multiple_of(t * 384, 384), 384)
            dst[rows, :] = side_f[rows, :].astype(BF16)
            return 0

        lax.fori_loop(0, LANES * cw // 384, step, 0, unroll=2)

    def spread_half(src, dst, sem, h):
        def step(d, _):
            target = lax.rem(q + d, n_col)
            to_col(
                target,
                src.at[pl.ds(pl.multiple_of(target * blk + h * hb, 16), hb)],
                dst.at[h, pl.ds(pl.multiple_of(q * hb, 16), hb)],
                sem_out.at[0],
                sem.at[h],
            ).start()
            return 0

        lax.fori_loop(1, n_col, step, 0)
        pltpu.make_async_copy(
            src.at[pl.ds(pl.multiple_of(q * blk + h * hb, 16), hb)],
            dst.at[h, pl.ds(pl.multiple_of(q * hb, 16), hb)],
            sem.at[h],
        ).start()

    wt[...] = rproj_ref[...].astype(F32).T.astype(BF16)

    def right_step(k, _):
        side_f[pl.ds(k, LANES, stride=cw), :] = gated(column(k))
        return 0

    lax.fori_loop(0, cw, right_step, 0, unroll=2)
    pack(side_r)
    pl.semaphore_wait(barrier, n_col + 1)
    spread_half(side_r, recv_r, sem_r, 0)
    spread_half(side_r, recv_r, sem_r, 1)

    for n in SECOND:
        loads[n].wait()
    wt[...] = lproj_ref[...].astype(F32).T.astype(BF16)
    gproj = gproj_ref[...]

    def left_step(k, _):
        xk = column(k)
        side_f[pl.ds(k, LANES, stride=cw), :] = gated(xk)
        gate[k] = jax.nn.sigmoid(dot(xk, gproj))[:rt]
        return 0

    lax.fori_loop(0, cw, left_step, 0, unroll=2)
    pack(side_l)
    spread_half(side_l, recv_l, sem_l, 0)
    spread_half(side_l, recv_l, sem_l, 1)

    def channel_rows(src, h, p, c):
        pair = src[h, pl.ds(pl.multiple_of(p * 2 * hb, 16), 2 * hb), :].astype(F32)
        return jnp.concatenate([pair[c * cw : (c + 1) * cw], pair[hb + c * cw : hb + (c + 1) * cw]], axis=0)

    sub_order = list(range(0, sub, 2)) + list(range(1, sub, 2))
    piece = rt // 2

    for h in range(2):
        wait_bytes(recv_r.at[h], sem_r.at[h])
        for cc in range(half):
            c = h * half + cc

            def gather_step(p, _, cc=cc, h=h):
                rtr[pl.ds(pl.multiple_of(p * 2 * cw, 16), 2 * cw), :] = channel_rows(recv_r, h, p, cc)
                return 0

            lax.fori_loop(0, n_col // 2, gather_step, 0, unroll=4)
            for b in range(n_col * cw // LANES):
                block = rtr[b * LANES : (b + 1) * LANES, :].T
                block = jnp.concatenate([block[k * cw : (k + 1) * cw] for k in sub_order], axis=0)
                ring[0, c, :, b * LANES : (b + 1) * LANES] = block.astype(BF16)
            to_row(right, ring.at[0, c], ring.at[1, c], ring_send.at[0, 0, c], ring_recv.at[0, 1, c]).start()
            to_row(left, ring.at[0, c], ring.at[far + 1, c], ring_send.at[1, 0, c], ring_recv.at[1, 1, c]).start()

    for n in THIRD:
        loads[n].wait()

    lane = lax.broadcasted_iota(jnp.int32, (LANES, LANES), 1)
    first = (r * rt).astype(F32)
    code_rows = jnp.where(mask_ref[...] > 0, tok_ref[...] + 1, 0).astype(F32)
    tok_rows = tok_ref[...].astype(F32) - first
    cond = padded(dot(single_ref[...], cproj_ref[...]).astype(BF16))
    lane_f = lane.astype(F32)
    again = again_ref[...]
    for g in range(slots // LANES):
        rows = slice(g * LANES, (g + 1) * LANES)
        code[HALO + g * LANES : HALO + (g + 1) * LANES, :] = jnp.broadcast_to(code_rows[g : g + 1], (LANES, LANES)).T
        tcol = jnp.broadcast_to(tok_rows[g : g + 1], (LANES, LANES)).T
        hot = (tcol == lane_f).astype(F32).astype(BF16)
        hot_q[rows, :] = hot
        hidden = (normalised(atom_ref[rows, :].astype(F32), -1) * again + dot(hot, cond)).astype(BF16)
        joined = dot(hidden, qkvproj_ref[...]).astype(BF16)
        q_s[rows, :] = joined[:, :LANES]
        kv[HALO + g * LANES : HALO + (g + 1) * LANES, :] = joined[:, LANES:]
    halos = []
    for n, buf in enumerate((kv, code)):
        halos.append(
            to_row(right, buf.at[pl.ds(slots, HALO)], buf.at[pl.ds(0, HALO)], halo_send.at[n, 0], halo_recv.at[n, 0])
        )
        halos.append(
            to_row(left, buf.at[pl.ds(HALO, HALO)], buf.at[pl.ds(HALO + slots, HALO)], halo_send.at[n, 1], halo_recv.at[n, 1])
        )
    for copy in halos:
        copy.start()

    def gather_left():
        for h in range(2):
            wait_bytes(recv_l.at[h], sem_l.at[h])

            def left_gather(p, _, h=h):
                for cc in range(half):
                    lt[h * half + cc, pl.ds(pl.multiple_of(p * 2 * cw, 16), 2 * cw), :] = channel_rows(recv_l, h, p, cc).astype(BF16)
                return 0

            lax.fori_loop(0, n_col // 2, left_gather, 0, unroll=2)

    gcol[...] = jnp.broadcast_to(mgain_ref[...], (LANES, LANES)).T
    bpt[...] = jnp.concatenate([bproj_ref[...].astype(F32), jnp.zeros((8 - HEADS, LANES), F32)], axis=0).astype(BF16)

    def multiply(slot, c, d):
        m = dot(ring[slot, c], lt[c])
        for k, s in enumerate(sub_order):
            mf[d, pl.ds(pl.multiple_of((s * cpd + c) * cw, 8), cw), :] = m[k * cw : (k + 1) * cw]

    def multiply_piece(slot, c, part):
        m = dot(ring[slot, c, part * piece : (part + 1) * piece, :], lt[c])
        for k, s in enumerate(range(part, sub, 2)):
            mf[0, pl.ds(pl.multiple_of((s * cpd + c) * cw, 8), cw), :] = m[k * cw : (k + 1) * cw]

    def send_half(slot, d, source, h, first=0, stride=1):
        def step(n, _):
            s = first + n * stride
            target = source * sub + s
            rows = pl.ds(pl.multiple_of(s * blk + h * hb, 16), hb)
            msend[slot, rows, :] = mf[d, rows, :].astype(BF16)
            src = msend.at[slot, rows]
            dst = mrecv.at[pl.ds(pl.multiple_of(q * blk + h * hb, 16), hb)]

            @pl.when(target == q)
            def _():
                pltpu.make_async_copy(src, dst, m_recv).start()

            @pl.when(target != q)
            def _():
                to_col(target, src, dst, m_send, m_recv).start()

            return 0

        lax.fori_loop(0, sub // stride, step, 0)

    owner = q // sub
    near = lax.rem(owner - r + 1 + n_row, n_row)
    is_near = near < 3
    final = (far - 1) * cpd
    events = final + half
    early = 3
    finish_at = cpd + 2
    attend_at = final
    pairs = slots // QWIN // 2

    def place(e):
        s = e // cpd + 1
        c = lax.rem(e, cpd)
        last = e // final
        c0 = c + last * c
        return s, c0, c0 + last, s + far * (1 - last), last

    def pass_on(e):
        s, c0, c1, slot1, last = place(e)
        before = (s + 1) // far
        for direction, slot, target in ((0, s, right), (1, slot1, left)):
            wait_bytes(ring.at[slot, c0], ring_recv.at[direction, s, c0])
            src = ring.at[slot, c0]
            sent = ring_send.at[direction, s, c0]

            @pl.when(before == 0)
            def _():
                to_row(target, src, ring.at[slot + 1, c0], sent, ring_recv.at[direction, s + 1, c0]).start()

            @pl.when((before == 1) & (lax.rem(c0 + direction, 2) == 0))
            def _():
                for part in range(2):
                    rows = pl.ds(part * piece, piece)
                    to_row(target, src.at[rows], ring.at[far, c0, rows], sent, ring_tail.at[part, c0]).start()

    def finish():
        wait_bytes(mrecv, m_recv)

        def widen(t, _):
            rows = pl.ds(pl.multiple_of(t * 384, 384), 384)
            mrf[rows, :] = mrecv[rows, :].astype(F32)
            return 0

        lax.fori_loop(0, LANES * cw // 384, widen, 0, unroll=2)
        oproj = oproj_ref[...]

        def step(j, _):
            v = mrf[pl.ds(j, LANES, stride=cw), :]
            n = (normalised(v, 0) * gcol[...]).astype(BF16)
            projected = dot(n, oproj, TN)[:rt]
            trif[pl.ds(j, rt, stride=cw), :] = (gate[j] * projected).astype(BF16).astype(F32)
            return 0

        lax.fori_loop(0, cw, step, 0, unroll=12)

        @pl.when(is_near)
        def _():
            def bias_step(j, _):
                updated = (xf[pl.ds(j, rt, stride=cw), :] + trif[pl.ds(j, rt, stride=cw), :]).astype(BF16)
                biasf[pl.ds(j, 8, stride=cw), :] = dot(bpt[...], padded(updated), NT)
                return 0

            lax.fori_loop(0, cw, bias_step, 0, unroll=8)
            bias_out[...] = biasf[: HEADS * cw, :].astype(BF16)
            dst = bias_in.at[pl.ds(pl.multiple_of((near * sub + lax.rem(q, sub)) * HEADS * cw, 16), HEADS * cw)]

            def share(d, _):
                to_col(lax.rem(q + d, n_col), bias_out, dst, b_send, b_recv).start()
                return 0

            lax.fori_loop(1, n_col, share, 0)
            pltpu.make_async_copy(bias_out, dst, b_recv).start()

        def narrow(t, _):
            rows = pl.ds(pl.multiple_of(t * 384, 384), 384)
            tri_ref[rows, :] = trif[rows, :].astype(BF16)
            return 0

        lax.fori_loop(0, rt * cw // 384, narrow, 0, unroll=2)

    ahead, prepare, window, conclude = attention(
        n_row, r, rt, cw, sub, slots, bias_in, b_recv, bm, bias_q, code, hot_q, hot_k, scores, q_s, kv, att, halos, start_ref,
        aproj_ref, tproj_ref, code_rows, aupd_ref, tupd_ref,
    )

    def early_step(e, _):
        pass_on(e)

        @pl.when(e == 1)
        def _():
            for copy in halos:
                copy.wait_recv()

        @pl.when(e > 0)
        def _():
            lax.fori_loop((e - 1) * (pairs // 2), e * (pairs // 2), ahead, 0)

        return 0

    lax.fori_loop(0, early, early_step, 0)
    gather_left()

    def own_step(c, _):
        multiply(0, c, 0)
        return 0

    lax.fori_loop(0, cpd, own_step, 0)
    send_half(0, 0, r, 0)
    send_half(0, 0, r, 1)

    def event(e, _):
        @pl.when((e >= early) & (e < final))
        def _():
            pass_on(e)

        @pl.when(e < final)
        def _():
            s, c0, c1, slot1, last = place(e)
            multiply(s, c0, 0)
            multiply(slot1, c1, 1)

            @pl.when(lax.rem(c0 + 1, half) == 0)
            def _():
                send_half(s, 0, lax.rem(r + n_row - s, n_row), c0 // half)
                send_half(slot1, 1, lax.rem(r + s, n_row), c0 // half)

        @pl.when((e >= final) & (e < events))
        def _():
            s, c0, c1, slot1, last = place(e)
            for part in range(2):
                rows = pl.ds(part * piece, piece)
                for c in (c0, c1):
                    wait_bytes(ring.at[far, c, rows], ring_tail.at[part, c])
                    multiply_piece(far, c, part)
                send_half(far, 0, lax.rem(r + far, n_row), c0 // half, part, 2)

        @pl.when(e == attend_at)
        def _():
            prepare()

        @pl.when((e >= attend_at) & (e < attend_at + 2))
        def _():
            begin = (e - attend_at) * pairs // 4
            end = (e - attend_at + 1) * pairs // 4
            lax.fori_loop(begin, end, window, 0)

        @pl.when(e == events)
        def _():
            conclude()
            for n, ref in ((1, aupd_ref), (2, tupd_ref)):
                pltpu.make_async_copy(ref, outs[n], out_sems.at[n]).start()

        @pl.when(e == jnp.where(is_near, finish_at, events))
        def _():
            finish()

        return 0

    lax.fori_loop(0, events + 1, event, 0)

    pltpu.make_async_copy(tri_ref, outs[0], out_sems.at[0]).start()
    for _ in range(2):
        wait_bytes(side_r.at[pl.ds(0, (n_col - 1) * blk)], sem_out.at[0])
    wait_bytes(mrecv.at[pl.ds(0, (n_col - 1) * blk)], m_send)

    @pl.when(is_near)
    def _():
        wait_bytes(mrecv.at[pl.ds(0, (n_col - 1) * HEADS * cw)], b_send)

    def ring_left(n, _):
        s = n // cpd
        c = lax.rem(n, cpd)
        wait_bytes(ring.at[0, c], ring_send.at[0, s, c])
        wait_bytes(ring.at[0, c], ring_send.at[1, s, c])
        return 0

    lax.fori_loop(0, final, ring_left, 0)
    for c in range(cpd):
        wait_bytes(ring.at[0, c], ring_send.at[c % 2, far - 1, c])
    for copy in halos:
        copy.wait_send()
    for n, ref in enumerate((tri_ref, aupd_ref, tupd_ref)):
        pltpu.make_async_copy(ref, outs[n], out_sems.at[n]).wait()


def attention(
    n_row, r, rt, cw, sub, slots, bias_in, b_recv, bm, bias_q, code, hot_q, hot_k, scores, q_s, kv, att, halos, start_ref,
    aproj_ref, tproj_ref, code_rows, aupd_ref, tupd_ref,
):
    hq = HEADS * QWIN
    span = QWIN + KWIN
    windows = slots // QWIN
    hb = HEADS * cw
    count = 3 * sub
    wide = bm.shape[0] // HEADS
    row_head = lax.broadcasted_iota(jnp.int32, (hq, LANES), 0) // QWIN
    col_head = lax.broadcasted_iota(jnp.int32, (hq, LANES), 1) // (LANES // HEADS)
    own_head = row_head == col_head
    place = lax.broadcasted_iota(jnp.int32, (span, LANES), 0)
    tokens = lax.broadcasted_iota(jnp.int32, (span, LANES), 1).astype(F32) + ((r - 1) * rt + 1).astype(F32)
    scale = 1.0 / math.sqrt(LANES // HEADS)

    def key_base(w):
        first = (1 - (r + n_row - 1) // n_row) * (1 - (w + windows - 1) // windows)
        last = ((r + 1) // n_row) * ((w + 1) // windows)
        return pl.multiple_of((w + first - last) * QWIN, QWIN)

    def ahead(w):
        at = pl.multiple_of(w * QWIN, QWIN)
        base = key_base(w)
        kw = kv[pl.ds(base, span), :LANES]
        qw = q_s[pl.ds(at, QWIN), :]
        qm = jnp.where(own_head, jnp.concatenate([qw] * HEADS, axis=0).astype(F32), 0.0).astype(BF16)
        key_code = code[pl.ds(base, span), :]
        for t in range(wide // LANES):
            hot_k[w, :, t * LANES : (t + 1) * LANES] = (key_code == tokens + float(t * LANES)).astype(F32).astype(BF16)
        begin = start_ref[w] - r * slots + HALO - base
        valid = (key_code > 0.0) & (place >= begin) & (place < begin + KWIN)
        scores[w] = jnp.where(valid, dot(kw, qm, NT) * scale, -1000000000.0)

    def prepare():
        wait_bytes(bias_in, b_recv)
        for p in range(count // 2):
            pair = bias_in[p * 2 * hb : (p + 1) * 2 * hb, :].astype(F32)
            for h in range(HEADS):
                rows = jnp.concatenate([pair[h * cw : (h + 1) * cw], pair[hb + h * cw : hb + (h + 1) * cw]], axis=0)
                bm[h * wide + p * 2 * cw : h * wide + (p + 1) * 2 * cw, :] = rows.astype(BF16)
        for h in range(HEADS):
            bm[h * wide + count * cw : (h + 1) * wide, :] = jnp.zeros((wide - count * cw, LANES), BF16)

        def spread(g, _):
            rows = pl.ds(pl.multiple_of(g * LANES, LANES), LANES)
            for h in range(HEADS):
                bias_q[rows, h * wide : (h + 1) * wide] = dot(hot_q[rows, :], bm[h * wide : (h + 1) * wide, :], NT).astype(BF16)
            return 0

        lax.fori_loop(0, slots // LANES, spread, 0)

    def window(w):
        at = pl.multiple_of(w * QWIN, QWIN)
        bias_w = jnp.concatenate([bias_q[pl.ds(at, QWIN), h * wide : (h + 1) * wide] for h in range(HEADS)], axis=0)
        total = scores[w] + dot(hot_k[w], bias_w, NT)
        raised = jnp.exp(total - jnp.max(total, axis=0, keepdims=True))
        weights = (raised / jnp.sum(raised, axis=0, keepdims=True)).astype(BF16)
        mixed = jnp.where(own_head, dot(weights, kv[pl.ds(key_base(w), span), LANES:], TN), 0.0)
        out = mixed[:QWIN]
        for h in range(1, HEADS):
            out = out + mixed[h * QWIN : (h + 1) * QWIN]
        att[pl.ds(at, QWIN), :] = out.astype(BF16)

    def conclude():
        live = code[HALO : HALO + slots, :] > 0.0
        updated = jnp.where(live, dot(att[...], aproj_ref[...]), 0.0).astype(BF16)
        aupd_ref[...] = updated
        terms = jnp.maximum(dot(updated, tproj_ref[...]), 0.0).astype(BF16)
        own = (lax.broadcasted_iota(jnp.int32, (rt, LANES), 0) + r * rt + 1).astype(F32)
        hot = jnp.concatenate([(own == code_rows[g : g + 1]).astype(F32) for g in range(slots // LANES)], axis=1)
        counts = jnp.maximum(jnp.sum(hot, axis=1, keepdims=True), 1.0)
        tupd_ref[...] = (dot(hot.astype(BF16), terms) / counts).astype(BF16)

    def in_pairs(work):
        def step(p, _):
            for k in range(2):
                work(2 * p + k)
            return 0

        return step

    def in_fours(work):
        def step(p, _):
            for k in range(4):
                work(4 * p + k)
            return 0

        return step

    return in_pairs(ahead), prepare, in_fours(window), conclude


def hand_over(a_ref, b_ref, c_ref, a_out, b_out, c_out, ins, outs, a_mid, b_mid, c_mid):
    steps = ((a_ref, a_mid, a_out), (b_ref, b_mid, b_out), (c_ref, c_mid, c_out))
    first = [pltpu.make_async_copy(src, mid, ins.at[n]) for n, (src, mid, _) in enumerate(steps)]
    then = [pltpu.make_async_copy(mid, dst, outs.at[n]) for n, (_, mid, dst) in enumerate(steps)]
    for copy in first:
        copy.start()
    for came, copy in zip(first, then):
        came.wait()
        copy.start()
    for copy in then:
        copy.wait()


def body(n_row, n_col, *args):
    (
        pair_act, pair_gain, left_proj, right_proj, gate_proj, mix_gain, out_proj, bias_proj, token_single, cond_proj,
        atom_act, atom_gain, qkv_proj, attn_proj, token_proj, atom_token, atom_mask, key_start,
    ) = args
    rt, cw, channels = pair_act.shape
    cpd = channels // n_col
    sub = rt // cw
    slots = atom_act.shape[1]
    far = n_row // 2
    depth = n_col * cw
    blk = cpd * cw
    hbm = pl.BlockSpec(memory_space=pl.ANY)
    dma = pltpu.SemaphoreType.DMA
    rows = rt * cw
    wide = -(-3 * rt // LANES) * LANES
    scratch = [
        pltpu.VMEM((rows, LANES), F32),
        pltpu.VMEM((rows, LANES), F32),
        pltpu.VMEM((2 * LANES, LANES), BF16),
        pltpu.VMEM((LANES * cw, LANES), F32),
        pltpu.VMEM((LANES * cw, LANES), BF16),
        pltpu.VMEM((LANES * cw, LANES), BF16),
        pltpu.VMEM((2, n_col * blk // 2, LANES), BF16),
        pltpu.VMEM((2, n_col * blk // 2, LANES), BF16),
        pltpu.VMEM((depth, LANES), F32),
        pltpu.VMEM((cpd, depth, LANES), BF16),
        pltpu.VMEM((2 * far, cpd, rt, depth), BF16),
        pltpu.VMEM((2, sub * blk, LANES), F32),
        pltpu.VMEM((2 * far, sub * blk, LANES), BF16),
        pltpu.VMEM((LANES * cw, LANES), BF16),
        pltpu.VMEM((LANES * cw, LANES), F32),
        pltpu.VMEM((cw, rt, LANES), F32),
        pltpu.VMEM((rows, LANES), F32),
        pltpu.VMEM((8 * cw, LANES), F32),
        pltpu.VMEM((HEADS * cw, LANES), BF16),
        pltpu.VMEM((3 * sub * HEADS * cw, LANES), BF16),
        pltpu.VMEM((HEADS * wide, LANES), BF16),
        pltpu.VMEM((LANES, LANES), F32),
        pltpu.VMEM((8, LANES), BF16),
        pltpu.VMEM((slots + 2 * HALO, LANES), F32),
        pltpu.VMEM((slots, LANES), BF16),
        pltpu.VMEM((slots // QWIN, QWIN + KWIN, wide), BF16),
        pltpu.VMEM((slots // QWIN, QWIN + KWIN, LANES), F32),
        pltpu.VMEM((slots, HEADS * wide), BF16),
        pltpu.VMEM((slots, LANES), BF16),
        pltpu.VMEM((slots + 2 * HALO, 2 * LANES), BF16),
        pltpu.VMEM((slots, LANES), BF16),
        dma((2,)),
        dma((2,)),
        dma((1,)),
        dma((2, far, cpd)),
        dma((2, far, cpd)),
        dma((2, cpd)),
        dma,
        dma,
        dma,
        dma,
        dma((2, 2)),
        dma((2, 2)),
    ]
    given = [
        pair_act.reshape(rows, channels), pair_gain.reshape(1, -1), left_proj, right_proj, gate_proj, mix_gain.reshape(1, -1),
        out_proj, bias_proj.T, token_single, cond_proj, atom_act.reshape(slots, channels), atom_gain.reshape(1, -1), qkv_proj,
        attn_proj, token_proj, atom_token.reshape(-1, LANES), atom_mask.reshape(-1, LANES), key_start,
    ]
    held = [pltpu.VMEM(a.shape, a.dtype) for a in given[:-1]] + [pltpu.SMEM(given[-1].shape, given[-1].dtype)]
    held += [pltpu.VMEM((rows, channels), BF16), pltpu.VMEM((slots, channels), BF16), pltpu.VMEM((rt, token_proj.shape[1]), BF16)]
    held += [dma((len(given),)), dma((3,))]
    n_in = len(given)

    def unpack(*refs):
        ins, outs, refs = refs[:n_in], refs[n_in : n_in + 3], refs[n_in + 3 :]
        here, results, sems, rest = refs[:n_in], refs[n_in : n_in + 3], refs[n_in + 3 : n_in + 5], refs[n_in + 5 :]
        kernel(n_row, n_col, rt, cw, ins, outs, here, *sems, *results, *rest)

    made = pl.pallas_call(
        unpack,
        out_shape=[
            jax.ShapeDtypeStruct((rows, channels), BF16),
            jax.ShapeDtypeStruct((slots, channels), BF16),
            jax.ShapeDtypeStruct((rt, token_proj.shape[1]), BF16),
        ],
        in_specs=[hbm] * len(given),
        out_specs=[hbm] * 3,
        scratch_shapes=held + scratch,
        compiler_params=pltpu.CompilerParams(collective_id=0, has_side_effects=True, vmem_limit_bytes=56 * 1024 * 1024),
        name="triangle_attention",
    )(*given)
    tri, aupd, tupd = pl.pallas_call(
        hand_over,
        out_shape=[jax.ShapeDtypeStruct(a.shape, a.dtype) for a in made],
        in_specs=[pl.BlockSpec(memory_space=pl.ANY)] * 3,
        out_specs=[pl.BlockSpec(memory_space=pl.ANY)] * 3,
        scratch_shapes=[dma((3,)), dma((3,))] + [pltpu.VMEM(a.shape, a.dtype) for a in made],
        name="hand_over",
    )(*made)
    return tri.reshape(pair_act.shape), aupd.reshape(atom_act.shape), tupd[None]


def solution(mesh):
    none = P()
    row = P("row")
    atoms = P("col", "row", None)
    pair = P("row", "col", None)
    placed = (pair,) + (none,) * 7 + (P("row", None), none, atoms) + (none,) * 4 + (row,) * 3
    return jax.shard_map(
        functools.partial(body, mesh.shape["row"], mesh.shape["col"]),
        mesh=mesh,
        in_specs=placed,
        out_specs=(pair, atoms, atoms),
        check_vma=False,
    )
```

```python
import functools
import math

import jax
import jax.numpy as jnp
from jax import lax
from jax.experimental import pallas as pl
from jax.experimental.pallas import tpu as pltpu
from jax.sharding import PartitionSpec as P

MESH = pl.DeviceIdType.MESH
HEADS = 4
QWIN = 32
KWIN = 128
HALO = 64
LANES = 128
F32 = jnp.float32
BF16 = jnp.bfloat16
NT = (((1,), (1,)), ((), ()))
TN = (((0,), (0,)), ((), ()))
FIRST = (0, 1, 3)
SECOND = (2, 4)
THIRD = (5, 6, 7, 8, 9, 10, 11, 12, 13, 14, 15, 16, 17)
LOAD_ORDER = FIRST + SECOND + THIRD


def dot(a, b, dims=None):
    if dims is None:
        return jnp.dot(a, b, preferred_element_type=F32)
    return lax.dot_general(a, b, dims, preferred_element_type=F32)


def normalised(values, axis):
    centre = values - jnp.mean(values, axis=axis, keepdims=True)
    spread = jnp.mean(centre * centre, axis=axis, keepdims=True)
    return centre * lax.rsqrt(spread + 1e-05)


def wait_bytes(ref, sem):
    pltpu.make_async_copy(ref, ref, sem).wait()


def padded(rows):
    return jnp.concatenate([rows, jnp.zeros((LANES - rows.shape[0], rows.shape[1]), rows.dtype)], axis=0)


def kernel(
    n_row,
    n_col,
    rt,
    cw,
    ins,
    outs,
    held,
    in_sems,
    out_sems,
    tri_ref,
    aupd_ref,
    tupd_ref,
    xf,
    xn,
    wt,
    side_f,
    side_r,
    side_l,
    recv_r,
    recv_l,
    rtr,
    lt,
    ring,
    mf,
    msend,
    mrecv,
    mrf,
    gate,
    trif,
    biasf,
    bias_out,
    bias_in,
    bm,
    gcol,
    bpt,
    code,
    hot_q,
    hot_k,
    scores,
    bias_q,
    q_s,
    kv,
    att,
    sem_r,
    sem_l,
    sem_out,
    ring_send,
    ring_recv,
    ring_tail,
    m_send,
    m_recv,
    b_send,
    b_recv,
    halo_send,
    halo_recv,
):
    (
        x_ref, pgain_ref, lproj_ref, rproj_ref, gproj_ref, mgain_ref, oproj_ref, bproj_ref, single_ref, cproj_ref, atom_ref,
        again_ref, qkvproj_ref, aproj_ref, tproj_ref, tok_ref, mask_ref, start_ref,
    ) = held
    loads = [pltpu.make_async_copy(src, dst, in_sems.at[n]) for n, (src, dst) in enumerate(zip(ins, held))]
    for n in LOAD_ORDER:
        loads[n].start()
    r = lax.axis_index("row")
    q = lax.axis_index("col")
    cpd = LANES // n_col
    half = cpd // 2
    sub = rt // cw
    blk = cpd * cw
    hb = half * cw
    right = lax.rem(r + 1, n_row)
    left = lax.rem(r + n_row - 1, n_row)
    slots = atom_ref.shape[0]
    far = n_row // 2

    def to_col(target, src, dst, send, recv):
        return pltpu.make_async_remote_copy(
            src_ref=src, dst_ref=dst, send_sem=send, recv_sem=recv, device_id={"col": target}, device_id_type=MESH
        )

    def to_row(target, src, dst, send, recv):
        return pltpu.make_async_remote_copy(
            src_ref=src, dst_ref=dst, send_sem=send, recv_sem=recv, device_id={"row": target}, device_id_type=MESH
        )

    barrier = pltpu.get_barrier_semaphore()

    def greet(d, _):
        pl.semaphore_signal(barrier, inc=1, device_id={"col": lax.rem(q + d, n_col)}, device_id_type=MESH)
        return 0

    lax.fori_loop(1, n_col, greet, 0)
    pl.semaphore_signal(barrier, inc=1, device_id={"row": right}, device_id_type=MESH)
    pl.semaphore_signal(barrier, inc=1, device_id={"row": left}, device_id_type=MESH)

    for n in FIRST:
        loads[n].wait()

    pgain = pgain_ref[...]

    def norm_step(t, _):
        rows = pl.ds(pl.multiple_of(t * rt, rt), rt)
        v = x_ref[rows, :].astype(F32)
        xf[rows, :] = v
        xn[rows, :] = normalised(v, -1) * pgain
        return 0

    lax.fori_loop(0, cw, norm_step, 0, unroll=2)

    def column(k):
        return padded(xn[pl.ds(k, rt, stride=cw), :].astype(BF16))

    def gated(xk):
        joined = dot(wt[...], xk, NT)
        return jax.nn.sigmoid(joined[:LANES]) * joined[LANES:]

    def pack(dst):
        def step(t, _):
            rows = pl.ds(pl.multiple_of(t * 384, 384), 384)
            dst[rows, :] = side_f[rows, :].astype(BF16)
            return 0

        lax.fori_loop(0, LANES * cw // 384, step, 0, unroll=2)

    def spread_half(src, dst, sem, h):
        def step(d, _):
            target = lax.rem(q + d, n_col)
            to_col(
                target,
                src.at[pl.ds(pl.multiple_of(target * blk + h * hb, 16), hb)],
                dst.at[h, pl.ds(pl.multiple_of(q * hb, 16), hb)],
                sem_out.at[0],
                sem.at[h],
            ).start()
            return 0

        lax.fori_loop(1, n_col, step, 0)
        pltpu.make_async_copy(
            src.at[pl.ds(pl.multiple_of(q * blk + h * hb, 16), hb)],
            dst.at[h, pl.ds(pl.multiple_of(q * hb, 16), hb)],
            sem.at[h],
        ).start()

    wt[...] = rproj_ref[...].astype(F32).T.astype(BF16)

    def right_step(k, _):
        side_f[pl.ds(k, LANES, stride=cw), :] = gated(column(k))
        return 0

    lax.fori_loop(0, cw, right_step, 0, unroll=2)
    pack(side_r)
    pl.semaphore_wait(barrier, n_col + 1)
    spread_half(side_r, recv_r, sem_r, 0)
    spread_half(side_r, recv_r, sem_r, 1)

    for n in SECOND:
        loads[n].wait()
    wt[...] = lproj_ref[...].astype(F32).T.astype(BF16)
    gproj = gproj_ref[...]

    def left_step(k, _):
        xk = column(k)
        side_f[pl.ds(k, LANES, stride=cw), :] = gated(xk)
        gate[k] = jax.nn.sigmoid(dot(xk, gproj))[:rt]
        return 0

    lax.fori_loop(0, cw, left_step, 0, unroll=2)
    pack(side_l)
    spread_half(side_l, recv_l, sem_l, 0)
    spread_half(side_l, recv_l, sem_l, 1)

    def channel_rows(src, h, p, c):
        pair = src[h, pl.ds(pl.multiple_of(p * 2 * hb, 16), 2 * hb), :].astype(F32)
        return jnp.concatenate([pair[c * cw : (c + 1) * cw], pair[hb + c * cw : hb + (c + 1) * cw]], axis=0)

    sub_order = list(range(0, sub, 2)) + list(range(1, sub, 2))
    piece = rt // 2

    for h in range(2):
        wait_bytes(recv_r.at[h], sem_r.at[h])
        for cc in range(half):
            c = h * half + cc

            def gather_step(p, _, cc=cc, h=h):
                rtr[pl.ds(pl.multiple_of(p * 2 * cw, 16), 2 * cw), :] = channel_rows(recv_r, h, p, cc)
                return 0

            lax.fori_loop(0, n_col // 2, gather_step, 0, unroll=4)
            for b in range(n_col * cw // LANES):
                block = rtr[b * LANES : (b + 1) * LANES, :].T
                block = jnp.concatenate([block[k * cw : (k + 1) * cw] for k in sub_order], axis=0)
                ring[0, c, :, b * LANES : (b + 1) * LANES] = block.astype(BF16)
            to_row(right, ring.at[0, c], ring.at[1, c], ring_send.at[0, 0, c], ring_recv.at[0, 1, c]).start()
            to_row(left, ring.at[0, c], ring.at[far + 1, c], ring_send.at[1, 0, c], ring_recv.at[1, 1, c]).start()

    for n in THIRD:
        loads[n].wait()

    lane = lax.broadcasted_iota(jnp.int32, (LANES, LANES), 1)
    first = (r * rt).astype(F32)
    code_rows = jnp.where(mask_ref[...] > 0, tok_ref[...] + 1, 0).astype(F32)
    tok_rows = tok_ref[...].astype(F32) - first
    cond = padded(dot(single_ref[...], cproj_ref[...]).astype(BF16))
    lane_f = lane.astype(F32)
    again = again_ref[...]
    for g in range(slots // LANES):
        rows = slice(g * LANES, (g + 1) * LANES)
        code[HALO + g * LANES : HALO + (g + 1) * LANES, :] = jnp.broadcast_to(code_rows[g : g + 1], (LANES, LANES)).T
        tcol = jnp.broadcast_to(tok_rows[g : g + 1], (LANES, LANES)).T
        hot = (tcol == lane_f).astype(F32).astype(BF16)
        hot_q[rows, :] = hot
        hidden = (normalised(atom_ref[rows, :].astype(F32), -1) * again + dot(hot, cond)).astype(BF16)
        joined = dot(hidden, qkvproj_ref[...]).astype(BF16)
        q_s[rows, :] = joined[:, :LANES]
        kv[HALO + g * LANES : HALO + (g + 1) * LANES, :] = joined[:, LANES:]
    halos = []
    for n, buf in enumerate((kv, code)):
        halos.append(
            to_row(right, buf.at[pl.ds(slots, HALO)], buf.at[pl.ds(0, HALO)], halo_send.at[n, 0], halo_recv.at[n, 0])
        )
        halos.append(
            to_row(left, buf.at[pl.ds(HALO, HALO)], buf.at[pl.ds(HALO + slots, HALO)], halo_send.at[n, 1], halo_recv.at[n, 1])
        )
    for copy in halos:
        copy.start()

    def gather_left():
        for h in range(2):
            wait_bytes(recv_l.at[h], sem_l.at[h])

            def left_gather(p, _, h=h):
                for cc in range(half):
                    lt[h * half + cc, pl.ds(pl.multiple_of(p * 2 * cw, 16), 2 * cw), :] = channel_rows(recv_l, h, p, cc).astype(BF16)
                return 0

            lax.fori_loop(0, n_col // 2, left_gather, 0, unroll=2)

    gcol[...] = jnp.broadcast_to(mgain_ref[...], (LANES, LANES)).T
    bpt[...] = jnp.concatenate([bproj_ref[...].astype(F32), jnp.zeros((8 - HEADS, LANES), F32)], axis=0).astype(BF16)

    def multiply(slot, c, d):
        m = dot(ring[slot, c], lt[c])
        for k, s in enumerate(sub_order):
            mf[d, pl.ds(pl.multiple_of((s * cpd + c) * cw, 8), cw), :] = m[k * cw : (k + 1) * cw]

    def multiply_piece(slot, c, part):
        m = dot(ring[slot, c, part * piece : (part + 1) * piece, :], lt[c])
        for k, s in enumerate(range(part, sub, 2)):
            mf[0, pl.ds(pl.multiple_of((s * cpd + c) * cw, 8), cw), :] = m[k * cw : (k + 1) * cw]

    def send_half(slot, d, source, h, first=0, stride=1):
        def step(n, _):
            s = first + n * stride
            target = source * sub + s
            rows = pl.ds(pl.multiple_of(s * blk + h * hb, 16), hb)
            msend[slot, rows, :] = mf[d, rows, :].astype(BF16)
            src = msend.at[slot, rows]
            dst = mrecv.at[pl.ds(pl.multiple_of(q * blk + h * hb, 16), hb)]

            @pl.when(target == q)
            def _():
                pltpu.make_async_copy(src, dst, m_recv).start()

            @pl.when(target != q)
            def _():
                to_col(target, src, dst, m_send, m_recv).start()

            return 0

        lax.fori_loop(0, sub // stride, step, 0)

    owner = q // sub
    near = lax.rem(owner - r + 1 + n_row, n_row)
    is_near = near < 3
    final = (far - 1) * cpd
    events = final + half
    early = 3
    finish_at = cpd + 2
    attend_at = final
    pairs = slots // QWIN // 2

    def place(e):
        s = e // cpd + 1
        c = lax.rem(e, cpd)
        last = e // final
        c0 = c + last * c
        return s, c0, c0 + last, s + far * (1 - last), last

    def pass_on(e):
        s, c0, c1, slot1, last = place(e)
        before = (s + 1) // far
        for direction, slot, target in ((0, s, right), (1, slot1, left)):
            wait_bytes(ring.at[slot, c0], ring_recv.at[direction, s, c0])
            src = ring.at[slot, c0]
            sent = ring_send.at[direction, s, c0]

            @pl.when(before == 0)
            def _():
                to_row(target, src, ring.at[slot + 1, c0], sent, ring_recv.at[direction, s + 1, c0]).start()

            @pl.when((before == 1) & (lax.rem(c0 + direction, 2) == 0))
            def _():
                for part in range(2):
                    rows = pl.ds(part * piece, piece)
                    to_row(target, src.at[rows], ring.at[far, c0, rows], sent, ring_tail.at[part, c0]).start()

    def finish():
        wait_bytes(mrecv, m_recv)

        def widen(t, _):
            rows = pl.ds(pl.multiple_of(t * 384, 384), 384)
            mrf[rows, :] = mrecv[rows, :].astype(F32)
            return 0

        lax.fori_loop(0, LANES * cw // 384, widen, 0, unroll=2)
        oproj = oproj_ref[...]

        def step(j, _):
            v = mrf[pl.ds(j, LANES, stride=cw), :]
            n = (normalised(v, 0) * gcol[...]).astype(BF16)
            projected = dot(n, oproj, TN)[:rt]
            trif[pl.ds(j, rt, stride=cw), :] = (gate[j] * projected).astype(BF16).astype(F32)
            return 0

        lax.fori_loop(0, cw, step, 0, unroll=12)

        @pl.when(is_near)
        def _():
            def bias_step(j, _):
                updated = (xf[pl.ds(j, rt, stride=cw), :] + trif[pl.ds(j, rt, stride=cw), :]).astype(BF16)
                biasf[pl.ds(j, 8, stride=cw), :] = dot(bpt[...], padded(updated), NT)
                return 0

            lax.fori_loop(0, cw, bias_step, 0, unroll=8)
            bias_out[...] = biasf[: HEADS * cw, :].astype(BF16)
            dst = bias_in.at[pl.ds(pl.multiple_of((near * sub + lax.rem(q, sub)) * HEADS * cw, 16), HEADS * cw)]

            def share(d, _):
                to_col(lax.rem(q + d, n_col), bias_out, dst, b_send, b_recv).start()
                return 0

            lax.fori_loop(1, n_col, share, 0)
            pltpu.make_async_copy(bias_out, dst, b_recv).start()

        def narrow(t, _):
            rows = pl.ds(pl.multiple_of(t * 384, 384), 384)
            tri_ref[rows, :] = trif[rows, :].astype(BF16)
            pltpu.make_async_copy(tri_ref.at[rows], outs[0].at[rows], out_sems.at[0]).start()
            return 0

        lax.fori_loop(0, rt * cw // 384, narrow, 0, unroll=2)

    ahead, prepare, window, conclude = attention(
        n_row, r, rt, cw, sub, slots, bias_in, b_recv, bm, bias_q, code, hot_q, hot_k, scores, q_s, kv, att, halos, start_ref,
        aproj_ref, tproj_ref, code_rows, aupd_ref, tupd_ref,
    )

    def early_step(e, _):
        pass_on(e)

        @pl.when(e == 1)
        def _():
            for copy in halos:
                copy.wait_recv()

        @pl.when(e > 0)
        def _():
            lax.fori_loop((e - 1) * (pairs // 2), e * (pairs // 2), ahead, 0)

        return 0

    lax.fori_loop(0, early, early_step, 0)
    gather_left()

    def own_step(c, _):
        multiply(0, c, 0)
        return 0

    lax.fori_loop(0, cpd, own_step, 0)
    send_half(0, 0, r, 0)
    send_half(0, 0, r, 1)

    def event(e, _):
        @pl.when((e >= early) & (e < final))
        def _():
            pass_on(e)

        @pl.when(e < final)
        def _():
            s, c0, c1, slot1, last = place(e)
            multiply(s, c0, 0)
            multiply(slot1, c1, 1)

            @pl.when(lax.rem(c0 + 1, half) == 0)
            def _():
                send_half(s, 0, lax.rem(r + n_row - s, n_row), c0 // half)
                send_half(slot1, 1, lax.rem(r + s, n_row), c0 // half)

        @pl.when((e >= final) & (e < events))
        def _():
            s, c0, c1, slot1, last = place(e)
            for part in range(2):
                rows = pl.ds(part * piece, piece)
                for c in (c0, c1):
                    wait_bytes(ring.at[far, c, rows], ring_tail.at[part, c])
                    multiply_piece(far, c, part)
                send_half(far, 0, lax.rem(r + far, n_row), c0 // half, part, 2)

        @pl.when(e == attend_at)
        def _():
            prepare()

        @pl.when((e >= attend_at) & (e < attend_at + 2))
        def _():
            begin = (e - attend_at) * pairs // 4
            end = (e - attend_at + 1) * pairs // 4
            lax.fori_loop(begin, end, window, 0)

        @pl.when(e == events)
        def _():
            conclude()
            for n, ref in ((1, aupd_ref), (2, tupd_ref)):
                pltpu.make_async_copy(ref, outs[n], out_sems.at[n]).start()

        @pl.when(e == jnp.where(is_near, finish_at, events))
        def _():
            finish()

        return 0

    lax.fori_loop(0, events + 1, event, 0)

    for _ in range(2):
        wait_bytes(side_r.at[pl.ds(0, (n_col - 1) * blk)], sem_out.at[0])
    wait_bytes(mrecv.at[pl.ds(0, (n_col - 1) * blk)], m_send)

    @pl.when(is_near)
    def _():
        wait_bytes(mrecv.at[pl.ds(0, (n_col - 1) * HEADS * cw)], b_send)

    def ring_left(n, _):
        s = n // cpd
        c = lax.rem(n, cpd)
        wait_bytes(ring.at[0, c], ring_send.at[0, s, c])
        wait_bytes(ring.at[0, c], ring_send.at[1, s, c])
        return 0

    lax.fori_loop(0, final, ring_left, 0)
    for c in range(cpd):
        wait_bytes(ring.at[0, c], ring_send.at[c % 2, far - 1, c])
    for copy in halos:
        copy.wait_send()
    for n, ref in enumerate((tri_ref, aupd_ref, tupd_ref)):
        pltpu.make_async_copy(ref, outs[n], out_sems.at[n]).wait()


def attention(
    n_row, r, rt, cw, sub, slots, bias_in, b_recv, bm, bias_q, code, hot_q, hot_k, scores, q_s, kv, att, halos, start_ref,
    aproj_ref, tproj_ref, code_rows, aupd_ref, tupd_ref,
):
    hq = HEADS * QWIN
    span = QWIN + KWIN
    windows = slots // QWIN
    hb = HEADS * cw
    count = 3 * sub
    wide = bm.shape[0] // HEADS
    row_head = lax.broadcasted_iota(jnp.int32, (hq, LANES), 0) // QWIN
    col_head = lax.broadcasted_iota(jnp.int32, (hq, LANES), 1) // (LANES // HEADS)
    own_head = row_head == col_head
    place = lax.broadcasted_iota(jnp.int32, (span, LANES), 0)
    tokens = lax.broadcasted_iota(jnp.int32, (span, LANES), 1).astype(F32) + ((r - 1) * rt + 1).astype(F32)
    scale = 1.0 / math.sqrt(LANES // HEADS)

    def key_base(w):
        first = (1 - (r + n_row - 1) // n_row) * (1 - (w + windows - 1) // windows)
        last = ((r + 1) // n_row) * ((w + 1) // windows)
        return pl.multiple_of((w + first - last) * QWIN, QWIN)

    def ahead(w):
        at = pl.multiple_of(w * QWIN, QWIN)
        base = key_base(w)
        kw = kv[pl.ds(base, span), :LANES]
        qw = q_s[pl.ds(at, QWIN), :]
        qm = jnp.where(own_head, jnp.concatenate([qw] * HEADS, axis=0).astype(F32), 0.0).astype(BF16)
        key_code = code[pl.ds(base, span), :]
        for t in range(wide // LANES):
            hot_k[w, :, t * LANES : (t + 1) * LANES] = (key_code == tokens + float(t * LANES)).astype(F32).astype(BF16)
        begin = start_ref[w] - r * slots + HALO - base
        valid = (key_code > 0.0) & (place >= begin) & (place < begin + KWIN)
        scores[w] = jnp.where(valid, dot(kw, qm, NT) * scale, -1000000000.0)

    def prepare():
        wait_bytes(bias_in, b_recv)
        for p in range(count // 2):
            pair = bias_in[p * 2 * hb : (p + 1) * 2 * hb, :].astype(F32)
            for h in range(HEADS):
                rows = jnp.concatenate([pair[h * cw : (h + 1) * cw], pair[hb + h * cw : hb + (h + 1) * cw]], axis=0)
                bm[h * wide + p * 2 * cw : h * wide + (p + 1) * 2 * cw, :] = rows.astype(BF16)
        for h in range(HEADS):
            bm[h * wide + count * cw : (h + 1) * wide, :] = jnp.zeros((wide - count * cw, LANES), BF16)

        def spread(g, _):
            rows = pl.ds(pl.multiple_of(g * LANES, LANES), LANES)
            for h in range(HEADS):
                bias_q[rows, h * wide : (h + 1) * wide] = dot(hot_q[rows, :], bm[h * wide : (h + 1) * wide, :], NT).astype(BF16)
            return 0

        lax.fori_loop(0, slots // LANES, spread, 0)

    def window(w):
        at = pl.multiple_of(w * QWIN, QWIN)
        bias_w = jnp.concatenate([bias_q[pl.ds(at, QWIN), h * wide : (h + 1) * wide] for h in range(HEADS)], axis=0)
        total = scores[w] + dot(hot_k[w], bias_w, NT)
        raised = jnp.exp(total - jnp.max(total, axis=0, keepdims=True))
        weights = (raised / jnp.sum(raised, axis=0, keepdims=True)).astype(BF16)
        mixed = jnp.where(own_head, dot(weights, kv[pl.ds(key_base(w), span), LANES:], TN), 0.0)
        out = mixed[:QWIN]
        for h in range(1, HEADS):
            out = out + mixed[h * QWIN : (h + 1) * QWIN]
        att[pl.ds(at, QWIN), :] = out.astype(BF16)

    def conclude():
        live = code[HALO : HALO + slots, :] > 0.0
        updated = jnp.where(live, dot(att[...], aproj_ref[...]), 0.0).astype(BF16)
        aupd_ref[...] = updated
        terms = jnp.maximum(dot(updated, tproj_ref[...]), 0.0).astype(BF16)
        own = (lax.broadcasted_iota(jnp.int32, (rt, LANES), 0) + r * rt + 1).astype(F32)
        hot = jnp.concatenate([(own == code_rows[g : g + 1]).astype(F32) for g in range(slots // LANES)], axis=1)
        counts = jnp.maximum(jnp.sum(hot, axis=1, keepdims=True), 1.0)
        tupd_ref[...] = (dot(hot.astype(BF16), terms) / counts).astype(BF16)

    def in_pairs(work):
        def step(p, _):
            for k in range(2):
                work(2 * p + k)
            return 0

        return step

    def in_fours(work):
        def step(p, _):
            for k in range(4):
                work(4 * p + k)
            return 0

        return step

    return in_pairs(ahead), prepare, in_fours(window), conclude


def hand_over(a_ref, b_ref, c_ref, a_out, b_out, c_out, ins, outs, a_mid, b_mid, c_mid):
    steps = ((a_ref, a_mid, a_out), (b_ref, b_mid, b_out), (c_ref, c_mid, c_out))
    first = [pltpu.make_async_copy(src, mid, ins.at[n]) for n, (src, mid, _) in enumerate(steps)]
    then = [pltpu.make_async_copy(mid, dst, outs.at[n]) for n, (_, mid, dst) in enumerate(steps)]
    for copy in first:
        copy.start()
    for came, copy in zip(first, then):
        came.wait()
        copy.start()
    for copy in then:
        copy.wait()


def body(n_row, n_col, *args):
    (
        pair_act, pair_gain, left_proj, right_proj, gate_proj, mix_gain, out_proj, bias_proj, token_single, cond_proj,
        atom_act, atom_gain, qkv_proj, attn_proj, token_proj, atom_token, atom_mask, key_start,
    ) = args
    rt, cw, channels = pair_act.shape
    cpd = channels // n_col
    sub = rt // cw
    slots = atom_act.shape[1]
    far = n_row // 2
    depth = n_col * cw
    blk = cpd * cw
    hbm = pl.BlockSpec(memory_space=pl.ANY)
    dma = pltpu.SemaphoreType.DMA
    rows = rt * cw
    wide = -(-3 * rt // LANES) * LANES
    scratch = [
        pltpu.VMEM((rows, LANES), F32),
        pltpu.VMEM((rows, LANES), F32),
        pltpu.VMEM((2 * LANES, LANES), BF16),
        pltpu.VMEM((LANES * cw, LANES), F32),
        pltpu.VMEM((LANES * cw, LANES), BF16),
        pltpu.VMEM((LANES * cw, LANES), BF16),
        pltpu.VMEM((2, n_col * blk // 2, LANES), BF16),
        pltpu.VMEM((2, n_col * blk // 2, LANES), BF16),
        pltpu.VMEM((depth, LANES), F32),
        pltpu.VMEM((cpd, depth, LANES), BF16),
        pltpu.VMEM((2 * far, cpd, rt, depth), BF16),
        pltpu.VMEM((2, sub * blk, LANES), F32),
        pltpu.VMEM((2 * far, sub * blk, LANES), BF16),
        pltpu.VMEM((LANES * cw, LANES), BF16),
        pltpu.VMEM((LANES * cw, LANES), F32),
        pltpu.VMEM((cw, rt, LANES), F32),
        pltpu.VMEM((rows, LANES), F32),
        pltpu.VMEM((8 * cw, LANES), F32),
        pltpu.VMEM((HEADS * cw, LANES), BF16),
        pltpu.VMEM((3 * sub * HEADS * cw, LANES), BF16),
        pltpu.VMEM((HEADS * wide, LANES), BF16),
        pltpu.VMEM((LANES, LANES), F32),
        pltpu.VMEM((8, LANES), BF16),
        pltpu.VMEM((slots + 2 * HALO, LANES), F32),
        pltpu.VMEM((slots, LANES), BF16),
        pltpu.VMEM((slots // QWIN, QWIN + KWIN, wide), BF16),
        pltpu.VMEM((slots // QWIN, QWIN + KWIN, LANES), F32),
        pltpu.VMEM((slots, HEADS * wide), BF16),
        pltpu.VMEM((slots, LANES), BF16),
        pltpu.VMEM((slots + 2 * HALO, 2 * LANES), BF16),
        pltpu.VMEM((slots, LANES), BF16),
        dma((2,)),
        dma((2,)),
        dma((1,)),
        dma((2, far, cpd)),
        dma((2, far, cpd)),
        dma((2, cpd)),
        dma,
        dma,
        dma,
        dma,
        dma((2, 2)),
        dma((2, 2)),
    ]
    given = [
        pair_act.reshape(rows, channels), pair_gain.reshape(1, -1), left_proj, right_proj, gate_proj, mix_gain.reshape(1, -1),
        out_proj, bias_proj.T, token_single, cond_proj, atom_act.reshape(slots, channels), atom_gain.reshape(1, -1), qkv_proj,
        attn_proj, token_proj, atom_token.reshape(-1, LANES), atom_mask.reshape(-1, LANES), key_start,
    ]
    held = [pltpu.VMEM(a.shape, a.dtype) for a in given[:-1]] + [pltpu.SMEM(given[-1].shape, given[-1].dtype)]
    held += [pltpu.VMEM((rows, channels), BF16), pltpu.VMEM((slots, channels), BF16), pltpu.VMEM((rt, token_proj.shape[1]), BF16)]
    held += [dma((len(given),)), dma((3,))]
    n_in = len(given)

    def unpack(*refs):
        ins, outs, refs = refs[:n_in], refs[n_in : n_in + 3], refs[n_in + 3 :]
        here, results, sems, rest = refs[:n_in], refs[n_in : n_in + 3], refs[n_in + 3 : n_in + 5], refs[n_in + 5 :]
        kernel(n_row, n_col, rt, cw, ins, outs, here, *sems, *results, *rest)

    made = pl.pallas_call(
        unpack,
        out_shape=[
            jax.ShapeDtypeStruct((rows, channels), BF16),
            jax.ShapeDtypeStruct((slots, channels), BF16),
            jax.ShapeDtypeStruct((rt, token_proj.shape[1]), BF16),
        ],
        in_specs=[hbm] * len(given),
        out_specs=[hbm] * 3,
        scratch_shapes=held + scratch,
        compiler_params=pltpu.CompilerParams(collective_id=0, has_side_effects=True, vmem_limit_bytes=56 * 1024 * 1024),
        name="triangle_attention",
    )(*given)
    tri, aupd, tupd = pl.pallas_call(
        hand_over,
        out_shape=[jax.ShapeDtypeStruct(a.shape, a.dtype) for a in made],
        in_specs=[pl.BlockSpec(memory_space=pl.ANY)] * 3,
        out_specs=[pl.BlockSpec(memory_space=pl.ANY)] * 3,
        scratch_shapes=[dma((3,)), dma((3,))] + [pltpu.VMEM(a.shape, a.dtype) for a in made],
        name="hand_over",
    )(*made)
    return tri.reshape(pair_act.shape), aupd.reshape(atom_act.shape), tupd[None]


def solution(mesh):
    none = P()
    row = P("row")
    atoms = P("col", "row", None)
    pair = P("row", "col", None)
    placed = (pair,) + (none,) * 7 + (P("row", None), none, atoms) + (none,) * 4 + (row,) * 3
    return jax.shard_map(
        functools.partial(body, mesh.shape["row"], mesh.shape["col"]),
        mesh=mesh,
        in_specs=placed,
        out_specs=(pair, atoms, atoms),
        check_vma=False,
    )
```
